128 devices in a mesh: grp: 16 (over x, y), blk: 8 (over z, core).
Axes of the slice: x: 4, y: 4, z: 4, core: 2. Of those that a mesh axis runs over, the one named last changes fastest.
Arguments:
- embeddings: bfloat16 [65536, 512], P(('grp', 'blk')), may hold values from -1000 to 1000
- cluster_sizes: int32 [32], replicated, may hold values from 1 to 8192, as said below
- cluster_of: int32 [65536], P(('grp', 'blk')), may hold values from 0 to 31, as said below
- rank_in: int32 [65536], P(('grp', 'blk')), may hold values from 0 to 8191, as said below
Outputs:
- max_cosine: float32 [65536], P(('grp', 'blk'))
The draws below stay inside these ranges and needn't reach their ends.
Inputs may be any that keep to these rules, and one draw needn't show every extreme that they name: `cluster_sizes`: the sizes sum to 65536; the largest is exactly 8192; clusters 2g and 2g + 1 together hold at most 10240, reached for one g. `cluster_of`: cluster c holds exactly cluster_sizes[c] embeddings. `rank_in`: within each cluster the ranks are 0 to its size - 1, each once. Let the position of an embedding be its rank plus, for an odd cluster c, cluster_sizes[c - 1]; among one device's entries on entry, at most 10 share one value of (cluster_of // 2, position // 1280), and that many do on some device.
All inputs are finite; a program needn't handle non-finite values.
Results may differ from the reference program's by a relative error of at most 0.0015.
Values may be sent and summed in bfloat16 or wider, within the bound.
No kernel may reach another device: no remote copies, remote signals or barrier semaphores. Data moves between devices by JAX's collectives and lax.ppermute only.
A program may use at most 64 MiB of HBM per device.

```python
import math
import jax
import jax.numpy as jnp
from jax import lax

D = 512
ROWS = 65536
CLUST = 32
MEAN = 2048
SLOTS = 1280
N_GRP = 16
N_BLK = 8


def layout(key):
    keys = jax.random.split(key, 5)
    groups = N_GRP
    devices = N_GRP * N_BLK
    big_group = jax.random.randint(keys[0], (), 0, groups)
    big_first = jax.random.randint(keys[1], (), 0, 2)
    remaining = MEAN * (2 * groups - 5)
    share = remaining // (2 * (groups - 1))
    extra = remaining - 2 * share * (groups - 1)
    spread = jax.random.randint(keys[2], (groups,), -(share // 2), share // 2 + 1)
    group_ids = jnp.arange(groups, dtype=jnp.int32)
    lower = share + spread + jnp.where(group_ids == (big_group + 1) % groups, extra, 0)
    upper = share - spread
    big_a = jnp.where(big_first == 0, 4 * MEAN, MEAN)
    big_b = 5 * MEAN - big_a
    lower = jnp.where(group_ids == big_group, big_a, lower)
    upper = jnp.where(group_ids == big_group, big_b, upper)
    sizes = jnp.stack([lower, upper], axis=1).reshape(CLUST).astype(jnp.int32)
    ends = jnp.cumsum(sizes).astype(jnp.int32)
    starts = ends - sizes
    position = jnp.arange(ROWS, dtype=jnp.int32)
    cluster = jnp.searchsorted(ends, position, side='right').astype(jnp.int32)
    rank = position - starts[cluster]
    previous = sizes[jnp.maximum(cluster - 1, 0)]
    place = rank + jnp.where(cluster % 2 == 1, previous, 0)
    target = cluster // 2 * N_BLK + place // SLOTS
    tie_one = jax.random.permutation(keys[3], ROWS).astype(jnp.int32)
    order = jnp.argsort(target * ROWS + tie_one).astype(jnp.int32)
    source = position % devices
    tie_two = jax.random.permutation(keys[4], ROWS).astype(jnp.int32)
    arrange = jnp.argsort(source * ROWS + tie_two).astype(jnp.int32)
    final = order[arrange]
    return (sizes, cluster[final], rank[final])


def draw_cluster_sizes(key, part):
    anchor = key
    return layout(anchor)[0]


def draw_cluster_of(key, part):
    anchor = key
    return layout(anchor)[1]


def draw_rank_in(key, part):
    anchor = key
    return layout(anchor)[2]


def draw_embeddings(key, part):
    key = jax.random.fold_in(key, 4)
    keys = jax.random.split(key, 3)
    noise = jnp.clip(jax.random.normal(keys[0], (ROWS, D), jnp.float32), -5.0, 5.0)
    row_scale = jnp.exp(jax.random.uniform(keys[1], (ROWS, 1), jnp.float32) * math.log(10.0))
    column_scale = jnp.exp(jax.random.uniform(keys[2], (1, D), jnp.float32) * math.log(10.0))
    values = row_scale * column_scale * noise
    return values.astype(jnp.bfloat16)


def setup_inputs(seed: int = 0) -> dict:
    seeds = jax.random.split(jax.random.key(seed), 5)
    return {
        "embeddings": draw_embeddings(jax.random.fold_in(seeds[4], 71), 0),
        "cluster_sizes": draw_cluster_sizes(jax.random.fold_in(seeds[4], 71), 0),
        "cluster_of": draw_cluster_of(jax.random.fold_in(seeds[4], 71), 0),
        "rank_in": draw_rank_in(jax.random.fold_in(seeds[4], 71), 0),
    }


def reference(embeddings, cluster_sizes, cluster_of, rank_in):
    values = embeddings.astype(jnp.float32)
    unit = (values / jnp.sqrt(lax.optimization_barrier(jnp.sum(values * values, axis=1, keepdims=True)) + 1e-06)).astype(jnp.bfloat16)
    order = jnp.argsort(cluster_of * ROWS + rank_in).astype(jnp.int32)
    sorted_unit = unit[order]
    sorted_cluster = cluster_of[order].astype(jnp.int32)
    span = N_BLK * SLOTS
    padded_unit = jnp.concatenate([sorted_unit, jnp.zeros((span, D), jnp.bfloat16)], axis=0)
    padded_cluster = jnp.concatenate([sorted_cluster, jnp.full((span,), -1, jnp.int32)], axis=0)
    ends = jnp.cumsum(cluster_sizes).astype(jnp.int32)
    starts = (ends - cluster_sizes).astype(jnp.int32)
    group_start = starts[0::2]
    columns = jnp.arange(span, dtype=jnp.int32)

    def one_group(begin):
        window = lax.dynamic_slice(padded_unit, (begin, jnp.int32(0)), (span, D))
        labels = lax.dynamic_slice(padded_cluster, (begin,), (span,))

        def one_block(index):
            first_row = (index * SLOTS).astype(jnp.int32)
            rows_here = lax.dynamic_slice(window, (first_row, jnp.int32(0)), (SLOTS, D))
            row_labels = lax.dynamic_slice(labels, (first_row,), (SLOTS,))
            row_place = first_row + jnp.arange(SLOTS, dtype=jnp.int32)
            scores = lax.dot_general(rows_here, window, (((1,), (1,)), ((), ())), preferred_element_type=jnp.float32)
            allowed = (row_labels[:, None] == labels[None, :]) & (row_labels[:, None] >= 0) & (columns[None, :] < row_place[:, None])
            return lax.optimization_barrier(jnp.max(jnp.where(allowed, scores, -1.0), axis=1))
        return lax.map(one_block, jnp.arange(N_BLK, dtype=jnp.int32)).reshape(span)
    per_group = lax.map(one_group, group_start)
    position = jnp.arange(ROWS, dtype=jnp.int32)
    group_of = sorted_cluster // 2
    offset = position - group_start[group_of]
    result = per_group[group_of, offset]
    scattered = jnp.zeros((ROWS,), jnp.float32).at[order].set(result)
    own_size = cluster_sizes[cluster_of]
    return jnp.where(rank_in < own_size, scattered, jnp.float32(-1.0))
```

```python
import itertools

import jax
import jax.numpy as jnp
import numpy as np
from jax import lax
from jax.experimental import pallas as pl
from jax.experimental.pallas import tpu as pltpu
from jax.sharding import Mesh
from jax.sharding import PartitionSpec as P

SLOTS = 1280
GROUPS = 16
BLOCKS = 8
WIDTH = 512
LOCAL = 512
CHIPS = 64
ROWS = 24
DATA = 20
PART = 5
SENT = CHIPS * ROWS
ODD = 16384

COVERS = {
    1: ((0, 1, 0, 1),),
    2: ((0, 1, 2, 3),),
    3: ((0, 1, 4, 5), (1, 2, 3, 5), (0, 2, 3, 4)),
    4: ((1, 3, 6, 7), (1, 4, 5, 7), (0, 3, 4, 6), (0, 2, 3, 5), (0, 1, 2, 7), (2, 4, 5, 6)),
    5: (
        (3, 4, 6, 8), (3, 5, 8, 9), (2, 5, 6, 9), (1, 2, 3, 8), (0, 1, 6, 7),
        (1, 4, 5, 9), (0, 2, 4, 7), (0, 7, 8, 9), (0, 3, 5, 7),
    ),
    6: (
        (4, 5, 8, 10), (3, 6, 8, 11), (0, 4, 7, 11), (0, 1, 6, 10), (1, 7, 8, 9),
        (3, 5, 7, 10), (1, 3, 4, 9), (0, 5, 6, 9), (2, 9, 10, 11), (0, 2, 3, 8),
        (1, 2, 5, 11), (2, 4, 6, 7),
    ),
    7: (
        (0, 1, 5, 13), (3, 5, 8, 10), (0, 7, 10, 11), (2, 11, 12, 13), (2, 7, 8, 11),
        (1, 4, 10, 12), (8, 9, 12, 13), (1, 3, 4, 7), (4, 7, 9, 13), (3, 6, 10, 13),
        (0, 1, 2, 8), (0, 4, 6, 8), (2, 4, 5, 11), (0, 3, 9, 12), (5, 6, 7, 12),
        (2, 5, 9, 10), (1, 6, 9, 11), (2, 3, 6, 11),
    ),
}


def affine_plane():
    times = ((0, 0, 0, 0), (0, 1, 2, 3), (0, 2, 3, 1), (0, 3, 1, 2))
    lines = [tuple(4 * x + y for y in range(4)) for x in range(4)]
    for slope in range(4):
        for shift in range(4):
            lines.append(tuple(4 * x + (times[slope][x] ^ shift) for x in range(4)))
    return tuple(lines)


COVERS[8] = affine_plane()
for _m, _units in COVERS.items():
    _met = {frozenset(p) for unit in _units for p in itertools.combinations(unit, 2)}
    assert all(frozenset(p) in _met for p in itertools.combinations(range(2 * _m), 2))

COUNT_AT = 80
BASE_AT = 96


def plan_table():
    table = np.zeros((128,), np.int32)
    at = 0
    for m in range(1, 9):
        table[COUNT_AT + m] = len(COVERS[m])
        table[BASE_AT + m] = at
        for unit in COVERS[m]:
            table[at] = sum(point << (4 * k) for k, point in enumerate(unit))
            at += 1
    assert at <= COUNT_AT
    return table


def plan(sizes, covers, first_unit, table):
    def emit(m, count, half, unit):
        base = covers[BASE_AT + m]

        def one(k, carry):
            here = unit + k - first_unit

            @pl.when((here >= 0) & (here < CHIPS))
            def _():
                points = covers[base + k]
                for a in range(4):
                    table[here * 4 + a] = half + ((points >> (4 * a)) & 15)

            return carry

        lax.fori_loop(0, count, one, 0)
        return unit + count

    def group(g, unit):
        first, second = sizes[2 * g], sizes[2 * g + 1]
        blocks_a = (first + SLOTS - 1) // SLOTS
        start_b = first // SLOTS
        blocks_b = (first + second + SLOTS - 1) // SLOTS - start_b
        shared = blocks_a > start_b
        skip_a = (blocks_a == 1) & shared & (blocks_b >= 2)
        skip_b = (blocks_b == 1) & shared
        count_a = jnp.where(skip_a, 0, covers[COUNT_AT + blocks_a])
        count_b = jnp.where(skip_b, 0, covers[COUNT_AT + blocks_b])
        unit = emit(blocks_a, count_a, g * 2 * BLOCKS, unit)
        return emit(blocks_b, count_b, g * 2 * BLOCKS + 2 * start_b, unit)

    total = lax.fori_loop(0, GROUPS, group, jnp.int32(0))

    def clear(k, carry):
        for a in range(4):
            table[k * 4 + a] = -1
        return carry

    lax.fori_loop(jnp.clip(total - first_unit, 0, CHIPS), CHIPS, clear, 0)
    return total


def pack_kernel(
    sizes, covers, first_unit, emb, cluster, rank,
    sent, row_key_out, slot_key_out, total_out, table, unit, pick,
):
    total_out[0] = plan(sizes, covers, first_unit[0], table)

    values = emb[...].astype(jnp.float32)
    scale = 1.0 / jnp.sqrt(jnp.sum(values * values, axis=1, keepdims=True) + 1e-06)
    unit[...] = (values * scale).astype(jnp.bfloat16)

    cluster_of = cluster[...]
    rank_in = rank[...]
    odd = cluster_of % 2
    previous = jnp.zeros_like(cluster_of)
    own_size = jnp.zeros_like(cluster_of)
    for c in range(2 * GROUPS):
        own_size = jnp.where(cluster_of == c, sizes[c], own_size)
        if c % 2 == 1:
            previous = jnp.where(cluster_of == c, sizes[c - 1], previous)
    place = rank_in + previous
    block = jnp.zeros_like(cluster_of)
    for k in range(1, BLOCKS):
        block = block + jnp.where(place >= k * SLOTS, 1, 0)
    bin_of = (cluster_of // 2) * BLOCKS + block
    bins = lax.broadcasted_iota(jnp.int32, (GROUPS * BLOCKS, LOCAL), 0)
    member = jnp.where(bins == bin_of, 1.0, 0.0)
    earlier = (
        lax.broadcasted_iota(jnp.int32, (LOCAL, LOCAL), 0)
        < lax.broadcasted_iota(jnp.int32, (LOCAL, LOCAL), 1)
    )
    before = jnp.dot(
        member.astype(jnp.bfloat16),
        jnp.where(earlier, 1.0, 0.0).astype(jnp.bfloat16),
        preferred_element_type=jnp.float32,
    )
    bucket = jnp.sum(member * before, axis=0, keepdims=True).astype(jnp.int32)
    row_key = (bin_of * 2 + bucket % 2) * 8 + bucket // 2
    row_key_out[...] = jnp.where(rank_in < own_size, row_key, -7)

    high = (rank_in // 128 + 1 + odd * (ODD // 128)).astype(jnp.float32)
    low = (rank_in % 128).astype(jnp.float32)
    upper_half = lax.broadcasted_iota(jnp.int32, (128, LOCAL), 0) >= 64
    tags = jnp.where(upper_half, low, high).astype(jnp.bfloat16)

    lane = lax.broadcasted_iota(jnp.int32, (1, 128), 1)
    slot = lax.broadcasted_iota(jnp.int32, (2 * ROWS, 128), 0)
    second = slot >= ROWS
    slot = jnp.where(second, slot - ROWS, slot)

    def keys_of(at, index):
        key = jnp.full(index.shape, -1, jnp.int32)
        for a in range(4):
            inside = (index >= PART * a) & (index < PART * (a + 1))
            key = jnp.where(inside, table[at * 4 + a] * 8 + index - PART * a, key)
        return key

    def build(k, carry):
        even, odd_key = keys_of(2 * k, slot), keys_of(2 * k + 1, slot)
        key = jnp.where(second, odd_key, even)
        for c in range(LOCAL // 128):
            lanes = pl.ds(c * 128, 128)
            hit = key == row_key[:, c * 128 : (c + 1) * 128]
            pick[pl.ds(pl.multiple_of(k * 48, 16), 48), lanes] = jnp.where(hit, 1.0, 0.0).astype(
                jnp.bfloat16
            )
        return carry

    lax.fori_loop(0, CHIPS // 2, build, 0)

    def slots(k, carry):
        slot_key_out[pl.ds(k, 1), :] = keys_of(k, lane)
        return carry

    lax.fori_loop(0, CHIPS, slots, 0)

    some = 16
    tag_slot = lax.broadcasted_iota(jnp.int32, (1, ROWS, 128), 1)
    tag_lane = lax.broadcasted_iota(jnp.int32, (1, ROWS, 128), 2)
    diagonal = (tag_lane % 64) == tag_slot

    def send(k, carry):
        rows = pl.ds(pl.multiple_of(k * some * ROWS, 16), some * ROWS)
        chosen = pick[rows, :]
        data = jnp.dot(chosen, unit[...], preferred_element_type=jnp.float32)
        tag = lax.dot_general(
            chosen, tags, (((1,), (1,)), ((), ())), preferred_element_type=jnp.float32
        ).reshape(some, ROWS, 128)
        tag = jnp.sum(jnp.where(diagonal, tag, 0.0), axis=1, keepdims=True)
        tag = jnp.where(tag_slot == DATA, tag, 0.0).reshape(some * ROWS, 128)
        sent[rows, pl.ds(0, 128)] = (data[:, :128] + tag).astype(jnp.bfloat16)
        sent[rows, pl.ds(128, WIDTH - 128)] = data[:, 128:].astype(jnp.bfloat16)
        return carry

    lax.fori_loop(0, CHIPS // some, send, 0)


def place_of(rows):
    source = lax.broadcasted_iota(jnp.int32, (CHIPS, SENT), 0)
    at = lax.broadcasted_iota(jnp.int32, (CHIPS, SENT), 1)
    is_tag = jnp.where(at == source * ROWS + DATA, 1.0, 0.0).astype(jnp.bfloat16)
    tag = jnp.dot(is_tag, rows[:, pl.ds(0, 128)], preferred_element_type=jnp.float32)
    slot = lax.broadcasted_iota(jnp.int32, (1, ROWS, 128), 1)
    lane = lax.broadcasted_iota(jnp.int32, (1, ROWS, 128), 2)
    weight = jnp.where(lane == slot, 128.0, 0.0) + jnp.where(lane == slot + 64, 1.0, 0.0)
    every = jnp.broadcast_to(tag.reshape(CHIPS, 1, 128), (CHIPS, ROWS, 128))
    return jnp.sum(every * weight, axis=2, keepdims=True).reshape(SENT, 1)


def along_lanes(column):
    diagonal = lax.broadcasted_iota(jnp.int32, (128, 128), 0) == lax.broadcasted_iota(
        jnp.int32, (128, 128), 1
    )
    parts = []
    for c in range(SENT // 128):
        part = jnp.broadcast_to(column[c * 128 : (c + 1) * 128, :], (128, 128))
        parts.append(jnp.sum(jnp.where(diagonal, part, 0.0), axis=0, keepdims=True))
    return jnp.concatenate(parts, axis=1)


def best_kernel(last, own, other, start, out, key_rows, key_lanes, best):
    mine = place_of(own)
    key_rows[...] = jnp.broadcast_to(mine, (SENT, 128))
    key_lanes[...] = along_lanes(place_of(other) if last else mine)
    best[...] = start[...] if last else jnp.full_like(best, -1.0)
    tall, wide = 512, 256
    for j in range(SENT // wide):
        columns = other[pl.ds(j * wide, wide), :]
        for i in range(SENT // tall):
            rows = pl.ds(i * tall, tall)
            score = lax.dot_general(
                own[rows, :], columns, (((1,), (1,)), ((), ())),
                preferred_element_type=jnp.float32,
            )
            key = key_rows[rows, :]
            floor = jnp.where(key >= ODD, float(ODD), 128.0)
            top = best[rows, :]
            for c in range(wide // 128):
                col = key_lanes[:, pl.ds(j * wide + c * 128, 128)]
                allowed = (col < key) & (col >= floor)
                top = jnp.maximum(
                    top, jnp.where(allowed, score[:, c * 128 : (c + 1) * 128], -1.0)
                )
            best[rows, :] = top
    if not last:
        out[...] = best[...]
    else:
        top = jnp.max(best[...], axis=1, keepdims=True)
        top = jnp.broadcast_to(top, (SENT, 128)).reshape(CHIPS, ROWS, 128)
        slot = lax.broadcasted_iota(jnp.int32, (1, ROWS, 128), 1)
        lane = lax.broadcasted_iota(jnp.int32, (1, ROWS, 128), 2)
        out[...] = jnp.max(jnp.where(slot == lane, top, -1.0), axis=1)


def merge_kernel(answers, slot_key, row_key, out):
    keys = row_key[...]
    best = jnp.full((CHIPS, LOCAL), -1.0, jnp.float32)
    for t in range(DATA):
        hit = slot_key[:, pl.ds(t, 1)] == keys
        best = jnp.maximum(best, jnp.where(hit, answers[:, pl.ds(t, 1)], -1.0))
    out[...] = jnp.max(best, axis=0, keepdims=True)


VMEM = pl.BlockSpec(memory_space=pltpu.VMEM)
SMEM = pl.BlockSpec(memory_space=pltpu.SMEM)
LIMIT = 48 * 1024 * 1024


def pack(sizes, first_unit, emb, cluster, rank):
    return pl.pallas_call(
        pack_kernel,
        out_shape=(
            jax.ShapeDtypeStruct((SENT, WIDTH), jnp.bfloat16),
            jax.ShapeDtypeStruct((1, LOCAL), jnp.int32),
            jax.ShapeDtypeStruct((CHIPS, 128), jnp.int32),
            jax.ShapeDtypeStruct((1,), jnp.int32),
        ),
        in_specs=[SMEM, SMEM, SMEM, VMEM, VMEM, VMEM],
        out_specs=(VMEM, VMEM, VMEM, SMEM),
        scratch_shapes=[
            pltpu.SMEM((CHIPS * 4,), jnp.int32),
            pltpu.VMEM((LOCAL, WIDTH), jnp.bfloat16),
            pltpu.VMEM((SENT, LOCAL), jnp.bfloat16),
        ],
        compiler_params=pltpu.CompilerParams(vmem_limit_bytes=LIMIT),
        cost_estimate=pl.CostEstimate(
            flops=2 * SENT * LOCAL * 640, bytes_accessed=2**21, transcendentals=0
        ),
        name="pack",
    )(sizes, jnp.asarray(plan_table()), first_unit, emb, cluster, rank)


def best_of(own, other, start):
    last = start is not None

    def kernel(*refs):
        if last:
            best_kernel(True, *refs)
        else:
            own, out, *scratch = refs
            best_kernel(False, own, own, None, out, *scratch)

    operands = (own, other, start) if last else (own,)
    shape = (CHIPS, 128) if last else (SENT, 128)
    return pl.pallas_call(
        kernel,
        out_shape=jax.ShapeDtypeStruct(shape, jnp.float32),
        in_specs=[VMEM] * len(operands),
        out_specs=VMEM,
        scratch_shapes=[
            pltpu.VMEM((SENT, 128), jnp.float32),
            pltpu.VMEM((1, SENT), jnp.float32),
            pltpu.VMEM((SENT, 128), jnp.float32),
        ],
        compiler_params=pltpu.CompilerParams(vmem_limit_bytes=LIMIT),
        cost_estimate=pl.CostEstimate(
            flops=2 * SENT * SENT * WIDTH, bytes_accessed=2**21, transcendentals=0
        ),
        name="best_last" if last else "best_own",
    )(*operands)


def merge(answers, slot_key, row_key):
    return pl.pallas_call(
        merge_kernel,
        out_shape=jax.ShapeDtypeStruct((1, LOCAL), jnp.float32),
        in_specs=[VMEM, VMEM, VMEM],
        out_specs=VMEM,
        name="merge",
    )(answers, slot_key, row_key)


def exchange(values):
    return lax.all_to_all(values, ("x", "y", "z"), split_axis=0, concat_axis=0, tiled=True)


def one_round(first_unit, embeddings, sizes, cluster, rank):
    sent, row_key, slot_key, total = pack(sizes, first_unit, embeddings, cluster, rank)
    own = exchange(sent.reshape(CHIPS, ROWS, WIDTH)).reshape(SENT, WIDTH)
    other = lax.ppermute(own, "core", [(0, 1), (1, 0)])
    answers = best_of(own, other, best_of(own, None, None))
    return merge(exchange(answers), slot_key, row_key), total


def body(embeddings, cluster_sizes, cluster_of, rank_in):
    cluster = cluster_of.reshape(1, LOCAL)
    rank = rank_in.reshape(1, LOCAL)
    result, total = one_round(
        jnp.zeros((1,), jnp.int32), embeddings, cluster_sizes, cluster, rank
    )

    def more(carry):
        return carry[0] < total[0]

    def again(carry):
        unit, best = carry
        extra, _ = one_round(unit.reshape(1), embeddings, cluster_sizes, cluster, rank)
        return unit + CHIPS, jnp.maximum(best, extra)

    _, result = lax.while_loop(more, again, (jnp.int32(CHIPS), result))
    return result.reshape(LOCAL)


def solution(mesh):
    chips = Mesh(mesh.devices.reshape(4, 4, 4, 2), ("x", "y", "z", "core"))
    every = ("x", "y", "z", "core")
    in_specs = (P(every, None), P(), P(every), P(every))
    return jax.shard_map(
        body, mesh=chips, in_specs=in_specs, out_specs=P(every), check_vma=False
    )
```

```python
import itertools

import jax
import jax.numpy as jnp
from jax import lax
from jax.experimental import pallas as pl
from jax.experimental.pallas import tpu as pltpu
from jax.sharding import Mesh
from jax.sharding import PartitionSpec as P

SLOTS = 1280
GROUPS = 16
BLOCKS = 8
WIDTH = 512
LOCAL = 512
CHIPS = 64
ROWS = 24
DATA = 20
PART = 5
SENT = CHIPS * ROWS
ODD = 16384

COVERS = {
    1: ((0, 1, 0, 1),),
    2: ((0, 1, 2, 3),),
    3: ((0, 1, 4, 5), (1, 2, 3, 5), (0, 2, 3, 4)),
    4: ((1, 3, 6, 7), (1, 4, 5, 7), (0, 3, 4, 6), (0, 2, 3, 5), (0, 1, 2, 7), (2, 4, 5, 6)),
    5: (
        (3, 4, 6, 8), (3, 5, 8, 9), (2, 5, 6, 9), (1, 2, 3, 8), (0, 1, 6, 7),
        (1, 4, 5, 9), (0, 2, 4, 7), (0, 7, 8, 9), (0, 3, 5, 7),
    ),
    6: (
        (4, 5, 8, 10), (3, 6, 8, 11), (0, 4, 7, 11), (0, 1, 6, 10), (1, 7, 8, 9),
        (3, 5, 7, 10), (1, 3, 4, 9), (0, 5, 6, 9), (2, 9, 10, 11), (0, 2, 3, 8),
        (1, 2, 5, 11), (2, 4, 6, 7),
    ),
    7: (
        (0, 1, 5, 13), (3, 5, 8, 10), (0, 7, 10, 11), (2, 11, 12, 13), (2, 7, 8, 11),
        (1, 4, 10, 12), (8, 9, 12, 13), (1, 3, 4, 7), (4, 7, 9, 13), (3, 6, 10, 13),
        (0, 1, 2, 8), (0, 4, 6, 8), (2, 4, 5, 11), (0, 3, 9, 12), (5, 6, 7, 12),
        (2, 5, 9, 10), (1, 6, 9, 11), (2, 3, 6, 11),
    ),
}


def affine_plane():
    times = ((0, 0, 0, 0), (0, 1, 2, 3), (0, 2, 3, 1), (0, 3, 1, 2))
    lines = [tuple(4 * x + y for y in range(4)) for x in range(4)]
    for slope in range(4):
        for shift in range(4):
            lines.append(tuple(4 * x + (times[slope][x] ^ shift) for x in range(4)))
    return tuple(lines)


COVERS[8] = affine_plane()
for _m, _units in COVERS.items():
    _met = {frozenset(p) for unit in _units for p in itertools.combinations(unit, 2)}
    assert all(frozenset(p) in _met for p in itertools.combinations(range(2 * _m), 2))


def covers_by_lane():
    lane = lax.broadcasted_iota(jnp.int32, (8, 128), 1)
    packed = jnp.zeros((8, 128), jnp.int32)
    at = 0
    for m in range(1, BLOCKS + 1):
        for unit in COVERS[m]:
            value = sum(point << (4 * k) for k, point in enumerate(unit))
            packed = packed + jnp.where(lane == at, value, 0)
            at += 1
    assert at <= 128
    return packed


def by_blocks(m, values):
    picked = jnp.zeros_like(m)
    for k in range(1, BLOCKS + 1):
        picked = jnp.where(m == k, float(values[k]), picked)
    return picked


def full_blocks(places):
    return jnp.floor((places + 0.5) * (1.0 / SLOTS))


def plan(row, first_unit):
    clusters = 2 * GROUPS
    down = lax.broadcasted_iota(jnp.int32, (clusters, clusters), 0)
    across = lax.broadcasted_iota(jnp.int32, (clusters, clusters), 1)
    row = jnp.broadcast_to(row, (clusters, clusters))

    def column(mask):
        picked = jnp.sum(jnp.where(mask, row, 0.0), axis=1, keepdims=True)
        return jnp.broadcast_to(picked, (clusters, 128))

    size = column(down == across)
    partner = column(down == across + 1 - 2 * (across % 2))
    index = lax.broadcasted_iota(jnp.int32, (clusters, 128), 0)
    odd = index % 2 == 1
    first = jnp.where(odd, partner, size)
    blocks_a = full_blocks(first + (SLOTS - 1))
    start_b = full_blocks(first)
    blocks_b = full_blocks(size + partner + (SLOTS - 1)) - start_b
    blocks = jnp.where(odd, blocks_b, blocks_a)
    begin = jnp.where(odd, start_b, 0.0)
    counts = [0] + [len(COVERS[m]) for m in range(1, BLOCKS + 1)]
    alone = by_blocks(blocks, counts)
    held = (blocks == 1.0) & (blocks_a > start_b) & (odd | (blocks_b >= 2.0))
    shared = jnp.where(jnp.sum(alone, axis=0, keepdims=True) <= CHIPS, 0.0, 1.0)
    count = alone * (1.0 - shared * jnp.where(held, 1.0, 0.0))
    total = jnp.sum(count, axis=0, keepdims=True)
    start = jnp.dot(
        jnp.where(across < down, 1.0, 0.0).astype(jnp.bfloat16),
        count.astype(jnp.bfloat16),
        preferred_element_type=jnp.float32,
    )
    unit = (lax.broadcasted_iota(jnp.int32, (1, 128), 1) + first_unit).astype(jnp.float32)
    mine = (unit >= start) & (unit < start + count)

    def of_unit(values):
        return jnp.sum(jnp.where(mine, values, 0.0), axis=0, keepdims=True)

    bases = [0] + [sum(counts[:m]) for m in range(1, BLOCKS + 1)]
    entry = of_unit(by_blocks(blocks, bases) - start) + unit
    group = (index // 2).astype(jnp.float32)
    kind = 2.0 * shared + (1.0 - shared) * jnp.where(odd, 1.0, 0.0)
    half = of_unit(group * (2 * BLOCKS) + 2.0 * begin + 256.0 * kind)
    used = of_unit(jnp.where(blocks == 1.0, 1.0, 2.0))
    entry = jnp.broadcast_to(jnp.clip(entry, 0.0, 127.0).astype(jnp.int32), (8, 128))
    points = jnp.take_along_axis(covers_by_lane(), entry, axis=1)[0:1, :]
    diagonal = lax.broadcasted_iota(jnp.int32, (CHIPS, 128), 0) == lax.broadcasted_iota(
        jnp.int32, (CHIPS, 128), 1
    )
    table = []
    for a in range(4):
        point = ((points >> (4 * a)) & 15).astype(jnp.float32)
        held_by = jnp.where(used > (a // 2) + 0.5, half + point, 1024.0)
        held_by = jnp.sum(jnp.where(diagonal, held_by, 0.0), axis=1, keepdims=True)
        table.append(jnp.broadcast_to(held_by, (CHIPS, 128)))
    return table, size, jnp.where(odd, partner, 0.0), shared, total


def pack_kernel(
    first_unit, sizes, emb, cluster, rank, sent, row_key_out, slot_key_out, total_out, unit
):
    values = emb[...].astype(jnp.float32)
    scale = 1.0 / jnp.sqrt(jnp.sum(values * values, axis=1, keepdims=True) + 1e-06)
    unit[...] = (values * scale).astype(jnp.bfloat16)

    table, size, previous, shared, total = plan(sizes[...].astype(jnp.float32), first_unit)
    total_out[...] = total.astype(jnp.int32)

    def wide(column):
        return jnp.concatenate([column] * (LOCAL // 128), axis=1)

    cluster_of = cluster[...]
    rank_in = rank[...].astype(jnp.float32)
    own = lax.broadcasted_iota(jnp.int32, (2 * GROUPS, LOCAL), 0) == cluster_of
    own_size = jnp.sum(jnp.where(own, wide(size), 0.0), axis=0, keepdims=True)
    place = rank_in + jnp.sum(jnp.where(own, wide(previous), 0.0), axis=0, keepdims=True)
    bin_of = (cluster_of // 2) * BLOCKS + full_blocks(place).astype(jnp.int32)
    bins = lax.broadcasted_iota(jnp.int32, (GROUPS * BLOCKS, LOCAL), 0)
    member = jnp.where(bins == bin_of, 1.0, 0.0)
    until = lax.broadcasted_iota(jnp.int32, (128, 256), 0) <= lax.broadcasted_iota(
        jnp.int32, (128, 256), 1
    )
    until = jnp.where(until, 1.0, 0.0).astype(jnp.bfloat16)
    passed = jnp.full((GROUPS * BLOCKS, 128), -1.0, jnp.float32)
    bucket = []
    for c in range(LOCAL // 128):
        part = member[:, c * 128 : (c + 1) * 128]
        seen = jnp.dot(part.astype(jnp.bfloat16), until, preferred_element_type=jnp.float32)
        before = passed + seen[:, :128]
        passed = passed + seen[:, 128:]
        bucket.append(jnp.sum(part * before, axis=0, keepdims=True))
    bucket = jnp.concatenate(bucket, axis=1)
    upper = jnp.floor((bucket + 0.5) * 0.5)
    odd = cluster_of % 2
    kind = wide(shared)
    kind = 2.0 * kind + (1.0 - kind) * odd.astype(jnp.float32)
    half_key = bin_of.astype(jnp.float32) * 2.0 + (bucket - 2.0 * upper) + 256.0 * kind
    row_key = half_key * 8.0 + upper
    row_key_out[...] = jnp.where(rank_in < own_size, row_key, -7.0)

    lane = lax.broadcasted_iota(jnp.int32, (1, 128), 1)
    slot_key = jnp.full((CHIPS, 128), -1.0, jnp.float32)
    for a in range(4):
        inside = (lane >= PART * a) & (lane < PART * (a + 1))
        slot_key = jnp.where(
            inside, table[a] * 8.0 + (lane - PART * a).astype(jnp.float32), slot_key
        )
    slot_key_out[...] = slot_key

    high = jnp.floor((rank_in + 0.5) * (1.0 / 128))
    low = rank_in - 128.0 * high
    high = high + 1.0 + (odd * (ODD // 128)).astype(jnp.float32)
    upper_half = lax.broadcasted_iota(jnp.int32, (128, LOCAL), 0) >= 64
    tags = jnp.where(upper_half, low, high).astype(jnp.bfloat16)

    some = 16
    slot = lax.broadcasted_iota(jnp.int32, (some, ROWS, 128), 1)
    tag_lane = lax.broadcasted_iota(jnp.int32, (some, ROWS, 128), 2)
    diagonal = (tag_lane % 64) == slot
    rest = slot
    for a in range(1, 4):
        rest = rest - jnp.where(slot >= PART * a, PART, 0)
    rest = rest.astype(jnp.float32)
    for k in range(CHIPS // some):
        key = jnp.full((some, ROWS, 128), -64.0, jnp.float32)
        for a in range(3, -1, -1):
            part = table[a][k * some : (k + 1) * some, :].reshape(some, 1, 128)
            part = jnp.broadcast_to(part, (some, ROWS, 128)) * 8.0
            key = jnp.where(slot < PART * (a + 1), part, key)
        key = (key + rest).reshape(some * ROWS, 128)
        chosen = []
        for c in range(LOCAL // 128):
            hit = key == row_key[:, c * 128 : (c + 1) * 128]
            chosen.append(jnp.where(hit, 1.0, 0.0).astype(jnp.bfloat16))
        chosen = jnp.concatenate(chosen, axis=1)
        rows = pl.ds(k * some * ROWS, some * ROWS)
        data = jnp.dot(chosen, unit[...], preferred_element_type=jnp.float32)
        tag = lax.dot_general(
            chosen, tags, (((1,), (1,)), ((), ())), preferred_element_type=jnp.float32
        ).reshape(some, ROWS, 128)
        tag = jnp.sum(jnp.where(diagonal, tag, 0.0), axis=1, keepdims=True)
        tag = jnp.where(slot == DATA, tag, 0.0).reshape(some * ROWS, 128)
        sent[rows, pl.ds(0, 128)] = (data[:, :128] + tag).astype(jnp.bfloat16)
        sent[rows, pl.ds(128, WIDTH - 128)] = data[:, 128:].astype(jnp.bfloat16)


def place_of(rows):
    source = lax.broadcasted_iota(jnp.int32, (CHIPS, SENT), 0)
    at = lax.broadcasted_iota(jnp.int32, (CHIPS, SENT), 1)
    is_tag = jnp.where(at == source * ROWS + DATA, 1.0, 0.0).astype(jnp.bfloat16)
    tag = jnp.dot(is_tag, rows[:, pl.ds(0, 128)], preferred_element_type=jnp.float32)
    slot = lax.broadcasted_iota(jnp.int32, (1, ROWS, 128), 1)
    lane = lax.broadcasted_iota(jnp.int32, (1, ROWS, 128), 2)
    weight = jnp.where(lane == slot, 128.0, 0.0) + jnp.where(lane == slot + 64, 1.0, 0.0)
    every = jnp.broadcast_to(tag.reshape(CHIPS, 1, 128), (CHIPS, ROWS, 128))
    return jnp.sum(every * weight, axis=2, keepdims=True).reshape(SENT, 1)


def along_lanes(column):
    diagonal = lax.broadcasted_iota(jnp.int32, (128, 128), 0) == lax.broadcasted_iota(
        jnp.int32, (128, 128), 1
    )
    parts = []
    for c in range(SENT // 128):
        part = jnp.broadcast_to(column[c * 128 : (c + 1) * 128, :], (128, 128))
        parts.append(jnp.sum(jnp.where(diagonal, part, 0.0), axis=0, keepdims=True))
    return jnp.concatenate(parts, axis=1)


def best_kernel(last, own, other, start, out, key_rows, key_lanes, best):
    mine = place_of(own)
    key_rows[...] = jnp.broadcast_to(mine, (SENT, 128))
    key_lanes[...] = along_lanes(place_of(other) if last else mine)
    best[...] = start[...] if last else jnp.full_like(best, -1.0)
    tall, wide = 512, 256
    for j in range(SENT // wide):
        columns = other[pl.ds(j * wide, wide), :]
        for i in range(SENT // tall):
            rows = pl.ds(i * tall, tall)
            score = lax.dot_general(
                own[rows, :], columns, (((1,), (1,)), ((), ())),
                preferred_element_type=jnp.float32,
            )
            key = key_rows[rows, :]
            floor = jnp.where(key >= ODD, float(ODD), 128.0)
            top = best[rows, :]
            for c in range(wide // 128):
                col = key_lanes[:, pl.ds(j * wide + c * 128, 128)]
                allowed = (col < key) & (col >= floor)
                top = jnp.maximum(
                    top, jnp.where(allowed, score[:, c * 128 : (c + 1) * 128], -1.0)
                )
            best[rows, :] = top
    if not last:
        out[...] = best[...]
    else:
        top = jnp.max(best[...], axis=1, keepdims=True)
        top = jnp.broadcast_to(top, (SENT, 128)).reshape(CHIPS, ROWS, 128)
        slot = lax.broadcasted_iota(jnp.int32, (1, ROWS, 128), 1)
        lane = lax.broadcasted_iota(jnp.int32, (1, ROWS, 128), 2)
        out[...] = jnp.max(jnp.where(slot == lane, top, -1.0), axis=1)


def merge_kernel(answers, slot_key, row_key, out):
    keys = row_key[...]
    best = jnp.full((CHIPS, LOCAL), -1.0, jnp.float32)
    for t in range(DATA):
        hit = slot_key[:, pl.ds(t, 1)] == keys
        best = jnp.maximum(best, jnp.where(hit, answers[:, pl.ds(t, 1)], -1.0))
    out[...] = jnp.max(best, axis=0, keepdims=True)


VMEM = pl.BlockSpec(memory_space=pltpu.VMEM)
SMEM = pl.BlockSpec(memory_space=pltpu.SMEM)
LIMIT = 48 * 1024 * 1024


def pack(sizes, first_unit, emb, cluster, rank):
    later = first_unit is not None

    def kernel(*refs):
        if later:
            pack_kernel(refs[0][0], *refs[1:])
        else:
            pack_kernel(0, *refs)

    return pl.pallas_call(
        kernel,
        out_shape=(
            jax.ShapeDtypeStruct((SENT, WIDTH), jnp.bfloat16),
            jax.ShapeDtypeStruct((1, LOCAL), jnp.float32),
            jax.ShapeDtypeStruct((CHIPS, 128), jnp.float32),
            jax.ShapeDtypeStruct((1, 128), jnp.int32),
        ),
        in_specs=[SMEM] * later + [VMEM, VMEM, VMEM, VMEM],
        out_specs=(VMEM, VMEM, VMEM, VMEM),
        scratch_shapes=[pltpu.VMEM((LOCAL, WIDTH), jnp.bfloat16)],
        compiler_params=pltpu.CompilerParams(vmem_limit_bytes=LIMIT),
        cost_estimate=pl.CostEstimate(
            flops=2 * SENT * LOCAL * 640, bytes_accessed=2**21, transcendentals=0
        ),
        name="pack_later" if later else "pack",
    )(*((first_unit,) if later else ()), sizes, emb, cluster, rank)


def best_of(own, other, start):
    last = start is not None

    def kernel(*refs):
        if last:
            best_kernel(True, *refs)
        else:
            own, out, *scratch = refs
            best_kernel(False, own, own, None, out, *scratch)

    operands = (own, other, start) if last else (own,)
    shape = (CHIPS, 128) if last else (SENT, 128)
    return pl.pallas_call(
        kernel,
        out_shape=jax.ShapeDtypeStruct(shape, jnp.float32),
        in_specs=[VMEM] * len(operands),
        out_specs=VMEM,
        scratch_shapes=[
            pltpu.VMEM((SENT, 128), jnp.float32),
            pltpu.VMEM((1, SENT), jnp.float32),
            pltpu.VMEM((SENT, 128), jnp.float32),
        ],
        compiler_params=pltpu.CompilerParams(vmem_limit_bytes=LIMIT),
        cost_estimate=pl.CostEstimate(
            flops=2 * SENT * SENT * WIDTH, bytes_accessed=2**21, transcendentals=0
        ),
        name="best_last" if last else "best_own",
    )(*operands)


def merge(answers, slot_key, row_key):
    return pl.pallas_call(
        merge_kernel,
        out_shape=jax.ShapeDtypeStruct((1, LOCAL), jnp.float32),
        in_specs=[VMEM, VMEM, VMEM],
        out_specs=VMEM,
        compiler_params=pltpu.CompilerParams(vmem_limit_bytes=16 * 1024 * 1024),
        name="merge",
    )(answers, slot_key, row_key)


def exchange(values):
    return lax.all_to_all(values, ("x", "y", "z"), split_axis=0, concat_axis=0, tiled=True)


def one_round(first_unit, embeddings, sizes, cluster, rank):
    sent, row_key, slot_key, total = pack(sizes, first_unit, embeddings, cluster, rank)
    own = exchange(sent.reshape(CHIPS, ROWS, WIDTH)).reshape(SENT, WIDTH)
    other = lax.ppermute(own, "core", [(0, 1), (1, 0)])
    answers = best_of(own, other, best_of(own, None, None))
    return merge(exchange(answers), slot_key, row_key), total


def body(embeddings, cluster_sizes, cluster_of, rank_in):
    sizes = cluster_sizes.reshape(1, 2 * GROUPS)
    cluster = cluster_of.reshape(1, LOCAL)
    rank = rank_in.reshape(1, LOCAL)
    result, total = one_round(None, embeddings, sizes, cluster, rank)

    def more(carry):
        return carry[0] < total[0, 0]

    def again(carry):
        unit, best = carry
        extra, _ = one_round(unit.reshape(1), embeddings, sizes, cluster, rank)
        return unit + CHIPS, jnp.maximum(best, extra)

    _, result = lax.while_loop(more, again, (jnp.int32(CHIPS), result))
    return result.reshape(LOCAL)


def solution(mesh):
    chips = Mesh(mesh.devices.reshape(4, 4, 4, 2), ("x", "y", "z", "core"))
    every = ("x", "y", "z", "core")
    in_specs = (P(every, None), P(), P(every), P(every))
    return jax.shard_map(
        body, mesh=chips, in_specs=in_specs, out_specs=P(every), check_vma=False
    )
```

```python
import itertools

import jax
import jax.numpy as jnp
from jax import lax
from jax.experimental import pallas as pl
from jax.experimental.pallas import tpu as pltpu
from jax.sharding import Mesh
from jax.sharding import PartitionSpec as P

SLOTS = 1280
GROUPS = 16
BLOCKS = 8
WIDTH = 512
LOCAL = 512
CHIPS = 64
ROWS = 24
DATA = 20
PART = 5
SENT = CHIPS * ROWS
ODD = 16384
EMPTY = 1048576.0

COVERS = {
    1: ((0, 1, 0, 1),),
    2: ((0, 1, 2, 3),),
    3: ((0, 1, 4, 5), (1, 2, 3, 5), (0, 2, 3, 4)),
    4: ((1, 3, 6, 7), (1, 4, 5, 7), (0, 3, 4, 6), (0, 2, 3, 5), (0, 1, 2, 7), (2, 4, 5, 6)),
    5: (
        (3, 4, 6, 8), (3, 5, 8, 9), (2, 5, 6, 9), (1, 2, 3, 8), (0, 1, 6, 7),
        (1, 4, 5, 9), (0, 2, 4, 7), (0, 7, 8, 9), (0, 3, 5, 7),
    ),
    6: (
        (4, 5, 8, 10), (3, 6, 8, 11), (0, 4, 7, 11), (0, 1, 6, 10), (1, 7, 8, 9),
        (3, 5, 7, 10), (1, 3, 4, 9), (0, 5, 6, 9), (2, 9, 10, 11), (0, 2, 3, 8),
        (1, 2, 5, 11), (2, 4, 6, 7),
    ),
    7: (
        (0, 1, 5, 13), (3, 5, 8, 10), (0, 7, 10, 11), (2, 11, 12, 13), (2, 7, 8, 11),
        (1, 4, 10, 12), (8, 9, 12, 13), (1, 3, 4, 7), (4, 7, 9, 13), (3, 6, 10, 13),
        (0, 1, 2, 8), (0, 4, 6, 8), (2, 4, 5, 11), (0, 3, 9, 12), (5, 6, 7, 12),
        (2, 5, 9, 10), (1, 6, 9, 11), (2, 3, 6, 11),
    ),
}


def affine_plane():
    times = ((0, 0, 0, 0), (0, 1, 2, 3), (0, 2, 3, 1), (0, 3, 1, 2))
    lines = [tuple(4 * x + y for y in range(4)) for x in range(4)]
    for slope in range(4):
        for shift in range(4):
            lines.append(tuple(4 * x + (times[slope][x] ^ shift) for x in range(4)))
    return tuple(lines)


COVERS[8] = affine_plane()
for _m, _units in COVERS.items():
    _met = {frozenset(p) for unit in _units for p in itertools.combinations(unit, 2)}
    assert all(frozenset(p) in _met for p in itertools.combinations(range(2 * _m), 2))


def covers_by_lane():
    lane = lax.broadcasted_iota(jnp.int32, (8, 128), 1)
    packed = jnp.zeros((8, 128), jnp.int32)
    at = 0
    for m in range(1, BLOCKS + 1):
        for unit in COVERS[m]:
            value = sum(point << (4 * k) for k, point in enumerate(unit))
            packed = packed + jnp.where(lane == at, value, 0)
            at += 1
    assert at <= 128
    return packed


def by_blocks(m, values):
    picked = jnp.zeros_like(m)
    for k in range(1, BLOCKS + 1):
        picked = jnp.where(m == k, float(values[k]), picked)
    return picked


def full_blocks(places):
    return jnp.floor((places + 0.5) * (1.0 / SLOTS))


def plan(row, first_unit):
    clusters = 2 * GROUPS
    down = lax.broadcasted_iota(jnp.int32, (clusters, clusters), 0)
    across = lax.broadcasted_iota(jnp.int32, (clusters, clusters), 1)
    row = jnp.broadcast_to(row, (clusters, clusters))

    def column(mask):
        picked = jnp.sum(jnp.where(mask, row, 0.0), axis=1, keepdims=True)
        return jnp.broadcast_to(picked, (clusters, 128))

    size = column(down == across)
    partner = column(down == across + 1 - 2 * (across % 2))
    index = lax.broadcasted_iota(jnp.int32, (clusters, 128), 0)
    odd = index % 2 == 1
    first = jnp.where(odd, partner, size)
    blocks_a = full_blocks(first + (SLOTS - 1))
    start_b = full_blocks(first)
    blocks_b = full_blocks(size + partner + (SLOTS - 1)) - start_b
    blocks = jnp.where(odd, blocks_b, blocks_a)
    begin = jnp.where(odd, start_b, 0.0)
    counts = [0] + [len(COVERS[m]) for m in range(1, BLOCKS + 1)]
    alone = by_blocks(blocks, counts)
    held = (blocks == 1.0) & (blocks_a > start_b) & (odd | (blocks_b >= 2.0))
    shared = jnp.where(jnp.sum(alone, axis=0, keepdims=True) <= CHIPS, 0.0, 1.0)
    count = alone * (1.0 - shared * jnp.where(held, 1.0, 0.0))
    total = jnp.sum(count, axis=0, keepdims=True)
    start = jnp.dot(
        jnp.where(across < down, 1.0, 0.0).astype(jnp.bfloat16),
        count.astype(jnp.bfloat16),
        preferred_element_type=jnp.float32,
    )
    unit = (lax.broadcasted_iota(jnp.int32, (1, 128), 1) + first_unit).astype(jnp.float32)
    mine = (unit >= start) & (unit < start + count)

    def of_unit(values):
        return jnp.sum(jnp.where(mine, values, 0.0), axis=0, keepdims=True)

    bases = [0] + [sum(counts[:m]) for m in range(1, BLOCKS + 1)]
    entry = of_unit(by_blocks(blocks, bases) - start) + unit
    group = (index // 2).astype(jnp.float32)
    kind = 2.0 * shared + (1.0 - shared) * jnp.where(odd, 1.0, 0.0)
    half = of_unit(group * (2 * BLOCKS) + 2.0 * begin + 256.0 * kind)
    used = of_unit(jnp.where(blocks == 1.0, 1.0, 2.0))
    entry = jnp.broadcast_to(jnp.clip(entry, 0.0, 127.0).astype(jnp.int32), (8, 128))
    points = jnp.take_along_axis(covers_by_lane(), entry, axis=1)[0:1, :]
    diagonal = lax.broadcasted_iota(jnp.int32, (CHIPS, 128), 0) == lax.broadcasted_iota(
        jnp.int32, (CHIPS, 128), 1
    )
    table = []
    for a in range(4):
        point = ((points >> (4 * a)) & 15).astype(jnp.float32)
        held_by = jnp.where(used > (a // 2) + 0.5, half + point, 1024.0)
        held_by = jnp.sum(jnp.where(diagonal, held_by, 0.0), axis=1, keepdims=True)
        table.append(jnp.broadcast_to(held_by, (CHIPS, 128)))
    return table, size, jnp.where(odd, partner, 0.0), shared, total


def pack_kernel(
    first_unit, sizes, emb, cluster, rank, sent, row_key_out, slot_key_out, total_out, unit
):
    values = emb[...].astype(jnp.float32)
    scale = 1.0 / jnp.sqrt(jnp.sum(values * values, axis=1, keepdims=True) + 1e-06)
    unit[...] = (values * scale).astype(jnp.bfloat16)

    table, size, previous, shared, total = plan(sizes[...].astype(jnp.float32), first_unit)
    total_out[...] = total.astype(jnp.int32)

    def wide(column):
        return jnp.concatenate([column] * (LOCAL // 128), axis=1)

    cluster_of = cluster[...]
    rank_in = rank[...].astype(jnp.float32)
    own = lax.broadcasted_iota(jnp.int32, (2 * GROUPS, LOCAL), 0) == cluster_of
    own_size = jnp.sum(jnp.where(own, wide(size), 0.0), axis=0, keepdims=True)
    place = rank_in + jnp.sum(jnp.where(own, wide(previous), 0.0), axis=0, keepdims=True)
    bin_of = (cluster_of // 2) * BLOCKS + full_blocks(place).astype(jnp.int32)
    bins = lax.broadcasted_iota(jnp.int32, (GROUPS * BLOCKS, LOCAL), 0)
    member = jnp.where(bins == bin_of, 1.0, 0.0)
    until = lax.broadcasted_iota(jnp.int32, (128, 256), 0) <= lax.broadcasted_iota(
        jnp.int32, (128, 256), 1
    )
    until = jnp.where(until, 1.0, 0.0).astype(jnp.bfloat16)
    passed = jnp.full((GROUPS * BLOCKS, 128), -1.0, jnp.float32)
    bucket = []
    for c in range(LOCAL // 128):
        part = member[:, c * 128 : (c + 1) * 128]
        seen = jnp.dot(part.astype(jnp.bfloat16), until, preferred_element_type=jnp.float32)
        before = passed + seen[:, :128]
        passed = passed + seen[:, 128:]
        bucket.append(jnp.sum(part * before, axis=0, keepdims=True))
    bucket = jnp.concatenate(bucket, axis=1)
    upper = jnp.floor((bucket + 0.5) * 0.5)
    odd = cluster_of % 2
    kind = wide(shared)
    kind = 2.0 * kind + (1.0 - kind) * odd.astype(jnp.float32)
    half_key = bin_of.astype(jnp.float32) * 2.0 + (bucket - 2.0 * upper) + 256.0 * kind
    row_key = half_key * 8.0 + upper
    row_key_out[...] = jnp.where(rank_in < own_size, row_key, -7.0)

    lane = lax.broadcasted_iota(jnp.int32, (1, 128), 1)
    slot_key = jnp.full((CHIPS, 128), -1.0, jnp.float32)
    for a in range(4):
        inside = (lane >= PART * a) & (lane < PART * (a + 1))
        slot_key = jnp.where(
            inside, table[a] * 8.0 + (lane - PART * a).astype(jnp.float32), slot_key
        )
    slot_key_out[...] = slot_key

    high = jnp.floor((rank_in + 0.5) * (1.0 / 128))
    low = rank_in - 128.0 * high
    high = high + 1.0 + (odd * (ODD // 128)).astype(jnp.float32)
    upper_half = lax.broadcasted_iota(jnp.int32, (128, LOCAL), 0) >= 64
    tags = jnp.where(upper_half, low, high).astype(jnp.bfloat16)

    some = 16
    slot = lax.broadcasted_iota(jnp.int32, (some, ROWS, 128), 1)
    tag_lane = lax.broadcasted_iota(jnp.int32, (some, ROWS, 128), 2)
    diagonal = (tag_lane % 64) == slot
    rest = slot
    for a in range(1, 4):
        rest = rest - jnp.where(slot >= PART * a, PART, 0)
    rest = rest.astype(jnp.float32)
    for k in range(CHIPS // some):
        key = jnp.full((some, ROWS, 128), -64.0, jnp.float32)
        for a in range(3, -1, -1):
            part = table[a][k * some : (k + 1) * some, :].reshape(some, 1, 128)
            part = jnp.broadcast_to(part, (some, ROWS, 128)) * 8.0
            key = jnp.where(slot < PART * (a + 1), part, key)
        key = (key + rest).reshape(some * ROWS, 128)
        chosen = []
        for c in range(LOCAL // 128):
            hit = key == row_key[:, c * 128 : (c + 1) * 128]
            chosen.append(jnp.where(hit, 1.0, 0.0).astype(jnp.bfloat16))
        chosen = jnp.concatenate(chosen, axis=1)
        rows = pl.ds(k * some * ROWS, some * ROWS)
        data = jnp.dot(chosen, unit[...], preferred_element_type=jnp.float32)
        tag = lax.dot_general(
            chosen, tags, (((1,), (1,)), ((), ())), preferred_element_type=jnp.float32
        ).reshape(some, ROWS, 128)
        tag = jnp.sum(jnp.where(diagonal, tag, 0.0), axis=1, keepdims=True)
        tag = jnp.where(slot == DATA, tag, 0.0).reshape(some * ROWS, 128)
        sent[rows, pl.ds(0, 128)] = (data[:, :128] + tag).astype(jnp.bfloat16)
        sent[rows, pl.ds(128, WIDTH - 128)] = data[:, 128:].astype(jnp.bfloat16)


def place_of(rows):
    source = lax.broadcasted_iota(jnp.int32, (CHIPS, SENT), 0)
    at = lax.broadcasted_iota(jnp.int32, (CHIPS, SENT), 1)
    is_tag = jnp.where(at == source * ROWS + DATA, 1.0, 0.0).astype(jnp.bfloat16)
    tag = jnp.dot(is_tag, rows[:, pl.ds(0, 128)], preferred_element_type=jnp.float32)
    slot = lax.broadcasted_iota(jnp.int32, (1, ROWS, 128), 1)
    lane = lax.broadcasted_iota(jnp.int32, (1, ROWS, 128), 2)
    weight = jnp.where(lane == slot, 128.0, 0.0) + jnp.where(lane == slot + 64, 1.0, 0.0)
    every = jnp.broadcast_to(tag.reshape(CHIPS, 1, 128), (CHIPS, ROWS, 128))
    key = jnp.sum(every * weight, axis=2, keepdims=True).reshape(SENT, 1)
    return jnp.where(key == 0.0, EMPTY, key)


def along_lanes(column):
    diagonal = lax.broadcasted_iota(jnp.int32, (128, 128), 0) == lax.broadcasted_iota(
        jnp.int32, (128, 128), 1
    )
    parts = []
    for c in range(SENT // 128):
        part = jnp.broadcast_to(column[c * 128 : (c + 1) * 128, :], (128, 128))
        parts.append(jnp.sum(jnp.where(diagonal, part, 0.0), axis=0, keepdims=True))
    return jnp.concatenate(parts, axis=1)


def down_sublanes(row):
    diagonal = lax.broadcasted_iota(jnp.int32, (128, 128), 0) == lax.broadcasted_iota(
        jnp.int32, (128, 128), 1
    )
    parts = []
    for c in range(SENT // 128):
        part = jnp.broadcast_to(row[:, c * 128 : (c + 1) * 128], (128, 128))
        parts.append(jnp.max(jnp.where(diagonal, part, -1.0), axis=1, keepdims=True))
    return jnp.concatenate(parts, axis=0)


def by_source(column):
    wide = jnp.broadcast_to(column, (SENT, 128)).reshape(CHIPS, ROWS, 128)
    slot = lax.broadcasted_iota(jnp.int32, (1, ROWS, 128), 1)
    lane = lax.broadcasted_iota(jnp.int32, (1, ROWS, 128), 2)
    return jnp.max(jnp.where(slot == lane, wide, -1.0), axis=1)


def kinds(key):
    even = jnp.max(jnp.where(key < ODD, 1.0, 0.0))
    odd = jnp.max(jnp.where((key >= ODD) & (key < EMPTY), 1.0, 0.0))
    return even > 0.5, odd > 0.5


def scores_of(rows, columns):
    return lax.dot_general(
        rows, columns, (((1,), (1,)), ((), ())), preferred_element_type=jnp.float32
    )


def is_odd(key):
    return jnp.where(key >= ODD, 1.0, 0.0)


def own_kernel(own, best, key_rows, key_lanes):
    key = place_of(own)
    key_rows[...] = jnp.broadcast_to(key, (SENT, 128))
    key_lanes[...] = along_lanes(key)
    even, odd = kinds(key)
    best[...] = jnp.full((SENT, 128), -1.0, jnp.float32)
    wide = 256

    def work(mixed):
        for j in range(SENT // wide):
            score = scores_of(own[...], own[pl.ds(j * wide, wide), :])
            row = key_rows[...]
            top = best[...]
            for c in range(wide // 128):
                col = key_lanes[:, pl.ds(j * wide + c * 128, 128)]
                earlier = col < row
                if mixed:
                    earlier = earlier & (is_odd(col) == is_odd(row))
                part = score[:, c * 128 : (c + 1) * 128]
                top = jnp.maximum(top, jnp.where(earlier, part, -1.0))
            best[...] = top

    pl.when(even & odd)(lambda: work(True))
    pl.when(~(even & odd))(lambda: work(False))


def cross_kernel(own, other, start, key_rows, out, key_lanes, best, best_lanes):
    core = lax.axis_index("core")
    key = place_of(other)
    key_lanes[...] = along_lanes(key)
    even, odd = kinds(key)
    own_even, own_odd = kinds(key_rows[...])
    mix = (even | own_even) & (odd | own_odd)
    tall, wide = SENT // 2, 256

    def work(mixed):
        for h in range(2):
            rows = pl.ds(h * tall, tall)
            for j in range(tall // wide):
                at = pl.multiple_of(jnp.where(core == h, 0, tall) + j * wide, wide)
                score = scores_of(own[rows, :], other[pl.ds(at, wide), :])
                row = key_rows[rows, :]
                top = start[rows, :] if j == 0 else best[rows, :]
                for c in range(wide // 128):
                    lanes = pl.ds(at + c * 128, 128)
                    col = key_lanes[:, lanes]
                    part = score[:, c * 128 : (c + 1) * 128]
                    earlier = col < row
                    if mixed:
                        same = is_odd(col) == is_odd(row)
                        later = (row < col) & same
                        above = jnp.where(earlier & same, part, -1.0)
                        below = jnp.where(later, part, -1.0)
                    else:
                        above = jnp.where(earlier, part, -1.0)
                        below = jnp.where(earlier, -1.0, part)
                    top = jnp.maximum(top, above)
                    below = jnp.max(below.reshape(tall // 8, 8, 128), axis=0)
                    best_lanes[:, lanes] = jnp.max(below, axis=0, keepdims=True)
                best[rows, :] = top

    pl.when(mix)(lambda: work(True))
    pl.when(~mix)(lambda: work(False))
    mine = pl.ds(pl.multiple_of(core * CHIPS, CHIPS), CHIPS)
    theirs = pl.ds(pl.multiple_of((1 - core) * CHIPS, CHIPS), CHIPS)
    out[mine, :] = by_source(jnp.max(best[...], axis=1, keepdims=True))
    out[theirs, :] = by_source(down_sublanes(best_lanes[...]))


def merge_kernel(answers, slot_key, row_key, extra, out):
    keys = row_key[...]
    answer = jnp.maximum(answers[pl.ds(0, CHIPS), :], answers[pl.ds(CHIPS, CHIPS), :])
    best = jnp.full((CHIPS, LOCAL), -1.0, jnp.float32)
    for t in range(DATA):
        hit = slot_key[:, pl.ds(t, 1)] == keys
        best = jnp.maximum(best, jnp.where(hit, answer[:, t : t + 1], -1.0))
    out[...] = jnp.maximum(jnp.max(best, axis=0, keepdims=True), extra[...])


VMEM = pl.BlockSpec(memory_space=pltpu.VMEM)
SMEM = pl.BlockSpec(memory_space=pltpu.SMEM)
LIMIT = 48 * 1024 * 1024


def pack(sizes, first_unit, emb, cluster, rank):
    later = first_unit is not None

    def kernel(*refs):
        if later:
            pack_kernel(refs[0][0], *refs[1:])
        else:
            pack_kernel(0, *refs)

    return pl.pallas_call(
        kernel,
        out_shape=(
            jax.ShapeDtypeStruct((SENT, WIDTH), jnp.bfloat16),
            jax.ShapeDtypeStruct((1, LOCAL), jnp.float32),
            jax.ShapeDtypeStruct((CHIPS, 128), jnp.float32),
            jax.ShapeDtypeStruct((1, 128), jnp.int32),
        ),
        in_specs=[SMEM] * later + [VMEM, VMEM, VMEM, VMEM],
        out_specs=(VMEM, VMEM, VMEM, VMEM),
        scratch_shapes=[pltpu.VMEM((LOCAL, WIDTH), jnp.bfloat16)],
        compiler_params=pltpu.CompilerParams(vmem_limit_bytes=LIMIT),
        cost_estimate=pl.CostEstimate(
            flops=2 * SENT * LOCAL * 640, bytes_accessed=2**21, transcendentals=0
        ),
        name="pack_later" if later else "pack",
    )(*((first_unit,) if later else ()), sizes, emb, cluster, rank)


def own_best(own):
    return pl.pallas_call(
        own_kernel,
        out_shape=(
            jax.ShapeDtypeStruct((SENT, 128), jnp.float32),
            jax.ShapeDtypeStruct((SENT, 128), jnp.float32),
        ),
        in_specs=[VMEM],
        out_specs=(VMEM, VMEM),
        scratch_shapes=[pltpu.VMEM((1, SENT), jnp.float32)],
        compiler_params=pltpu.CompilerParams(vmem_limit_bytes=LIMIT),
        cost_estimate=pl.CostEstimate(
            flops=2 * SENT * SENT * WIDTH, bytes_accessed=2**21, transcendentals=0
        ),
        name="own_best",
    )(own)


def cross_best(own, other, start, key_rows):
    return pl.pallas_call(
        cross_kernel,
        out_shape=jax.ShapeDtypeStruct((2 * CHIPS, 128), jnp.float32),
        in_specs=[VMEM] * 4,
        out_specs=VMEM,
        scratch_shapes=[
            pltpu.VMEM((1, SENT), jnp.float32),
            pltpu.VMEM((SENT, 128), jnp.float32),
            pltpu.VMEM((1, SENT), jnp.float32),
        ],
        compiler_params=pltpu.CompilerParams(vmem_limit_bytes=LIMIT),
        cost_estimate=pl.CostEstimate(
            flops=SENT * SENT * WIDTH, bytes_accessed=2**21, transcendentals=0
        ),
        name="cross_best",
    )(own, other, start, key_rows)


def merge(answers, slot_key, row_key, extra):
    return pl.pallas_call(
        merge_kernel,
        out_shape=jax.ShapeDtypeStruct((1, LOCAL), jnp.float32),
        in_specs=[VMEM] * 4,
        out_specs=VMEM,
        compiler_params=pltpu.CompilerParams(vmem_limit_bytes=16 * 1024 * 1024),
        name="merge",
    )(answers, slot_key, row_key, extra)


def exchange(values, axes):
    return lax.all_to_all(values, axes, split_axis=0, concat_axis=0, tiled=True)


def answers_of(sent):
    own = exchange(sent.reshape(CHIPS, ROWS, WIDTH), ("x", "y", "z")).reshape(SENT, WIDTH)
    other = lax.ppermute(own, "core", [(0, 1), (1, 0)])
    return exchange(cross_best(own, other, *own_best(own)), ("core", "x", "y", "z"))


def body(embeddings, cluster_sizes, cluster_of, rank_in):
    sizes = cluster_sizes.reshape(1, 2 * GROUPS)
    cluster = cluster_of.reshape(1, LOCAL)
    rank = rank_in.reshape(1, LOCAL)
    sent, row_key, slot_key, total = pack(sizes, None, embeddings, cluster, rank)
    answers = answers_of(sent)

    def more(carry):
        return carry[0] < total[0, 0]

    def again(carry):
        unit, best = carry
        sent, row_key, slot_key, _ = pack(sizes, unit.reshape(1), embeddings, cluster, rank)
        return unit + CHIPS, merge(answers_of(sent), slot_key, row_key, best)

    none = jnp.full((1, LOCAL), -1.0, jnp.float32)
    _, extra = lax.while_loop(more, again, (jnp.int32(CHIPS), none))
    return merge(answers, slot_key, row_key, extra).reshape(LOCAL)


def solution(mesh):
    chips = Mesh(mesh.devices.reshape(4, 4, 4, 2), ("x", "y", "z", "core"))
    every = ("x", "y", "z", "core")
    in_specs = (P(every, None), P(), P(every), P(every))
    return jax.shard_map(
        body, mesh=chips, in_specs=in_specs, out_specs=P(every), check_vma=False
    )
```

```python
import itertools

import jax
import jax.numpy as jnp
from jax import lax
from jax.experimental import pallas as pl
from jax.experimental.pallas import tpu as pltpu
from jax.sharding import Mesh
from jax.sharding import PartitionSpec as P

SLOTS = 1280
GROUPS = 16
BLOCKS = 8
WIDTH = 512
LOCAL = 512
CHIPS = 64
DATA = 20
EARLY = 16
PART = 5
HELD = CHIPS * DATA
LATE_AT = 4 * EARLY
TAGS_AT = LATE_AT + 16
LINES = TAGS_AT + 8
ODD = 16384
EMPTY = 1048576.0

COVERS = {
    1: ((0, 1, 0, 1),),
    2: ((0, 1, 2, 3),),
    3: ((0, 1, 4, 5), (1, 2, 3, 5), (0, 2, 3, 4)),
    4: ((1, 3, 6, 7), (1, 4, 5, 7), (0, 3, 4, 6), (0, 2, 3, 5), (0, 1, 2, 7), (2, 4, 5, 6)),
    5: (
        (3, 4, 6, 8), (3, 5, 8, 9), (2, 5, 6, 9), (1, 2, 3, 8), (0, 1, 6, 7),
        (1, 4, 5, 9), (0, 2, 4, 7), (0, 7, 8, 9), (0, 3, 5, 7),
    ),
    6: (
        (4, 5, 8, 10), (3, 6, 8, 11), (0, 4, 7, 11), (0, 1, 6, 10), (1, 7, 8, 9),
        (3, 5, 7, 10), (1, 3, 4, 9), (0, 5, 6, 9), (2, 9, 10, 11), (0, 2, 3, 8),
        (1, 2, 5, 11), (2, 4, 6, 7),
    ),
    7: (
        (0, 1, 5, 13), (3, 5, 8, 10), (0, 7, 10, 11), (2, 11, 12, 13), (2, 7, 8, 11),
        (1, 4, 10, 12), (8, 9, 12, 13), (1, 3, 4, 7), (4, 7, 9, 13), (3, 6, 10, 13),
        (0, 1, 2, 8), (0, 4, 6, 8), (2, 4, 5, 11), (0, 3, 9, 12), (5, 6, 7, 12),
        (2, 5, 9, 10), (1, 6, 9, 11), (2, 3, 6, 11),
    ),
}


def affine_plane():
    times = ((0, 0, 0, 0), (0, 1, 2, 3), (0, 2, 3, 1), (0, 3, 1, 2))
    lines = [tuple(4 * x + y for y in range(4)) for x in range(4)]
    for slope in range(4):
        for shift in range(4):
            lines.append(tuple(4 * x + (times[slope][x] ^ shift) for x in range(4)))
    return tuple(lines)


COVERS[8] = affine_plane()
for _m, _units in COVERS.items():
    _met = {frozenset(p) for unit in _units for p in itertools.combinations(unit, 2)}
    assert all(frozenset(p) in _met for p in itertools.combinations(range(2 * _m), 2))


def covers_by_lane():
    lane = lax.broadcasted_iota(jnp.int32, (8, 128), 1)
    packed = jnp.zeros((8, 128), jnp.int32)
    at = 0
    for m in range(1, BLOCKS + 1):
        for unit in COVERS[m]:
            value = sum(point << (4 * k) for k, point in enumerate(unit))
            packed = packed + jnp.where(lane == at, value, 0)
            at += 1
    assert at <= 128
    return packed


def by_blocks(m, values):
    picked = jnp.zeros_like(m)
    for k in range(1, BLOCKS + 1):
        picked = jnp.where(m == k, float(values[k]), picked)
    return picked


def full_blocks(places):
    return jnp.floor((places + 0.5) * (1.0 / SLOTS))


def plan(row, first_unit):
    clusters = 2 * GROUPS
    down = lax.broadcasted_iota(jnp.int32, (clusters, clusters), 0)
    across = lax.broadcasted_iota(jnp.int32, (clusters, clusters), 1)
    row = jnp.broadcast_to(row, (clusters, clusters))

    def column(mask):
        picked = jnp.sum(jnp.where(mask, row, 0.0), axis=1, keepdims=True)
        return jnp.broadcast_to(picked, (clusters, 128))

    size = column(down == across)
    partner = column(down == across + 1 - 2 * (across % 2))
    index = lax.broadcasted_iota(jnp.int32, (clusters, 128), 0)
    odd = index % 2 == 1
    first = jnp.where(odd, partner, size)
    blocks_a = full_blocks(first + (SLOTS - 1))
    start_b = full_blocks(first)
    blocks_b = full_blocks(size + partner + (SLOTS - 1)) - start_b
    blocks = jnp.where(odd, blocks_b, blocks_a)
    begin = jnp.where(odd, start_b, 0.0)
    counts = [0] + [len(COVERS[m]) for m in range(1, BLOCKS + 1)]
    alone = by_blocks(blocks, counts)
    held = (blocks == 1.0) & (blocks_a > start_b) & (odd | (blocks_b >= 2.0))
    shared = jnp.where(jnp.sum(alone, axis=0, keepdims=True) <= CHIPS, 0.0, 1.0)
    count = alone * (1.0 - shared * jnp.where(held, 1.0, 0.0))
    total = jnp.sum(count, axis=0, keepdims=True)
    start = jnp.dot(
        jnp.where(across < down, 1.0, 0.0).astype(jnp.bfloat16),
        count.astype(jnp.bfloat16),
        preferred_element_type=jnp.float32,
    )
    unit = (lax.broadcasted_iota(jnp.int32, (1, 128), 1) + first_unit).astype(jnp.float32)
    mine = (unit >= start) & (unit < start + count)

    def of_unit(values):
        return jnp.sum(jnp.where(mine, values, 0.0), axis=0, keepdims=True)

    bases = [0] + [sum(counts[:m]) for m in range(1, BLOCKS + 1)]
    entry = of_unit(by_blocks(blocks, bases) - start) + unit
    group = (index // 2).astype(jnp.float32)
    kind = 2.0 * shared + (1.0 - shared) * jnp.where(odd, 1.0, 0.0)
    half = of_unit(group * (2 * BLOCKS) + 2.0 * begin + 256.0 * kind)
    used = of_unit(jnp.where(blocks == 1.0, 1.0, 2.0))
    entry = jnp.broadcast_to(jnp.clip(entry, 0.0, 127.0).astype(jnp.int32), (8, 128))
    points = jnp.take_along_axis(covers_by_lane(), entry, axis=1)[0:1, :]
    diagonal = lax.broadcasted_iota(jnp.int32, (CHIPS, 128), 0) == lax.broadcasted_iota(
        jnp.int32, (CHIPS, 128), 1
    )
    table = []
    for a in range(4):
        point = ((points >> (4 * a)) & 15).astype(jnp.float32)
        held_by = jnp.where(used > (a // 2) + 0.5, half + point, 1024.0)
        held_by = jnp.sum(jnp.where(diagonal, held_by, 0.0), axis=1, keepdims=True)
        table.append(jnp.broadcast_to(held_by, (CHIPS, 128)))
    return table, size, jnp.where(odd, partner, 0.0), shared, total


def pack_kernel(
    first_unit, sizes, emb, cluster, rank, sent, row_key_out, slot_key_out, total_out, unit
):
    values = emb[...].astype(jnp.float32)
    scale = 1.0 / jnp.sqrt(jnp.sum(values * values, axis=1, keepdims=True) + 1e-06)
    unit[...] = (values * scale).astype(jnp.bfloat16)

    table, size, previous, shared, total = plan(sizes[...].astype(jnp.float32), first_unit)
    total_out[...] = total.astype(jnp.int32)

    def wide(column):
        return jnp.concatenate([column] * (LOCAL // 128), axis=1)

    cluster_of = cluster[...]
    rank_in = rank[...].astype(jnp.float32)
    own = lax.broadcasted_iota(jnp.int32, (2 * GROUPS, LOCAL), 0) == cluster_of
    own_size = jnp.sum(jnp.where(own, wide(size), 0.0), axis=0, keepdims=True)
    place = rank_in + jnp.sum(jnp.where(own, wide(previous), 0.0), axis=0, keepdims=True)
    bin_of = (cluster_of // 2) * BLOCKS + full_blocks(place).astype(jnp.int32)
    bins = lax.broadcasted_iota(jnp.int32, (GROUPS * BLOCKS, LOCAL), 0)
    member = jnp.where(bins == bin_of, 1.0, 0.0)
    until = lax.broadcasted_iota(jnp.int32, (128, 256), 0) <= lax.broadcasted_iota(
        jnp.int32, (128, 256), 1
    )
    until = jnp.where(until, 1.0, 0.0).astype(jnp.bfloat16)
    passed = jnp.full((GROUPS * BLOCKS, 128), -1.0, jnp.float32)
    bucket = []
    for c in range(LOCAL // 128):
        part = member[:, c * 128 : (c + 1) * 128]
        seen = jnp.dot(part.astype(jnp.bfloat16), until, preferred_element_type=jnp.float32)
        before = passed + seen[:, :128]
        passed = passed + seen[:, 128:]
        bucket.append(jnp.sum(part * before, axis=0, keepdims=True))
    bucket = jnp.concatenate(bucket, axis=1)
    upper = jnp.floor((bucket + 0.5) * 0.5)
    odd = cluster_of % 2
    kind = wide(shared)
    kind = 2.0 * kind + (1.0 - kind) * odd.astype(jnp.float32)
    half_key = bin_of.astype(jnp.float32) * 2.0 + (bucket - 2.0 * upper) + 256.0 * kind
    row_key = half_key * 8.0 + upper
    row_key_out[...] = jnp.where(rank_in < own_size, row_key, -7.0)

    lane = lax.broadcasted_iota(jnp.int32, (1, 128), 1)
    slot_key = jnp.full((CHIPS, 128), -1.0, jnp.float32)
    for a in range(4):
        inside = (lane >= PART * a) & (lane < PART * (a + 1))
        slot_key = jnp.where(
            inside, table[a] * 8.0 + (lane - PART * a).astype(jnp.float32), slot_key
        )
    slot_key_out[...] = slot_key

    high = jnp.floor((rank_in + 0.5) * (1.0 / 128))
    low = rank_in - 128.0 * high
    high = high + 1.0 + (odd * (ODD // 128)).astype(jnp.float32)
    upper_half = lax.broadcasted_iota(jnp.int32, (128, LOCAL), 0) >= 64
    tags = jnp.where(upper_half, low, high).astype(jnp.bfloat16)

    some, picks = 16, EARLY + 8
    row = lax.broadcasted_iota(jnp.int32, (some, picks, 128), 1)
    slot = jnp.where(row >= DATA, row - 4, row)
    tag_lane = lax.broadcasted_iota(jnp.int32, (some, picks, 128), 2)
    diagonal = ((tag_lane % 64) == slot) & (row < DATA)
    rest = slot
    for a in range(1, 4):
        rest = rest - jnp.where(slot >= PART * a, PART, 0)
    rest = rest.astype(jnp.float32)
    low_rows = lax.broadcasted_iota(jnp.int32, (some, 8, 128), 1) < 4
    for k in range(CHIPS // some):
        key = jnp.zeros((some, picks, 128), jnp.float32)
        for a in range(3, -1, -1):
            part = table[a][k * some : (k + 1) * some, :].reshape(some, 1, 128)
            part = jnp.broadcast_to(part, (some, picks, 128)) * 8.0
            key = part if a == 3 else jnp.where(slot < PART * (a + 1), part, key)
        key = (key + rest).reshape(some * picks, 128)
        chosen = []
        for c in range(LOCAL // 128):
            hit = key == row_key[:, c * 128 : (c + 1) * 128]
            chosen.append(jnp.where(hit, 1.0, 0.0).astype(jnp.bfloat16))
        chosen = jnp.concatenate(chosen, axis=1)
        chips = pl.ds(k * some, some)
        data = jnp.dot(chosen, unit[...], preferred_element_type=jnp.float32)
        tag = lax.dot_general(
            chosen, tags, (((1,), (1,)), ((), ())), preferred_element_type=jnp.float32
        ).reshape(some, picks, 128)
        tag = jnp.sum(jnp.where(diagonal, tag, 0.0), axis=1, keepdims=True)
        quarters = [
            data[:, q * 128 : (q + 1) * 128].reshape(some, picks, 128) for q in range(4)
        ]
        for q in range(4):
            sent[chips, pl.ds(q * EARLY, EARLY), :] = quarters[q][:, :EARLY].astype(jnp.bfloat16)
        late = [quarter[:, EARLY:] for quarter in quarters]
        late = [jnp.where(low_rows, late[q], late[q + 1]) for q in (0, 2)]
        sent[chips, pl.ds(LATE_AT, 16), :] = jnp.concatenate(late, axis=1).astype(jnp.bfloat16)
        sent[chips, pl.ds(TAGS_AT, 8), :] = jnp.broadcast_to(tag, (some, 8, 128)).astype(
            jnp.bfloat16
        )


def unfold(lines, rows):
    for q in range(4):
        part = lines[:, pl.ds(q * EARLY, EARLY), :]
        rows[pl.ds(0, CHIPS * EARLY), pl.ds(q * 128, 128)] = part.reshape(CHIPS * EARLY, 128)
    late = lines[:, pl.ds(LATE_AT, 16), :].astype(jnp.float32).reshape(CHIPS // 2, 2, 16, 128)
    low_rows = lax.broadcasted_iota(jnp.int32, (CHIPS // 2, 8, 128), 1) < 4
    for q in (0, 2):
        even, odd = late[:, 0, q * 4 : q * 4 + 8], late[:, 1, q * 4 : q * 4 + 8]
        quarters = (
            jnp.where(low_rows, even, pltpu.roll(odd, 4, 1)),
            jnp.where(low_rows, pltpu.roll(even, 4, 1), odd),
        )
        for k in range(2):
            part = quarters[k].reshape(CHIPS * 4, 128).astype(jnp.bfloat16)
            rows[pl.ds(CHIPS * EARLY, CHIPS * 4), pl.ds((q + k) * 128, 128)] = part


def place_of(lines):
    tag = lines[:, pl.ds(TAGS_AT, 8), :].astype(jnp.float32)[:, 0:1, :]

    def read(tags, slot):
        lane = lax.broadcasted_iota(jnp.int32, slot.shape, 2)
        weight = jnp.where(lane == slot, 128.0, 0.0) + jnp.where(lane == slot + 64, 1.0, 0.0)
        return jnp.sum(tags * weight, axis=2, keepdims=True)

    early = lax.broadcasted_iota(jnp.int32, (1, EARLY, 128), 1)
    first = read(jnp.broadcast_to(tag, (CHIPS, EARLY, 128)), early)
    row = lax.broadcasted_iota(jnp.int32, (1, 8, 128), 1)
    pair = tag.reshape(CHIPS // 2, 2, 1, 128)
    shape = (CHIPS // 2, 8, 128)
    pair = jnp.where(
        row < 4, jnp.broadcast_to(pair[:, 0], shape), jnp.broadcast_to(pair[:, 1], shape)
    )
    last = read(pair, EARLY + row % 4)
    key = jnp.concatenate(
        [first.reshape(CHIPS * EARLY, 1), last.reshape(CHIPS * 4, 1)], axis=0
    )
    return jnp.where(key == 0.0, EMPTY, key)


def along_lanes(column):
    diagonal = lax.broadcasted_iota(jnp.int32, (128, 128), 0) == lax.broadcasted_iota(
        jnp.int32, (128, 128), 1
    )
    parts = []
    for c in range(HELD // 128):
        part = jnp.broadcast_to(column[c * 128 : (c + 1) * 128, :], (128, 128))
        parts.append(jnp.sum(jnp.where(diagonal, part, 0.0), axis=0, keepdims=True))
    return jnp.concatenate(parts, axis=1)


def down_sublanes(row):
    diagonal = lax.broadcasted_iota(jnp.int32, (128, 128), 0) == lax.broadcasted_iota(
        jnp.int32, (128, 128), 1
    )
    parts = []
    for c in range(HELD // 128):
        part = jnp.broadcast_to(row[:, c * 128 : (c + 1) * 128], (128, 128))
        parts.append(jnp.max(jnp.where(diagonal, part, -1.0), axis=1, keepdims=True))
    return jnp.concatenate(parts, axis=0)


def by_source(column):
    wide = jnp.broadcast_to(column, (HELD, 128))
    first = wide[: CHIPS * EARLY].reshape(CHIPS, EARLY, 128)
    last = wide[CHIPS * EARLY :].reshape(CHIPS // 2, 8, 128)
    slot = lax.broadcasted_iota(jnp.int32, (1, EARLY, 128), 1)
    lane = lax.broadcasted_iota(jnp.int32, (1, EARLY, 128), 2)
    first = jnp.max(jnp.where(slot == lane, first, -1.0), axis=1, keepdims=True)
    row = lax.broadcasted_iota(jnp.int32, (1, 8, 128), 1)
    lane = lax.broadcasted_iota(jnp.int32, (1, 8, 128), 2)
    last = jnp.where(lane == EARLY + row % 4, last, -1.0)
    even = jnp.max(jnp.where(row < 4, last, -1.0), axis=1, keepdims=True)
    odd = jnp.max(jnp.where(row >= 4, last, -1.0), axis=1, keepdims=True)
    pair = first.reshape(CHIPS // 2, 2, 1, 128)
    both = jnp.stack([jnp.maximum(pair[:, 0], even), jnp.maximum(pair[:, 1], odd)], axis=1)
    return both.reshape(CHIPS, 128)


def kinds(key):
    even = jnp.max(jnp.where(key < ODD, 1.0, 0.0))
    odd = jnp.max(jnp.where((key >= ODD) & (key < EMPTY), 1.0, 0.0))
    return even > 0.5, odd > 0.5


def scores_of(rows, columns):
    return lax.dot_general(
        rows, columns, (((1,), (1,)), ((), ())), preferred_element_type=jnp.float32
    )


def is_odd(key):
    return jnp.where(key >= ODD, 1.0, 0.0)


def own_kernel(lines, best, key_rows, own, key_lanes):
    unfold(lines, own)
    key = place_of(lines)
    key_rows[...] = jnp.broadcast_to(key, (HELD, 128))
    key_lanes[...] = along_lanes(key)
    even, odd = kinds(key)
    best[...] = jnp.full((HELD, 128), -1.0, jnp.float32)
    wide = 256

    def work(mixed):
        for j in range(HELD // wide):
            score = scores_of(own[...], own[pl.ds(j * wide, wide), :])
            row = key_rows[...]
            top = best[...]
            for c in range(wide // 128):
                col = key_lanes[:, pl.ds(j * wide + c * 128, 128)]
                earlier = col < row
                if mixed:
                    earlier = earlier & (is_odd(col) == is_odd(row))
                part = score[:, c * 128 : (c + 1) * 128]
                top = jnp.maximum(top, jnp.where(earlier, part, -1.0))
            best[...] = top

    pl.when(even & odd)(lambda: work(True))
    pl.when(~(even & odd))(lambda: work(False))


def cross_kernel(own, lines, start, key_rows, out, other, key_lanes, best, best_lanes):
    core = lax.axis_index("core")
    unfold(lines, other)
    key = place_of(lines)
    key_lanes[...] = along_lanes(key)
    even, odd = kinds(key)
    own_even, own_odd = kinds(key_rows[...])
    mix = (even | own_even) & (odd | own_odd)
    wide = 256
    parts = ((0, 3 * wide), (3 * wide, HELD - 3 * wide))

    def work(mixed, swap):
        for h in range(2):
            row_at, tall = parts[h]
            col_at, length = parts[1 - h if swap else h]
            rows = pl.ds(row_at, tall)
            for j in range(length // wide):
                at = col_at + j * wide
                score = scores_of(own[rows, :], other[pl.ds(at, wide), :])
                row = key_rows[rows, :]
                top = start[rows, :] if j == 0 else best[rows, :]
                for c in range(wide // 128):
                    lanes = pl.ds(at + c * 128, 128)
                    col = key_lanes[:, lanes]
                    part = score[:, c * 128 : (c + 1) * 128]
                    earlier = col < row
                    if mixed:
                        same = is_odd(col) == is_odd(row)
                        later = (row < col) & same
                        above = jnp.where(earlier & same, part, -1.0)
                        below = jnp.where(later, part, -1.0)
                    else:
                        above = jnp.where(earlier, part, -1.0)
                        below = jnp.where(earlier, -1.0, part)
                    top = jnp.maximum(top, above)
                    below = jnp.max(below.reshape(tall // 8, 8, 128), axis=0)
                    best_lanes[:, lanes] = jnp.max(below, axis=0, keepdims=True)
                best[rows, :] = top

    for swap in (False, True):
        here = core == (1 if swap else 0)
        pl.when(here & mix)(lambda swap=swap: work(True, swap))
        pl.when(here & ~mix)(lambda swap=swap: work(False, swap))
    mine = pl.ds(pl.multiple_of(core * CHIPS, CHIPS), CHIPS)
    theirs = pl.ds(pl.multiple_of((1 - core) * CHIPS, CHIPS), CHIPS)
    out[mine, :] = by_source(jnp.max(best[...], axis=1, keepdims=True))
    out[theirs, :] = by_source(down_sublanes(best_lanes[...]))


def merge_kernel(answers, slot_key, row_key, extra, out):
    keys = row_key[...]
    answer = jnp.maximum(answers[pl.ds(0, CHIPS), :], answers[pl.ds(CHIPS, CHIPS), :])
    best = jnp.full((CHIPS, LOCAL), -1.0, jnp.float32)
    for t in range(DATA):
        hit = slot_key[:, pl.ds(t, 1)] == keys
        best = jnp.maximum(best, jnp.where(hit, answer[:, t : t + 1], -1.0))
    out[...] = jnp.maximum(jnp.max(best, axis=0, keepdims=True), extra[...])


VMEM = pl.BlockSpec(memory_space=pltpu.VMEM)
SMEM = pl.BlockSpec(memory_space=pltpu.SMEM)
LIMIT = 48 * 1024 * 1024


def pack(sizes, first_unit, emb, cluster, rank):
    later = first_unit is not None

    def kernel(*refs):
        if later:
            pack_kernel(refs[0][0], *refs[1:])
        else:
            pack_kernel(0, *refs)

    return pl.pallas_call(
        kernel,
        out_shape=(
            jax.ShapeDtypeStruct((CHIPS, LINES, 128), jnp.bfloat16),
            jax.ShapeDtypeStruct((1, LOCAL), jnp.float32),
            jax.ShapeDtypeStruct((CHIPS, 128), jnp.float32),
            jax.ShapeDtypeStruct((1, 128), jnp.int32),
        ),
        in_specs=[SMEM] * later + [VMEM, VMEM, VMEM, VMEM],
        out_specs=(VMEM, VMEM, VMEM, VMEM),
        scratch_shapes=[pltpu.VMEM((LOCAL, WIDTH), jnp.bfloat16)],
        compiler_params=pltpu.CompilerParams(vmem_limit_bytes=LIMIT),
        cost_estimate=pl.CostEstimate(
            flops=2 * CHIPS * 24 * LOCAL * 640, bytes_accessed=2**21, transcendentals=0
        ),
        name="pack_later" if later else "pack",
    )(*((first_unit,) if later else ()), sizes, emb, cluster, rank)


def own_best(lines):
    return pl.pallas_call(
        own_kernel,
        out_shape=(
            jax.ShapeDtypeStruct((HELD, 128), jnp.float32),
            jax.ShapeDtypeStruct((HELD, 128), jnp.float32),
            jax.ShapeDtypeStruct((HELD, WIDTH), jnp.bfloat16),
        ),
        in_specs=[VMEM],
        out_specs=(VMEM,) * 3,
        scratch_shapes=[pltpu.VMEM((1, HELD), jnp.float32)],
        compiler_params=pltpu.CompilerParams(vmem_limit_bytes=LIMIT),
        cost_estimate=pl.CostEstimate(
            flops=2 * HELD * HELD * WIDTH, bytes_accessed=2**21, transcendentals=0
        ),
        name="own_best",
    )(lines)


def cross_best(own, lines, start, key_rows):
    return pl.pallas_call(
        cross_kernel,
        out_shape=jax.ShapeDtypeStruct((2 * CHIPS, 128), jnp.float32),
        in_specs=[VMEM] * 4,
        out_specs=VMEM,
        scratch_shapes=[
            pltpu.VMEM((HELD, WIDTH), jnp.bfloat16),
            pltpu.VMEM((1, HELD), jnp.float32),
            pltpu.VMEM((HELD, 128), jnp.float32),
            pltpu.VMEM((1, HELD), jnp.float32),
        ],
        compiler_params=pltpu.CompilerParams(vmem_limit_bytes=LIMIT),
        cost_estimate=pl.CostEstimate(
            flops=HELD * HELD * WIDTH, bytes_accessed=2**21, transcendentals=0
        ),
        name="cross_best",
    )(own, lines, start, key_rows)


def merge(answers, slot_key, row_key, extra):
    return pl.pallas_call(
        merge_kernel,
        out_shape=jax.ShapeDtypeStruct((1, LOCAL), jnp.float32),
        in_specs=[VMEM] * 4,
        out_specs=VMEM,
        compiler_params=pltpu.CompilerParams(vmem_limit_bytes=16 * 1024 * 1024),
        name="merge",
    )(answers, slot_key, row_key, extra)


def exchange(values, axes):
    return lax.all_to_all(values, axes, split_axis=0, concat_axis=0, tiled=True)


def answers_of(sent):
    lines = exchange(sent, ("x", "y", "z"))
    other = lax.ppermute(lines, "core", [(0, 1), (1, 0)])
    start, key_rows, own = own_best(lines)
    return exchange(cross_best(own, other, start, key_rows), ("core", "x", "y", "z"))


def body(embeddings, cluster_sizes, cluster_of, rank_in):
    sizes = cluster_sizes.reshape(1, 2 * GROUPS)
    cluster = cluster_of.reshape(1, LOCAL)
    rank = rank_in.reshape(1, LOCAL)
    sent, row_key, slot_key, total = pack(sizes, None, embeddings, cluster, rank)
    answers = answers_of(sent)

    def more(carry):
        return carry[0] < total[0, 0]

    def again(carry):
        unit, best = carry
        sent, row_key, slot_key, _ = pack(sizes, unit.reshape(1), embeddings, cluster, rank)
        return unit + CHIPS, merge(answers_of(sent), slot_key, row_key, best)

    none = jnp.full((1, LOCAL), -1.0, jnp.float32)
    _, extra = lax.while_loop(more, again, (jnp.int32(CHIPS), none))
    return merge(answers, slot_key, row_key, extra).reshape(LOCAL)


def solution(mesh):
    chips = Mesh(mesh.devices.reshape(4, 4, 4, 2), ("x", "y", "z", "core"))
    every = ("x", "y", "z", "core")
    in_specs = (P(every, None), P(), P(every), P(every))
    return jax.shard_map(
        body, mesh=chips, in_specs=in_specs, out_specs=P(every), check_vma=False
    )
```

```python
import itertools

import jax
import jax.numpy as jnp
from jax import lax
from jax.experimental import pallas as pl
from jax.experimental.pallas import tpu as pltpu
from jax.sharding import Mesh
from jax.sharding import PartitionSpec as P

SLOTS = 1280
GROUPS = 16
BLOCKS = 8
WIDTH = 512
LOCAL = 512
CHIPS = 64
DATA = 20
EARLY = 16
PART = 5
HELD = CHIPS * DATA
TILE = 256
TILES = HELD // TILE
LATE_AT = 4 * EARLY
TAGS_AT = LATE_AT + 16
LINES = TAGS_AT + 8
ODD = 16384
EMPTY = 1048576.0

COVERS = {
    1: ((0, 1, 0, 1),),
    2: ((0, 1, 2, 3),),
    3: ((0, 1, 4, 5), (1, 2, 3, 5), (0, 2, 3, 4)),
    4: ((1, 3, 6, 7), (1, 4, 5, 7), (0, 3, 4, 6), (0, 2, 3, 5), (0, 1, 2, 7), (2, 4, 5, 6)),
    5: (
        (3, 4, 6, 8), (3, 5, 8, 9), (2, 5, 6, 9), (1, 2, 3, 8), (0, 1, 6, 7),
        (1, 4, 5, 9), (0, 2, 4, 7), (0, 7, 8, 9), (0, 3, 5, 7),
    ),
    6: (
        (4, 5, 8, 10), (3, 6, 8, 11), (0, 4, 7, 11), (0, 1, 6, 10), (1, 7, 8, 9),
        (3, 5, 7, 10), (1, 3, 4, 9), (0, 5, 6, 9), (2, 9, 10, 11), (0, 2, 3, 8),
        (1, 2, 5, 11), (2, 4, 6, 7),
    ),
    7: (
        (0, 1, 5, 13), (3, 5, 8, 10), (0, 7, 10, 11), (2, 11, 12, 13), (2, 7, 8, 11),
        (1, 4, 10, 12), (8, 9, 12, 13), (1, 3, 4, 7), (4, 7, 9, 13), (3, 6, 10, 13),
        (0, 1, 2, 8), (0, 4, 6, 8), (2, 4, 5, 11), (0, 3, 9, 12), (5, 6, 7, 12),
        (2, 5, 9, 10), (1, 6, 9, 11), (2, 3, 6, 11),
    ),
}


def affine_plane():
    times = ((0, 0, 0, 0), (0, 1, 2, 3), (0, 2, 3, 1), (0, 3, 1, 2))
    lines = [tuple(4 * x + y for y in range(4)) for x in range(4)]
    for slope in range(4):
        for shift in range(4):
            lines.append(tuple(4 * x + (times[slope][x] ^ shift) for x in range(4)))
    return tuple(lines)


COVERS[8] = affine_plane()
for _m, _units in COVERS.items():
    _met = {frozenset(p) for unit in _units for p in itertools.combinations(unit, 2)}
    assert all(frozenset(p) in _met for p in itertools.combinations(range(2 * _m), 2))


def covers_by_lane():
    lane = lax.broadcasted_iota(jnp.int32, (8, 128), 1)
    packed = jnp.zeros((8, 128), jnp.int32)
    at = 0
    for m in range(1, BLOCKS + 1):
        for unit in COVERS[m]:
            value = sum(point << (4 * k) for k, point in enumerate(unit))
            packed = packed + jnp.where(lane == at, value, 0)
            at += 1
    assert at <= 128
    return packed


def by_blocks(m, values):
    picked = jnp.zeros_like(m)
    for k in range(1, BLOCKS + 1):
        picked = jnp.where(m == k, float(values[k]), picked)
    return picked


def full_blocks(places):
    return jnp.floor((places + 0.5) * (1.0 / SLOTS))


def plan(row, first_unit):
    clusters = 2 * GROUPS
    down = lax.broadcasted_iota(jnp.int32, (clusters, clusters), 0)
    across = lax.broadcasted_iota(jnp.int32, (clusters, clusters), 1)
    row = jnp.broadcast_to(row, (clusters, clusters))

    def column(mask):
        picked = jnp.sum(jnp.where(mask, row, 0.0), axis=1, keepdims=True)
        return jnp.broadcast_to(picked, (clusters, 128))

    size = column(down == across)
    partner = column(down == across + 1 - 2 * (across % 2))
    index = lax.broadcasted_iota(jnp.int32, (clusters, 128), 0)
    odd = index % 2 == 1
    first = jnp.where(odd, partner, size)
    blocks_a = full_blocks(first + (SLOTS - 1))
    start_b = full_blocks(first)
    blocks_b = full_blocks(size + partner + (SLOTS - 1)) - start_b
    blocks = jnp.where(odd, blocks_b, blocks_a)
    begin = jnp.where(odd, start_b, 0.0)
    counts = [0] + [len(COVERS[m]) for m in range(1, BLOCKS + 1)]
    alone = by_blocks(blocks, counts)
    held = (blocks == 1.0) & (blocks_a > start_b) & (odd | (blocks_b >= 2.0))
    shared = jnp.where(jnp.sum(alone, axis=0, keepdims=True) <= CHIPS, 0.0, 1.0)
    count = alone * (1.0 - shared * jnp.where(held, 1.0, 0.0))
    total = jnp.sum(count, axis=0, keepdims=True)
    start = jnp.dot(
        jnp.where(across < down, 1.0, 0.0).astype(jnp.bfloat16),
        count.astype(jnp.bfloat16),
        preferred_element_type=jnp.float32,
    )
    unit = (lax.broadcasted_iota(jnp.int32, (1, 128), 1) + first_unit).astype(jnp.float32)
    mine = (unit >= start) & (unit < start + count)

    def of_unit(values):
        return jnp.sum(jnp.where(mine, values, 0.0), axis=0, keepdims=True)

    bases = [0] + [sum(counts[:m]) for m in range(1, BLOCKS + 1)]
    entry = of_unit(by_blocks(blocks, bases) - start) + unit
    group = (index // 2).astype(jnp.float32)
    kind = 2.0 * shared + (1.0 - shared) * jnp.where(odd, 1.0, 0.0)
    half = of_unit(group * (2 * BLOCKS) + 2.0 * begin + 256.0 * kind)
    used = of_unit(jnp.where(blocks == 1.0, 1.0, 2.0))
    entry = jnp.broadcast_to(jnp.clip(entry, 0.0, 127.0).astype(jnp.int32), (8, 128))
    points = jnp.take_along_axis(covers_by_lane(), entry, axis=1)[0:1, :]
    diagonal = lax.broadcasted_iota(jnp.int32, (CHIPS, 128), 0) == lax.broadcasted_iota(
        jnp.int32, (CHIPS, 128), 1
    )
    table = []
    for a in range(4):
        point = ((points >> (4 * a)) & 15).astype(jnp.float32)
        held_by = jnp.where(used > (a // 2) + 0.5, half + point, 1024.0)
        held_by = jnp.sum(jnp.where(diagonal, held_by, 0.0), axis=1, keepdims=True)
        table.append(jnp.broadcast_to(held_by, (CHIPS, 128)))
    return table, size, jnp.where(odd, partner, 0.0), shared, total


def pack_kernel(
    first_unit, sizes, emb, cluster, rank, sent, row_key_out, slot_key_out, total_out, none_out, unit
):
    values = emb[...].astype(jnp.float32)
    scale = 1.0 / jnp.sqrt(jnp.sum(values * values, axis=1, keepdims=True) + 1e-06)
    unit[...] = (values * scale).astype(jnp.bfloat16)

    table, size, previous, shared, total = plan(sizes[...].astype(jnp.float32), first_unit)
    total_out[...] = total.astype(jnp.int32)
    none_out[...] = jnp.full((1, LOCAL), -1.0, jnp.float32)

    def wide(column):
        return jnp.concatenate([column] * (LOCAL // 128), axis=1)

    cluster_of = cluster[...]
    rank_in = rank[...].astype(jnp.float32)
    own = lax.broadcasted_iota(jnp.int32, (2 * GROUPS, LOCAL), 0) == cluster_of
    own_size = jnp.sum(jnp.where(own, wide(size), 0.0), axis=0, keepdims=True)
    place = rank_in + jnp.sum(jnp.where(own, wide(previous), 0.0), axis=0, keepdims=True)
    bin_of = (cluster_of // 2) * BLOCKS + full_blocks(place).astype(jnp.int32)
    bins = lax.broadcasted_iota(jnp.int32, (GROUPS * BLOCKS, LOCAL), 0)
    member = jnp.where(bins == bin_of, 1.0, 0.0)
    until = lax.broadcasted_iota(jnp.int32, (128, 256), 0) <= lax.broadcasted_iota(
        jnp.int32, (128, 256), 1
    )
    until = jnp.where(until, 1.0, 0.0).astype(jnp.bfloat16)
    passed = jnp.full((GROUPS * BLOCKS, 128), -1.0, jnp.float32)
    bucket = []
    for c in range(LOCAL // 128):
        part = member[:, c * 128 : (c + 1) * 128]
        seen = jnp.dot(part.astype(jnp.bfloat16), until, preferred_element_type=jnp.float32)
        before = passed + seen[:, :128]
        passed = passed + seen[:, 128:]
        bucket.append(jnp.sum(part * before, axis=0, keepdims=True))
    bucket = jnp.concatenate(bucket, axis=1)
    upper = jnp.floor((bucket + 0.5) * 0.5)
    odd = cluster_of % 2
    kind = wide(shared)
    kind = 2.0 * kind + (1.0 - kind) * odd.astype(jnp.float32)
    half_key = bin_of.astype(jnp.float32) * 2.0 + (bucket - 2.0 * upper) + 256.0 * kind
    row_key = half_key * 8.0 + upper
    row_key_out[...] = jnp.where(rank_in < own_size, row_key, -7.0)

    for a in range(4):
        table[a] = table[a] * 8.0
        slot_key_out[pl.ds(a * CHIPS, CHIPS), :] = table[a]

    high = jnp.floor((rank_in + 0.5) * (1.0 / 128))
    low = rank_in - 128.0 * high
    high = high + 1.0 + (odd * (ODD // 128)).astype(jnp.float32)
    upper_half = lax.broadcasted_iota(jnp.int32, (128, LOCAL), 0) >= 64
    tags = jnp.where(upper_half, low, high).astype(jnp.bfloat16)

    some, picks = 16, EARLY + 8
    row = lax.broadcasted_iota(jnp.int32, (some, picks, 128), 1)
    slot = jnp.where(row >= DATA, row - 4, row)
    tag_lane = lax.broadcasted_iota(jnp.int32, (some, picks, 128), 2)
    diagonal = ((tag_lane % 64) == slot) & (row < DATA)
    rest = slot
    for a in range(1, 4):
        rest = rest - jnp.where(slot >= PART * a, PART, 0)
    rest = rest.astype(jnp.float32)
    low_rows = lax.broadcasted_iota(jnp.int32, (some, 8, 128), 1) < 4
    for k in range(CHIPS // some):
        key = jnp.zeros((some, picks, 128), jnp.float32)
        for a in range(3, -1, -1):
            part = table[a][k * some : (k + 1) * some, :].reshape(some, 1, 128)
            part = jnp.broadcast_to(part, (some, picks, 128))
            key = part if a == 3 else jnp.where(slot < PART * (a + 1), part, key)
        key = (key + rest).reshape(some * picks, 128)
        chosen = []
        for c in range(LOCAL // 128):
            hit = key == row_key[:, c * 128 : (c + 1) * 128]
            chosen.append(jnp.where(hit, 1.0, 0.0).astype(jnp.bfloat16))
        chosen = jnp.concatenate(chosen, axis=1)
        chips = pl.ds(k * some, some)
        data = jnp.dot(chosen, unit[...], preferred_element_type=jnp.float32)
        tag = lax.dot_general(
            chosen, tags, (((1,), (1,)), ((), ())), preferred_element_type=jnp.float32
        ).reshape(some, picks, 128)
        tag = jnp.sum(jnp.where(diagonal, tag, 0.0), axis=1, keepdims=True)
        quarters = [
            data[:, q * 128 : (q + 1) * 128].reshape(some, picks, 128) for q in range(4)
        ]
        for q in range(4):
            sent[chips, pl.ds(q * EARLY, EARLY), :] = quarters[q][:, :EARLY].astype(jnp.bfloat16)
        late = [quarter[:, EARLY:] for quarter in quarters]
        late = [jnp.where(low_rows, late[q], late[q + 1]) for q in (0, 2)]
        sent[chips, pl.ds(LATE_AT, 16), :] = jnp.concatenate(late, axis=1).astype(jnp.bfloat16)
        sent[chips, pl.ds(TAGS_AT, 8), :] = jnp.broadcast_to(tag, (some, 8, 128)).astype(
            jnp.bfloat16
        )


def unfold_late(lines, late):
    part = lines[:, pl.ds(LATE_AT, 16), :].astype(jnp.float32).reshape(CHIPS // 2, 2, 16, 128)
    low_rows = lax.broadcasted_iota(jnp.int32, (CHIPS // 2, 8, 128), 1) < 4
    for q in (0, 2):
        even, odd = part[:, 0, q * 4 : q * 4 + 8], part[:, 1, q * 4 : q * 4 + 8]
        quarters = (
            jnp.where(low_rows, even, pltpu.roll(odd, 4, 1)),
            jnp.where(low_rows, pltpu.roll(even, 4, 1), odd),
        )
        for k in range(2):
            late[:, pl.ds((q + k) * 128, 128)] = (
                quarters[k].reshape(CHIPS * 4, 128).astype(jnp.bfloat16)
            )


def tile(lines, late, n):
    if n == TILES - 1:
        return late[...]
    sources = pl.ds(n * (TILE // EARLY), TILE // EARLY)
    quarters = [lines[sources, pl.ds(q * EARLY, EARLY), :] for q in range(4)]
    return jnp.concatenate([part.reshape(TILE, 128) for part in quarters], axis=1)


def tiles(lines, late, some):
    return jnp.concatenate([tile(lines, late, n) for n in some], axis=0)


def place_of(lines):
    tag = lines[:, pl.ds(TAGS_AT, 8), :].astype(jnp.float32)[:, 0:1, :]

    def weighed(tags, slot):
        lane = lax.broadcasted_iota(jnp.int32, slot.shape, 2)
        weight = jnp.where(lane == slot, 128.0, 0.0) + jnp.where(lane == slot + 64, 1.0, 0.0)
        return (tags * weight).astype(jnp.bfloat16)

    early = lax.broadcasted_iota(jnp.int32, (1, EARLY, 128), 1)
    first = weighed(jnp.broadcast_to(tag, (CHIPS, EARLY, 128)), early)
    row = lax.broadcasted_iota(jnp.int32, (1, 8, 128), 1)
    pair = tag.reshape(CHIPS // 2, 2, 1, 128)
    shape = (CHIPS // 2, 8, 128)
    pair = jnp.where(
        row < 4, jnp.broadcast_to(pair[:, 0], shape), jnp.broadcast_to(pair[:, 1], shape)
    )
    last = weighed(pair, EARLY + row % 4)
    terms = jnp.concatenate(
        [first.reshape(CHIPS * EARLY, 128), last.reshape(CHIPS * 4, 128)], axis=0
    )
    key = jnp.dot(terms, jnp.ones((128, 128), jnp.bfloat16), preferred_element_type=jnp.float32)
    return jnp.where(key == 0.0, EMPTY, key)


def along_lanes(key):
    diagonal = lax.broadcasted_iota(jnp.int32, (128, 128), 0) == lax.broadcasted_iota(
        jnp.int32, (128, 128), 1
    )
    parts = []
    for c in range(HELD // 128):
        part = jnp.where(diagonal, key[c * 128 : (c + 1) * 128, :], 0.0)
        parts.append(jnp.sum(part, axis=0, keepdims=True))
    return jnp.concatenate(parts, axis=1)


def is_mixed(key):
    even = jnp.max(jnp.where(key < ODD, 1.0, 0.0), axis=1, keepdims=True)
    odd = jnp.max(jnp.where((key >= ODD) & (key < EMPTY), 1.0, 0.0), axis=1, keepdims=True)
    return jnp.max(even * odd) > 0.5


def scores_of(rows, columns):
    return lax.dot_general(
        rows, columns, (((1,), (1,)), ((), ())), preferred_element_type=jnp.float32
    )


def is_odd(key):
    return jnp.where(key >= ODD, 1.0, 0.0)


def highest(part):
    return jnp.max(part.reshape(part.shape[0] // 8, 8, 128), axis=0)


def lanes_of(chip):
    first = chip % 8 * EARLY
    last = chip % 32 * 4
    meet = (last > first - 4) & (last < first + EARLY)
    return first, jnp.where(meet, (last + 64) % 128, last)


def own_kernel(lines, best, key_rows, key_lanes, late):
    unfold_late(lines, late)
    key_rows[...] = place_of(lines)
    key_lanes[...] = along_lanes(key_rows)

    def work(mixed):
        for j in range(TILES):
            score = scores_of(tiles(lines, late, range(TILES)), tile(lines, late, j))
            row = key_rows[...]
            for c in range(TILE // 128):
                lanes = pl.ds(j * TILE + c * 128, 128)
                col = key_lanes[:, lanes]
                earlier = row < col
                if mixed:
                    earlier = earlier & (is_odd(col) == is_odd(row))
                part = score[:, c * 128 : (c + 1) * 128]
                best[:, lanes] = highest(jnp.where(earlier, part, -1.0))

    mixed = is_mixed(key_lanes[...])
    pl.when(mixed)(lambda: work(True))
    pl.when(~mixed)(lambda: work(False))


def cross_kernel(
    lines, late, start, key_rows, own_lanes, other_lines, out,
    other_late, key_lanes, best, best_lanes,
):
    core = lax.axis_index("core")
    unfold_late(other_lines, other_late)
    key_lanes[...] = along_lanes(place_of(other_lines))
    halves = ((0, 1, 2), (3, 4))

    def work(mixed, swap):
        for h in range(2):
            rows = pl.ds(halves[h][0] * TILE, len(halves[h]) * TILE)
            for j in halves[1 - h if swap else h]:
                score = scores_of(tiles(lines, late, halves[h]), tile(other_lines, other_late, j))
                row = key_rows[rows, :]
                top = None if j in (0, 3) else best[rows, :]
                for c in range(TILE // 128):
                    lanes = pl.ds(j * TILE + c * 128, 128)
                    col = key_lanes[:, lanes]
                    part = score[:, c * 128 : (c + 1) * 128]
                    earlier = col < row
                    if mixed:
                        same = is_odd(col) == is_odd(row)
                        above = jnp.where(earlier & same, part, -1.0)
                        below = jnp.where((row < col) & same, part, -1.0)
                    else:
                        above = jnp.where(earlier, part, -1.0)
                        below = jnp.where(earlier, -1.0, part)
                    top = above if top is None else jnp.maximum(top, above)
                    best_lanes[:, lanes] = highest(below)
                best[rows, :] = top

    mixed = is_mixed(jnp.concatenate([own_lanes[...], key_lanes[...]], axis=1))
    for swap in (False, True):
        here = core == (1 if swap else 0)
        pl.when(here & mixed)(lambda swap=swap: work(True, swap))
        pl.when(here & ~mixed)(lambda swap=swap: work(False, swap))

    def answer(at, chunks):
        rows = [jnp.broadcast_to(chunk, (8, 128)) for chunk in chunks[:-2]]
        early = jnp.concatenate(rows, axis=0)
        late = jnp.concatenate([jnp.broadcast_to(c, (32, 128)) for c in chunks[-2:]], axis=0)
        chip = lax.broadcasted_iota(jnp.int32, (CHIPS, 128), 0)
        lane = lax.broadcasted_iota(jnp.int32, (CHIPS, 128), 1)
        first, last = lanes_of(chip)
        late = jnp.where(last == chip % 32 * 4, late, pltpu.roll(late, 64, 1))
        here = pl.ds(pl.multiple_of(at, CHIPS), CHIPS)
        out[here, :] = jnp.where((lane >= first) & (lane < first + EARLY), early, late)

    mine, theirs = [], []
    for c in range(HELD // 128):
        lanes = pl.ds(c * 128, 128)
        eight = highest(jnp.transpose(best[pl.ds(c * 128, 128), :]))
        eight = jnp.maximum(eight, start[:, lanes])
        mine.append(jnp.max(eight, axis=0, keepdims=True))
        theirs.append(jnp.max(best_lanes[:, lanes], axis=0, keepdims=True))
    answer(core * CHIPS, mine)
    answer((1 - core) * CHIPS, theirs)


def merge_kernel(answers, slot_key, row_key, extra, out):
    keys = row_key[...]
    chip = (lax.axis_index("x") * 4 + lax.axis_index("y")) * 4 + lax.axis_index("z")
    answer = jnp.maximum(answers[pl.ds(0, CHIPS), :], answers[pl.ds(CHIPS, CHIPS), :])
    first, last = lanes_of(chip)
    early = pltpu.roll(answer, 128 - first, 1)
    late = pltpu.roll(answer, 128 - last, 1)
    best = jnp.full((CHIPS, LOCAL), -1.0, jnp.float32)
    for t in range(DATA):
        slot = slot_key[pl.ds(t // PART * CHIPS, CHIPS), :]
        slot = jnp.concatenate([slot] * (LOCAL // 128), axis=1)
        hit = slot == keys - float(t % PART)
        value = early[:, t : t + 1] if t < EARLY else late[:, t - EARLY : t - EARLY + 1]
        best = jnp.maximum(best, jnp.where(hit, value, -1.0))
    out[...] = jnp.maximum(jnp.max(best, axis=0, keepdims=True), extra[...])


VMEM = pl.BlockSpec(memory_space=pltpu.VMEM)
SMEM = pl.BlockSpec(memory_space=pltpu.SMEM)
LIMIT = 16 * 1024 * 1024


def pack(sizes, first_unit, emb, cluster, rank):
    later = first_unit is not None

    def kernel(*refs):
        if later:
            pack_kernel(refs[0][0], *refs[1:])
        else:
            pack_kernel(0, *refs)

    return pl.pallas_call(
        kernel,
        out_shape=(
            jax.ShapeDtypeStruct((CHIPS, LINES, 128), jnp.bfloat16),
            jax.ShapeDtypeStruct((1, LOCAL), jnp.float32),
            jax.ShapeDtypeStruct((4 * CHIPS, 128), jnp.float32),
            jax.ShapeDtypeStruct((1, 128), jnp.int32),
            jax.ShapeDtypeStruct((1, LOCAL), jnp.float32),
        ),
        in_specs=[SMEM] * later + [VMEM, VMEM, VMEM, VMEM],
        out_specs=(VMEM,) * 5,
        scratch_shapes=[pltpu.VMEM((LOCAL, WIDTH), jnp.bfloat16)],
        compiler_params=pltpu.CompilerParams(vmem_limit_bytes=LIMIT),
        cost_estimate=pl.CostEstimate(
            flops=2 * CHIPS * 24 * LOCAL * 640, bytes_accessed=2**21, transcendentals=0
        ),
        name="pack_later" if later else "pack",
    )(*((first_unit,) if later else ()), sizes, emb, cluster, rank)


def own_best(lines):
    return pl.pallas_call(
        own_kernel,
        out_shape=(
            jax.ShapeDtypeStruct((8, HELD), jnp.float32),
            jax.ShapeDtypeStruct((HELD, 128), jnp.float32),
            jax.ShapeDtypeStruct((1, HELD), jnp.float32),
            jax.ShapeDtypeStruct((TILE, WIDTH), jnp.bfloat16),
        ),
        in_specs=[VMEM],
        out_specs=(VMEM,) * 4,
        compiler_params=pltpu.CompilerParams(vmem_limit_bytes=LIMIT),
        cost_estimate=pl.CostEstimate(
            flops=2 * HELD * HELD * WIDTH, bytes_accessed=2**21, transcendentals=0
        ),
        name="own_best",
    )(lines)


def cross_best(lines, other):
    start, key_rows, key_lanes, late = own_best(lines)
    return pl.pallas_call(
        cross_kernel,
        out_shape=jax.ShapeDtypeStruct((2 * CHIPS, 128), jnp.float32),
        in_specs=[VMEM] * 6,
        out_specs=VMEM,
        scratch_shapes=[
            pltpu.VMEM((TILE, WIDTH), jnp.bfloat16),
            pltpu.VMEM((1, HELD), jnp.float32),
            pltpu.VMEM((HELD, 128), jnp.float32),
            pltpu.VMEM((8, HELD), jnp.float32),
        ],
        compiler_params=pltpu.CompilerParams(vmem_limit_bytes=LIMIT),
        cost_estimate=pl.CostEstimate(
            flops=HELD * HELD * WIDTH, bytes_accessed=2**21, transcendentals=0
        ),
        name="cross_best",
    )(lines, late, start, key_rows, key_lanes, other)


def merge(answers, slot_key, row_key, extra):
    return pl.pallas_call(
        merge_kernel,
        out_shape=jax.ShapeDtypeStruct((1, LOCAL), jnp.float32),
        in_specs=[VMEM] * 4,
        out_specs=VMEM,
        compiler_params=pltpu.CompilerParams(vmem_limit_bytes=16 * 1024 * 1024),
        name="merge",
    )(answers, slot_key, row_key, extra)


def exchange(values, axes):
    return lax.all_to_all(values, axes, split_axis=0, concat_axis=0, tiled=True)


def answers_of(sent):
    lines = exchange(sent, ("x", "y", "z"))
    other = lax.ppermute(lines, "core", [(0, 1), (1, 0)])
    return exchange(cross_best(lines, other), ("core", "x", "y", "z"))


def body(embeddings, cluster_sizes, cluster_of, rank_in):
    sizes = cluster_sizes.reshape(1, 2 * GROUPS)
    cluster = cluster_of.reshape(1, LOCAL)
    rank = rank_in.reshape(1, LOCAL)
    sent, row_key, slot_key, total, none = pack(sizes, None, embeddings, cluster, rank)

    def more(carry):
        return carry[0] < total[0, 0]

    def again(carry):
        unit, best = carry
        sent, row_key, slot_key, _, _ = pack(sizes, unit.reshape(1), embeddings, cluster, rank)
        return unit + CHIPS, merge(answers_of(sent), slot_key, row_key, best)

    def rounds():
        return lax.while_loop(more, again, (jnp.int32(CHIPS), none))[1]

    extra = lax.cond(total[0, 0] > CHIPS, rounds, lambda: none)
    return merge(answers_of(sent), slot_key, row_key, extra).reshape(LOCAL)


def solution(mesh):
    chips = Mesh(mesh.devices.reshape(4, 4, 4, 2), ("x", "y", "z", "core"))
    every = ("x", "y", "z", "core")
    in_specs = (P(every, None), P(), P(every), P(every))
    return jax.shard_map(
        body, mesh=chips, in_specs=in_specs, out_specs=P(every), check_vma=False
    )
```

```python
import itertools

import jax
import jax.numpy as jnp
from jax import lax
from jax.experimental import pallas as pl
from jax.experimental.pallas import tpu as pltpu
from jax.sharding import Mesh
from jax.sharding import PartitionSpec as P

SLOTS = 1280
GROUPS = 16
BLOCKS = 8
WIDTH = 512
LOCAL = 512
CHIPS = 64
DATA = 20
EARLY = 16
PART = 5
HELD = CHIPS * DATA
TILE = 256
TILES = HELD // TILE
LATE_AT = 4 * EARLY
TAGS_AT = LATE_AT + 16
LINES = TAGS_AT + 8
ODD = 16384
EMPTY = 1048576.0

COVERS = {
    1: ((0, 1, 0, 1),),
    2: ((0, 1, 2, 3),),
    3: ((0, 1, 4, 5), (1, 2, 3, 5), (0, 2, 3, 4)),
    4: ((1, 3, 6, 7), (1, 4, 5, 7), (0, 3, 4, 6), (0, 2, 3, 5), (0, 1, 2, 7), (2, 4, 5, 6)),
    5: (
        (3, 4, 6, 8), (3, 5, 8, 9), (2, 5, 6, 9), (1, 2, 3, 8), (0, 1, 6, 7),
        (1, 4, 5, 9), (0, 2, 4, 7), (0, 7, 8, 9), (0, 3, 5, 7),
    ),
    6: (
        (4, 5, 8, 10), (3, 6, 8, 11), (0, 4, 7, 11), (0, 1, 6, 10), (1, 7, 8, 9),
        (3, 5, 7, 10), (1, 3, 4, 9), (0, 5, 6, 9), (2, 9, 10, 11), (0, 2, 3, 8),
        (1, 2, 5, 11), (2, 4, 6, 7),
    ),
    7: (
        (0, 1, 5, 13), (3, 5, 8, 10), (0, 7, 10, 11), (2, 11, 12, 13), (2, 7, 8, 11),
        (1, 4, 10, 12), (8, 9, 12, 13), (1, 3, 4, 7), (4, 7, 9, 13), (3, 6, 10, 13),
        (0, 1, 2, 8), (0, 4, 6, 8), (2, 4, 5, 11), (0, 3, 9, 12), (5, 6, 7, 12),
        (2, 5, 9, 10), (1, 6, 9, 11), (2, 3, 6, 11),
    ),
}


def affine_plane():
    times = ((0, 0, 0, 0), (0, 1, 2, 3), (0, 2, 3, 1), (0, 3, 1, 2))
    lines = [tuple(4 * x + y for y in range(4)) for x in range(4)]
    for slope in range(4):
        for shift in range(4):
            lines.append(tuple(4 * x + (times[slope][x] ^ shift) for x in range(4)))
    return tuple(lines)


COVERS[8] = affine_plane()
for _m, _units in COVERS.items():
    _met = {frozenset(p) for unit in _units for p in itertools.combinations(unit, 2)}
    assert all(frozenset(p) in _met for p in itertools.combinations(range(2 * _m), 2))


def covers_by_lane():
    lane = lax.broadcasted_iota(jnp.int32, (8, 128), 1)
    packed = jnp.zeros((8, 128), jnp.int32)
    at = 0
    for m in range(1, BLOCKS + 1):
        for unit in COVERS[m]:
            value = sum(point << (4 * k) for k, point in enumerate(unit))
            packed = packed + jnp.where(lane == at, value, 0)
            at += 1
    assert at <= 128
    return packed


def by_blocks(m, values):
    picked = jnp.zeros_like(m)
    for k in range(1, BLOCKS + 1):
        picked = jnp.where(m == k, float(values[k]), picked)
    return picked


def full_blocks(places):
    return jnp.floor((places + 0.5) * (1.0 / SLOTS))


def plan(row, first_unit):
    clusters = 2 * GROUPS
    down = lax.broadcasted_iota(jnp.int32, (clusters, clusters), 0)
    across = lax.broadcasted_iota(jnp.int32, (clusters, clusters), 1)
    row = jnp.broadcast_to(row, (clusters, clusters))

    def column(mask):
        picked = jnp.sum(jnp.where(mask, row, 0.0), axis=1, keepdims=True)
        return jnp.broadcast_to(picked, (clusters, 128))

    size = column(down == across)
    partner = column(down == across + 1 - 2 * (across % 2))
    index = lax.broadcasted_iota(jnp.int32, (clusters, 128), 0)
    odd = index % 2 == 1
    first = jnp.where(odd, partner, size)
    blocks_a = full_blocks(first + (SLOTS - 1))
    start_b = full_blocks(first)
    blocks_b = full_blocks(size + partner + (SLOTS - 1)) - start_b
    blocks = jnp.where(odd, blocks_b, blocks_a)
    begin = jnp.where(odd, start_b, 0.0)
    counts = [0] + [len(COVERS[m]) for m in range(1, BLOCKS + 1)]
    alone = by_blocks(blocks, counts)
    held = (blocks == 1.0) & (blocks_a > start_b) & (odd | (blocks_b >= 2.0))
    shared = jnp.where(jnp.sum(alone, axis=0, keepdims=True) <= CHIPS, 0.0, 1.0)
    count = alone * (1.0 - shared * jnp.where(held, 1.0, 0.0))
    total = jnp.sum(count, axis=0, keepdims=True)
    start = jnp.dot(
        jnp.where(across < down, 1.0, 0.0).astype(jnp.bfloat16),
        count.astype(jnp.bfloat16),
        preferred_element_type=jnp.float32,
    )
    unit = (lax.broadcasted_iota(jnp.int32, (1, 128), 1) + first_unit).astype(jnp.float32)
    mine = (unit >= start) & (unit < start + count)

    def of_unit(values):
        return jnp.sum(jnp.where(mine, values, 0.0), axis=0, keepdims=True)

    bases = [0] + [sum(counts[:m]) for m in range(1, BLOCKS + 1)]
    entry = of_unit(by_blocks(blocks, bases) - start) + unit
    group = (index // 2).astype(jnp.float32)
    kind = 2.0 * shared + (1.0 - shared) * jnp.where(odd, 1.0, 0.0)
    half = of_unit(group * (2 * BLOCKS) + 2.0 * begin + 256.0 * kind)
    used = of_unit(jnp.where(blocks == 1.0, 1.0, 2.0))
    entry = jnp.broadcast_to(jnp.clip(entry, 0.0, 127.0).astype(jnp.int32), (8, 128))
    points = jnp.take_along_axis(covers_by_lane(), entry, axis=1)[0:1, :]
    diagonal = lax.broadcasted_iota(jnp.int32, (CHIPS, 128), 0) == lax.broadcasted_iota(
        jnp.int32, (CHIPS, 128), 1
    )
    table = []
    for a in range(4):
        point = ((points >> (4 * a)) & 15).astype(jnp.float32)
        held_by = jnp.where(used > (a // 2) + 0.5, half + point, 1024.0)
        held_by = jnp.sum(jnp.where(diagonal, held_by, 0.0), axis=1, keepdims=True)
        table.append(jnp.broadcast_to(held_by, (CHIPS, 128)))
    return table, size, jnp.where(odd, partner, 0.0), shared, total


def chip_index():
    return (lax.axis_index("x") * 4 + lax.axis_index("y")) * 4 + lax.axis_index("z")


def pack_kernel(
    first_unit, sizes, emb, cluster, rank,
    sent, row_key_out, slot_key_out, total_out, shared_out, none_out, unit,
):
    table, size, previous, shared, total = plan(sizes[...].astype(jnp.float32), first_unit)
    total_out[...] = total.astype(jnp.int32)
    shared_out[...] = jnp.broadcast_to(shared, (8, 128))
    none_out[...] = jnp.full((1, LOCAL), -1.0, jnp.float32)

    def wide(column):
        return jnp.concatenate([column] * (LOCAL // 128), axis=1)

    cluster_of = cluster[...]
    rank_in = rank[...].astype(jnp.float32)
    own = lax.broadcasted_iota(jnp.int32, (2 * GROUPS, LOCAL), 0) == cluster_of
    own_size = jnp.sum(jnp.where(own, wide(size), 0.0), axis=0, keepdims=True)
    place = rank_in + jnp.sum(jnp.where(own, wide(previous), 0.0), axis=0, keepdims=True)
    bin_of = (cluster_of // 2) * BLOCKS + full_blocks(place).astype(jnp.int32)
    bins = lax.broadcasted_iota(jnp.int32, (GROUPS * BLOCKS, LOCAL), 0)
    member = jnp.where(bins == bin_of, 1.0, 0.0)
    until = lax.broadcasted_iota(jnp.int32, (128, 256), 0) <= lax.broadcasted_iota(
        jnp.int32, (128, 256), 1
    )
    until = jnp.where(until, 1.0, 0.0).astype(jnp.bfloat16)
    passed = jnp.full((GROUPS * BLOCKS, 128), -1.0, jnp.float32)
    bucket = []
    for c in range(LOCAL // 128):
        part = member[:, c * 128 : (c + 1) * 128]
        seen = jnp.dot(part.astype(jnp.bfloat16), until, preferred_element_type=jnp.float32)
        before = passed + seen[:, :128]
        passed = passed + seen[:, 128:]
        bucket.append(jnp.sum(part * before, axis=0, keepdims=True))
    bucket = jnp.concatenate(bucket, axis=1)
    upper = jnp.floor((bucket + 0.5) * 0.5)
    odd = cluster_of % 2
    kind = wide(shared)
    kind = 2.0 * kind + (1.0 - kind) * odd.astype(jnp.float32)
    half_key = bin_of.astype(jnp.float32) * 2.0 + (bucket - 2.0 * upper) + 256.0 * kind
    row_key = half_key * 8.0 + upper
    row_key_out[...] = jnp.where(rank_in < own_size, row_key, -7.0)

    high = jnp.floor((rank_in + 0.5) * (1.0 / 128))
    low = rank_in - 128.0 * high
    high = high + 1.0 + (odd * (ODD // 128)).astype(jnp.float32)
    down = lax.broadcasted_iota(jnp.int32, (128, LOCAL), 0)
    parts = jnp.where(down >= 64, low, high)
    seat = (down % 64).astype(jnp.float32)
    holds, tags = [], []
    for a in range(4):
        holds.append(jnp.where(wide(table[a]) == half_key, 1.0, 0.0).astype(jnp.bfloat16))
        here = seat == upper + float(PART * a)
        tags.append(jnp.where(here, parts, 0.0).astype(jnp.bfloat16))
    tag = lax.dot_general(
        jnp.concatenate(holds, axis=1),
        jnp.concatenate(tags, axis=1),
        (((1,), (1,)), ((), ())),
        preferred_element_type=jnp.float32,
    )
    chip = chip_index()
    lane = lax.broadcasted_iota(jnp.int32, (CHIPS, 128), 1)
    row = lax.broadcasted_iota(jnp.int32, (CHIPS, 8, 128), 1)
    lines = jnp.zeros((CHIPS, 8, 128), jnp.float32)
    moves = (
        (0, EARLY, chip % 8 * EARLY),
        (64, EARLY, chip % 8 * EARLY),
        (EARLY, 4, chip % 32 * 4),
        (64 + EARLY, 4, chip % 32 * 4),
    )
    for k, (first, count, to) in enumerate(moves):
        part = jnp.where((lane >= first) & (lane < first + count), tag, 0.0)
        part = pltpu.roll(part, (to + 128 - first) % 128, 1).reshape(CHIPS, 1, 128)
        lines = jnp.where(row == k, jnp.broadcast_to(part, (CHIPS, 8, 128)), lines)
    sent[:, pl.ds(TAGS_AT, 8), :] = lines.astype(jnp.bfloat16)

    for a in range(4):
        table[a] = table[a] * 8.0
        slot_key_out[pl.ds(a * CHIPS, CHIPS), :] = table[a]

    values = emb[...].astype(jnp.float32)
    scale = 1.0 / jnp.sqrt(jnp.sum(values * values, axis=1, keepdims=True) + 1e-06)
    unit[...] = (values * scale).astype(jnp.bfloat16)

    some, picks = 16, EARLY + 8
    row = lax.broadcasted_iota(jnp.int32, (some, picks, 128), 1)
    slot = jnp.where(row >= DATA, row - 4, row)
    rest = slot
    for a in range(1, 4):
        rest = rest - jnp.where(slot >= PART * a, PART, 0)
    rest = rest.astype(jnp.float32)
    low_rows = lax.broadcasted_iota(jnp.int32, (some, 8, 128), 1) < 4
    for k in range(CHIPS // some):
        key = jnp.zeros((some, picks, 128), jnp.float32)
        for a in range(3, -1, -1):
            part = table[a][k * some : (k + 1) * some, :].reshape(some, 1, 128)
            part = jnp.broadcast_to(part, (some, picks, 128))
            key = part if a == 3 else jnp.where(slot < PART * (a + 1), part, key)
        key = (key + rest).reshape(some * picks, 128)
        chosen = []
        for c in range(LOCAL // 128):
            hit = key == row_key[:, c * 128 : (c + 1) * 128]
            chosen.append(jnp.where(hit, 1.0, 0.0).astype(jnp.bfloat16))
        chosen = jnp.concatenate(chosen, axis=1)
        chips = pl.ds(k * some, some)
        data = jnp.dot(chosen, unit[...], preferred_element_type=jnp.float32)
        quarters = [
            data[:, q * 128 : (q + 1) * 128].reshape(some, picks, 128) for q in range(4)
        ]
        for q in range(4):
            sent[chips, pl.ds(q * EARLY, EARLY), :] = quarters[q][:, :EARLY].astype(jnp.bfloat16)
        late = [quarter[:, EARLY:] for quarter in quarters]
        late = [jnp.where(low_rows, late[q], late[q + 1]) for q in (0, 2)]
        sent[chips, pl.ds(LATE_AT, 16), :] = jnp.concatenate(late, axis=1).astype(jnp.bfloat16)


def unfold_late(lines, late):
    part = lines[:, pl.ds(LATE_AT, 16), :].astype(jnp.float32).reshape(CHIPS // 2, 2, 16, 128)
    low_rows = lax.broadcasted_iota(jnp.int32, (CHIPS // 2, 8, 128), 1) < 4
    for q in (0, 2):
        even, odd = part[:, 0, q * 4 : q * 4 + 8], part[:, 1, q * 4 : q * 4 + 8]
        quarters = (
            jnp.where(low_rows, even, pltpu.roll(odd, 4, 1)),
            jnp.where(low_rows, pltpu.roll(even, 4, 1), odd),
        )
        for k in range(2):
            late[:, pl.ds((q + k) * 128, 128)] = (
                quarters[k].reshape(CHIPS * 4, 128).astype(jnp.bfloat16)
            )


def tile(lines, late, n):
    if n == TILES - 1:
        return late[...]
    sources = pl.ds(n * (TILE // EARLY), TILE // EARLY)
    quarters = [lines[sources, pl.ds(q * EARLY, EARLY), :] for q in range(4)]
    return jnp.concatenate([part.reshape(TILE, 128) for part in quarters], axis=1)


def tiles(lines, late, some):
    return jnp.concatenate([tile(lines, late, n) for n in some], axis=0)


def keys_of(lines):
    tags = lines[:, pl.ds(TAGS_AT, 8), :].astype(jnp.float32)
    row = lax.broadcasted_iota(jnp.int32, (8, 128), 0)
    first = jnp.where(row == 0, 128.0, 0.0) + jnp.where(row == 1, 1.0, 0.0)
    last = jnp.where(row == 2, 128.0, 0.0) + jnp.where(row == 3, 1.0, 0.0)
    eights = [jnp.sum(tags[c * 8 : (c + 1) * 8], axis=0) for c in range(CHIPS // 8)]
    early = [eight * first for eight in eights]
    late = [sum(eights[c * 4 : (c + 1) * 4]) * last for c in range(CHIPS // 32)]
    key = jnp.concatenate([jnp.sum(k, axis=0, keepdims=True) for k in early + late], axis=1)
    return jnp.where(key == 0.0, EMPTY, key)


def scores_of(rows, columns):
    return lax.dot_general(
        rows, columns, (((1,), (1,)), ((), ())), preferred_element_type=jnp.float32
    )


def is_odd(key):
    return jnp.where(key >= ODD, 1.0, 0.0)


def highest(part):
    return jnp.max(part.reshape(part.shape[0] // 8, 8, 128), axis=0)


def lanes_of(chip):
    first = chip % 8 * EARLY
    last = chip % 32 * 4
    meet = (last > first - 4) & (last < first + EARLY)
    return first, jnp.where(meet, (last + 64) % 128, last)


def own_kernel(lines, shared, best, key_rows, late, key_lanes):
    unfold_late(lines, late)
    key_lanes[...] = keys_of(lines)
    for c in range(HELD // 128):
        chunk = pl.ds(c * 128, 128)
        key_rows[chunk, :] = jnp.transpose(jnp.broadcast_to(key_lanes[:, chunk], (128, 128)))

    def work(mixed):
        for j in range(TILES):
            score = scores_of(tiles(lines, late, range(TILES)), tile(lines, late, j))
            row = key_rows[...]
            for c in range(TILE // 128):
                lanes = pl.ds(j * TILE + c * 128, 128)
                col = key_lanes[:, lanes]
                earlier = row < col
                if mixed:
                    earlier = earlier & (is_odd(col) == is_odd(row))
                part = score[:, c * 128 : (c + 1) * 128]
                best[:, lanes] = highest(jnp.where(earlier, part, -1.0))

    mixed = shared[...][0, 0] > 0.5
    pl.when(mixed)(lambda: work(True))
    pl.when(~mixed)(lambda: work(False))


def cross_kernel(
    lines, late, start, key_rows, other_lines, shared, out,
    other_late, key_lanes, best, best_lanes,
):
    core = lax.axis_index("core")
    unfold_late(other_lines, other_late)
    key_lanes[...] = keys_of(other_lines)
    halves = ((0, 1, 2), (3, 4))

    def work(mixed, swap):
        for h in range(2):
            rows = pl.ds(halves[h][0] * TILE, len(halves[h]) * TILE)
            for j in halves[1 - h if swap else h]:
                score = scores_of(tiles(lines, late, halves[h]), tile(other_lines, other_late, j))
                row = key_rows[rows, :]
                top = None if j in (0, 3) else best[rows, :]
                for c in range(TILE // 128):
                    lanes = pl.ds(j * TILE + c * 128, 128)
                    col = key_lanes[:, lanes]
                    part = score[:, c * 128 : (c + 1) * 128]
                    earlier = col < row
                    if mixed:
                        same = is_odd(col) == is_odd(row)
                        above = jnp.where(earlier & same, part, -1.0)
                        below = jnp.where((row < col) & same, part, -1.0)
                    else:
                        above = jnp.where(earlier, part, -1.0)
                        below = jnp.where(earlier, -1.0, part)
                    top = above if top is None else jnp.maximum(top, above)
                    best_lanes[:, lanes] = highest(below)
                best[rows, :] = top

    mixed = shared[...][0, 0] > 0.5
    for swap in (False, True):
        here = core == (1 if swap else 0)
        pl.when(here & mixed)(lambda swap=swap: work(True, swap))
        pl.when(here & ~mixed)(lambda swap=swap: work(False, swap))

    def answer(at, chunks):
        rows = [jnp.broadcast_to(chunk, (8, 128)) for chunk in chunks[:-2]]
        early = jnp.concatenate(rows, axis=0)
        late = jnp.concatenate([jnp.broadcast_to(c, (32, 128)) for c in chunks[-2:]], axis=0)
        chip = lax.broadcasted_iota(jnp.int32, (CHIPS, 128), 0)
        lane = lax.broadcasted_iota(jnp.int32, (CHIPS, 128), 1)
        first, last = lanes_of(chip)
        late = jnp.where(last == chip % 32 * 4, late, pltpu.roll(late, 64, 1))
        here = pl.ds(pl.multiple_of(at, CHIPS), CHIPS)
        out[here, :] = jnp.where((lane >= first) & (lane < first + EARLY), early, late)

    mine, theirs = [], []
    for c in range(HELD // 128):
        lanes = pl.ds(c * 128, 128)
        eight = highest(jnp.transpose(best[pl.ds(c * 128, 128), :]))
        eight = jnp.maximum(eight, start[:, lanes])
        mine.append(jnp.max(eight, axis=0, keepdims=True))
        theirs.append(jnp.max(best_lanes[:, lanes], axis=0, keepdims=True))
    answer(core * CHIPS, mine)
    answer((1 - core) * CHIPS, theirs)


def merge_kernel(answers, slot_key, row_key, extra, out):
    keys = row_key[...]
    chip = chip_index()
    answer = jnp.maximum(answers[pl.ds(0, CHIPS), :], answers[pl.ds(CHIPS, CHIPS), :])
    first, last = lanes_of(chip)
    early = pltpu.roll(answer, 128 - first, 1)
    late = pltpu.roll(answer, 128 - last, 1)
    best = jnp.full((CHIPS, LOCAL), -1.0, jnp.float32)
    for t in range(DATA):
        slot = slot_key[pl.ds(t // PART * CHIPS, CHIPS), :]
        slot = jnp.concatenate([slot] * (LOCAL // 128), axis=1)
        hit = slot == keys - float(t % PART)
        value = early[:, t : t + 1] if t < EARLY else late[:, t - EARLY : t - EARLY + 1]
        best = jnp.maximum(best, jnp.where(hit, value, -1.0))
    out[...] = jnp.maximum(jnp.max(best, axis=0, keepdims=True), extra[...])


VMEM = pl.BlockSpec(memory_space=pltpu.VMEM)
SMEM = pl.BlockSpec(memory_space=pltpu.SMEM)
LIMIT = 16 * 1024 * 1024


def pack(sizes, first_unit, emb, cluster, rank):
    later = first_unit is not None

    def kernel(*refs):
        if later:
            pack_kernel(refs[0][0], *refs[1:])
        else:
            pack_kernel(0, *refs)

    return pl.pallas_call(
        kernel,
        out_shape=(
            jax.ShapeDtypeStruct((CHIPS, LINES, 128), jnp.bfloat16),
            jax.ShapeDtypeStruct((1, LOCAL), jnp.float32),
            jax.ShapeDtypeStruct((4 * CHIPS, 128), jnp.float32),
            jax.ShapeDtypeStruct((1, 128), jnp.int32),
            jax.ShapeDtypeStruct((8, 128), jnp.float32),
            jax.ShapeDtypeStruct((1, LOCAL), jnp.float32),
        ),
        in_specs=[SMEM] * later + [VMEM, VMEM, VMEM, VMEM],
        out_specs=(VMEM,) * 6,
        scratch_shapes=[pltpu.VMEM((LOCAL, WIDTH), jnp.bfloat16)],
        compiler_params=pltpu.CompilerParams(vmem_limit_bytes=LIMIT),
        cost_estimate=pl.CostEstimate(
            flops=2 * CHIPS * 24 * LOCAL * 640, bytes_accessed=2**21, transcendentals=0
        ),
        name="pack_later" if later else "pack",
    )(*((first_unit,) if later else ()), sizes, emb, cluster, rank)


def own_best(lines, shared):
    return pl.pallas_call(
        own_kernel,
        out_shape=(
            jax.ShapeDtypeStruct((8, HELD), jnp.float32),
            jax.ShapeDtypeStruct((HELD, 128), jnp.float32),
            jax.ShapeDtypeStruct((TILE, WIDTH), jnp.bfloat16),
        ),
        in_specs=[VMEM] * 2,
        out_specs=(VMEM,) * 3,
        scratch_shapes=[pltpu.VMEM((1, HELD), jnp.float32)],
        compiler_params=pltpu.CompilerParams(vmem_limit_bytes=LIMIT),
        cost_estimate=pl.CostEstimate(
            flops=2 * HELD * HELD * WIDTH, bytes_accessed=2**21, transcendentals=0
        ),
        name="own_best",
    )(lines, shared)


def cross_best(lines, other, shared):
    start, key_rows, late = own_best(lines, shared)
    return pl.pallas_call(
        cross_kernel,
        out_shape=jax.ShapeDtypeStruct((2 * CHIPS, 128), jnp.float32),
        in_specs=[VMEM] * 6,
        out_specs=VMEM,
        scratch_shapes=[
            pltpu.VMEM((TILE, WIDTH), jnp.bfloat16),
            pltpu.VMEM((1, HELD), jnp.float32),
            pltpu.VMEM((HELD, 128), jnp.float32),
            pltpu.VMEM((8, HELD), jnp.float32),
        ],
        compiler_params=pltpu.CompilerParams(vmem_limit_bytes=LIMIT),
        cost_estimate=pl.CostEstimate(
            flops=HELD * HELD * WIDTH, bytes_accessed=2**21, transcendentals=0
        ),
        name="cross_best",
    )(lines, late, start, key_rows, other, shared)


def merge(answers, slot_key, row_key, extra):
    return pl.pallas_call(
        merge_kernel,
        out_shape=jax.ShapeDtypeStruct((1, LOCAL), jnp.float32),
        in_specs=[VMEM] * 4,
        out_specs=VMEM,
        compiler_params=pltpu.CompilerParams(vmem_limit_bytes=16 * 1024 * 1024),
        name="merge",
    )(answers, slot_key, row_key, extra)


def exchange(values, axes):
    return lax.all_to_all(values, axes, split_axis=0, concat_axis=0, tiled=True)


def answers_of(sent, shared):
    lines = exchange(sent, ("x", "y", "z"))
    other = lax.ppermute(lines, "core", [(0, 1), (1, 0)])
    return exchange(cross_best(lines, other, shared), ("core", "x", "y", "z"))


def body(embeddings, cluster_sizes, cluster_of, rank_in):
    sizes = cluster_sizes.reshape(1, 2 * GROUPS)
    cluster = cluster_of.reshape(1, LOCAL)
    rank = rank_in.reshape(1, LOCAL)
    sent, row_key, slot_key, total, shared, none = pack(sizes, None, embeddings, cluster, rank)

    def more(carry):
        return carry[0] < total[0, 0]

    def again(carry):
        unit, best = carry
        sent, row_key, slot_key, _, _, _ = pack(sizes, unit.reshape(1), embeddings, cluster, rank)
        return unit + CHIPS, merge(answers_of(sent, shared), slot_key, row_key, best)

    def rounds():
        return lax.while_loop(more, again, (jnp.int32(CHIPS), none))[1]

    extra = lax.cond(total[0, 0] > CHIPS, rounds, lambda: none)
    return merge(answers_of(sent, shared), slot_key, row_key, extra).reshape(LOCAL)


def solution(mesh):
    chips = Mesh(mesh.devices.reshape(4, 4, 4, 2), ("x", "y", "z", "core"))
    every = ("x", "y", "z", "core")
    in_specs = (P(every, None), P(), P(every), P(every))
    return jax.shard_map(
        body, mesh=chips, in_specs=in_specs, out_specs=P(every), check_vma=False
    )
```

```python
import itertools

import jax
import jax.numpy as jnp
from jax import lax
from jax.experimental import pallas as pl
from jax.experimental.pallas import tpu as pltpu
from jax.sharding import Mesh
from jax.sharding import PartitionSpec as P

SLOTS = 1280
GROUPS = 16
BLOCKS = 8
WIDTH = 512
LOCAL = 512
CHIPS = 64
DATA = 20
EARLY = 16
PART = 5
HELD = CHIPS * DATA
TILE = 256
TILES = HELD // TILE
LATE_AT = 4 * EARLY
TAGS_AT = LATE_AT + 16
LINES = TAGS_AT + 8
ODD = 16384
EMPTY = 1048576.0

COVERS = {
    1: ((0, 1, 0, 1),),
    2: ((0, 1, 2, 3),),
    3: ((0, 1, 4, 5), (1, 2, 3, 5), (0, 2, 3, 4)),
    4: ((1, 3, 6, 7), (1, 4, 5, 7), (0, 3, 4, 6), (0, 2, 3, 5), (0, 1, 2, 7), (2, 4, 5, 6)),
    5: (
        (3, 4, 6, 8), (3, 5, 8, 9), (2, 5, 6, 9), (1, 2, 3, 8), (0, 1, 6, 7),
        (1, 4, 5, 9), (0, 2, 4, 7), (0, 7, 8, 9), (0, 3, 5, 7),
    ),
    6: (
        (4, 5, 8, 10), (3, 6, 8, 11), (0, 4, 7, 11), (0, 1, 6, 10), (1, 7, 8, 9),
        (3, 5, 7, 10), (1, 3, 4, 9), (0, 5, 6, 9), (2, 9, 10, 11), (0, 2, 3, 8),
        (1, 2, 5, 11), (2, 4, 6, 7),
    ),
    7: (
        (0, 1, 5, 13), (3, 5, 8, 10), (0, 7, 10, 11), (2, 11, 12, 13), (2, 7, 8, 11),
        (1, 4, 10, 12), (8, 9, 12, 13), (1, 3, 4, 7), (4, 7, 9, 13), (3, 6, 10, 13),
        (0, 1, 2, 8), (0, 4, 6, 8), (2, 4, 5, 11), (0, 3, 9, 12), (5, 6, 7, 12),
        (2, 5, 9, 10), (1, 6, 9, 11), (2, 3, 6, 11),
    ),
}


def affine_plane():
    times = ((0, 0, 0, 0), (0, 1, 2, 3), (0, 2, 3, 1), (0, 3, 1, 2))
    lines = [tuple(4 * x + y for y in range(4)) for x in range(4)]
    for slope in range(4):
        for shift in range(4):
            lines.append(tuple(4 * x + (times[slope][x] ^ shift) for x in range(4)))
    return tuple(lines)


COVERS[8] = affine_plane()
for _m, _units in COVERS.items():
    _met = {frozenset(p) for unit in _units for p in itertools.combinations(unit, 2)}
    assert all(frozenset(p) in _met for p in itertools.combinations(range(2 * _m), 2))


def covers_by_lane():
    lane = lax.broadcasted_iota(jnp.int32, (8, 128), 1)
    packed = jnp.zeros((8, 128), jnp.int32)
    at = 0
    for m in range(1, BLOCKS + 1):
        for unit in COVERS[m]:
            value = sum(point << (4 * k) for k, point in enumerate(unit))
            packed = packed + jnp.where(lane == at, value, 0)
            at += 1
    assert at <= 128
    return packed


def by_blocks(m, values):
    picked = jnp.zeros_like(m)
    for k in range(1, BLOCKS + 1):
        picked = jnp.where(m == k, float(values[k]), picked)
    return picked


def full_blocks(places):
    return jnp.floor((places + 0.5) * (1.0 / SLOTS))


def plan(row, first_unit):
    clusters = 2 * GROUPS
    down = lax.broadcasted_iota(jnp.int32, (clusters, clusters), 0)
    across = lax.broadcasted_iota(jnp.int32, (clusters, clusters), 1)
    row = jnp.broadcast_to(row, (clusters, clusters))

    def column(mask):
        picked = jnp.sum(jnp.where(mask, row, 0.0), axis=1, keepdims=True)
        return jnp.broadcast_to(picked, (clusters, 128))

    size = column(down == across)
    partner = column(down == across + 1 - 2 * (across % 2))
    index = lax.broadcasted_iota(jnp.int32, (clusters, 128), 0)
    odd = index % 2 == 1
    first = jnp.where(odd, partner, size)
    blocks_a = full_blocks(first + (SLOTS - 1))
    start_b = full_blocks(first)
    blocks_b = full_blocks(size + partner + (SLOTS - 1)) - start_b
    blocks = jnp.where(odd, blocks_b, blocks_a)
    begin = jnp.where(odd, start_b, 0.0)
    counts = [0] + [len(COVERS[m]) for m in range(1, BLOCKS + 1)]
    alone = by_blocks(blocks, counts)
    held = (blocks == 1.0) & (blocks_a > start_b) & (odd | (blocks_b >= 2.0))
    shared = jnp.where(jnp.sum(alone, axis=0, keepdims=True) <= CHIPS, 0.0, 1.0)
    count = alone * (1.0 - shared * jnp.where(held, 1.0, 0.0))
    total = jnp.sum(count, axis=0, keepdims=True)
    start = jnp.dot(
        jnp.where(across < down, 1.0, 0.0).astype(jnp.bfloat16),
        count.astype(jnp.bfloat16),
        preferred_element_type=jnp.float32,
    )
    unit = (lax.broadcasted_iota(jnp.int32, (1, 128), 1) + first_unit).astype(jnp.float32)
    mine = (unit >= start) & (unit < start + count)

    def of_unit(values):
        return jnp.sum(jnp.where(mine, values, 0.0), axis=0, keepdims=True)

    bases = [0] + [sum(counts[:m]) for m in range(1, BLOCKS + 1)]
    entry = of_unit(by_blocks(blocks, bases) - start) + unit
    group = (index // 2).astype(jnp.float32)
    kind = 2.0 * shared + (1.0 - shared) * jnp.where(odd, 1.0, 0.0)
    half = of_unit(group * (2 * BLOCKS) + 2.0 * begin + 256.0 * kind)
    used = of_unit(jnp.where(blocks == 1.0, 1.0, 2.0))
    entry = jnp.broadcast_to(jnp.clip(entry, 0.0, 127.0).astype(jnp.int32), (8, 128))
    points = jnp.take_along_axis(covers_by_lane(), entry, axis=1)[0:1, :]
    diagonal = lax.broadcasted_iota(jnp.int32, (CHIPS, 128), 0) == lax.broadcasted_iota(
        jnp.int32, (CHIPS, 128), 1
    )
    table = []
    for a in range(4):
        point = ((points >> (4 * a)) & 15).astype(jnp.float32)
        held_by = jnp.where(used > (a // 2) + 0.5, half + point, 1024.0)
        held_by = jnp.sum(jnp.where(diagonal, held_by, 0.0), axis=1, keepdims=True)
        table.append(jnp.broadcast_to(held_by, (CHIPS, 128)))
    return table, size, jnp.where(odd, partner, 0.0), shared, total


def chip_index():
    return (lax.axis_index("x") * 4 + lax.axis_index("y")) * 4 + lax.axis_index("z")


def pack_kernel(
    first_unit, sizes, emb, cluster, rank,
    sent, row_key_out, slot_key_out, total_out, shared_out, none_out, unit,
):
    table, size, previous, shared, total = plan(sizes[...].astype(jnp.float32), first_unit)
    total_out[...] = total.astype(jnp.int32)
    shared_out[...] = jnp.broadcast_to(shared, (8, 128))
    none_out[...] = jnp.full((1, LOCAL), -1.0, jnp.float32)

    def wide(column):
        return jnp.concatenate([column] * (LOCAL // 128), axis=1)

    cluster_of = cluster[...]
    rank_in = rank[...].astype(jnp.float32)
    own = lax.broadcasted_iota(jnp.int32, (2 * GROUPS, LOCAL), 0) == cluster_of
    own_size = jnp.sum(jnp.where(own, wide(size), 0.0), axis=0, keepdims=True)
    place = rank_in + jnp.sum(jnp.where(own, wide(previous), 0.0), axis=0, keepdims=True)
    bin_of = (cluster_of // 2) * BLOCKS + full_blocks(place).astype(jnp.int32)
    bins = lax.broadcasted_iota(jnp.int32, (GROUPS * BLOCKS, LOCAL), 0)
    member = jnp.where(bins == bin_of, 1.0, 0.0)
    until = lax.broadcasted_iota(jnp.int32, (128, 256), 0) <= lax.broadcasted_iota(
        jnp.int32, (128, 256), 1
    )
    until = jnp.where(until, 1.0, 0.0).astype(jnp.bfloat16)
    passed = jnp.full((GROUPS * BLOCKS, 128), -1.0, jnp.float32)
    bucket = []
    for c in range(LOCAL // 128):
        part = member[:, c * 128 : (c + 1) * 128]
        seen = jnp.dot(part.astype(jnp.bfloat16), until, preferred_element_type=jnp.float32)
        before = passed + seen[:, :128]
        passed = passed + seen[:, 128:]
        bucket.append(jnp.sum(part * before, axis=0, keepdims=True))
    bucket = jnp.concatenate(bucket, axis=1)
    upper = jnp.floor((bucket + 0.5) * 0.5)
    odd = cluster_of % 2
    kind = wide(shared)
    kind = 2.0 * kind + (1.0 - kind) * odd.astype(jnp.float32)
    half_key = bin_of.astype(jnp.float32) * 2.0 + (bucket - 2.0 * upper) + 256.0 * kind
    row_key = half_key * 8.0 + upper
    row_key_out[...] = jnp.where(rank_in < own_size, row_key, -7.0)

    high = jnp.floor((rank_in + 0.5) * (1.0 / 128))
    low = rank_in - 128.0 * high
    high = high + 1.0 + (odd * (ODD // 128)).astype(jnp.float32)
    down = lax.broadcasted_iota(jnp.int32, (128, LOCAL), 0)
    parts = jnp.where(down >= 64, low, high)
    seat = (down % 64).astype(jnp.float32)
    holds, tags = [], []
    for a in range(4):
        holds.append(jnp.where(wide(table[a]) == half_key, 1.0, 0.0).astype(jnp.bfloat16))
        here = seat == upper + float(PART * a)
        tags.append(jnp.where(here, parts, 0.0).astype(jnp.bfloat16))
    tag = lax.dot_general(
        jnp.concatenate(holds, axis=1),
        jnp.concatenate(tags, axis=1),
        (((1,), (1,)), ((), ())),
        preferred_element_type=jnp.float32,
    )
    chip = chip_index()
    lane = lax.broadcasted_iota(jnp.int32, (CHIPS, 128), 1)
    row = lax.broadcasted_iota(jnp.int32, (CHIPS, 8, 128), 1)
    lines = jnp.zeros((CHIPS, 8, 128), jnp.float32)
    moves = (
        (0, EARLY, chip % 8 * EARLY),
        (64, EARLY, chip % 8 * EARLY),
        (EARLY, 4, chip % 32 * 4),
        (64 + EARLY, 4, chip % 32 * 4),
    )
    for k, (first, count, to) in enumerate(moves):
        part = jnp.where((lane >= first) & (lane < first + count), tag, 0.0)
        part = pltpu.roll(part, (to + 128 - first) % 128, 1).reshape(CHIPS, 1, 128)
        lines = jnp.where(row == k, jnp.broadcast_to(part, (CHIPS, 8, 128)), lines)
    sent[:, pl.ds(TAGS_AT, 8), :] = lines.astype(jnp.bfloat16)

    for a in range(4):
        table[a] = table[a] * 8.0
        slot_key_out[pl.ds(a * CHIPS, CHIPS), :] = table[a]

    values = emb[...].astype(jnp.float32)
    scale = 1.0 / jnp.sqrt(jnp.sum(values * values, axis=1, keepdims=True) + 1e-06)
    unit[...] = (values * scale).astype(jnp.bfloat16)

    def picked(parts, slot):
        key = jnp.broadcast_to(parts[-1], slot.shape)
        rest = slot
        for a in range(1, 4):
            rest = rest - jnp.where(slot >= PART * a, PART, 0)
        for a in range(2, -1, -1):
            part = jnp.broadcast_to(parts[a], slot.shape)
            key = jnp.where(slot < PART * (a + 1), part, key)
        key = (key + rest.astype(jnp.float32)).reshape(slot.shape[0] * slot.shape[1], 128)
        chosen = []
        for c in range(LOCAL // 128):
            hit = key == row_key[:, c * 128 : (c + 1) * 128]
            chosen.append(jnp.where(hit, 1.0, 0.0).astype(jnp.bfloat16))
        data = jnp.dot(
            jnp.concatenate(chosen, axis=1), unit[...], preferred_element_type=jnp.float32
        )
        return [data[:, q * 128 : (q + 1) * 128].reshape(slot.shape) for q in range(4)]

    pairs = CHIPS // 2
    row = lax.broadcasted_iota(jnp.int32, (pairs, 8, 128), 1)
    last = table[3].reshape(pairs, 2, 1, 128)
    even, odd_one = (jnp.broadcast_to(last[:, k], (pairs, 8, 128)) for k in range(2))
    last = jnp.where(row < 4, even, odd_one)
    late = picked([last] * 4, EARLY + row % 4)
    moved = [pltpu.roll(part, 4, 1) for part in late]
    folded = [
        jnp.concatenate([jnp.where(row < 4, late[q], moved[q + 1]) for q in (0, 2)], axis=1),
        jnp.concatenate([jnp.where(row < 4, moved[q], late[q + 1]) for q in (0, 2)], axis=1),
    ]
    folded = jnp.stack(folded, axis=1).reshape(CHIPS, 16, 128)
    sent[:, pl.ds(LATE_AT, 16), :] = folded.astype(jnp.bfloat16)

    some = 16
    slot = lax.broadcasted_iota(jnp.int32, (some, EARLY, 128), 1)
    for k in range(CHIPS // some):
        chips = pl.ds(k * some, some)
        parts = [part[k * some : (k + 1) * some, :].reshape(some, 1, 128) for part in table]
        quarters = picked(parts, slot)
        for q in range(4):
            sent[chips, pl.ds(q * EARLY, EARLY), :] = quarters[q].astype(jnp.bfloat16)


def unfold_late(lines, late):
    part = lines[:, pl.ds(LATE_AT, 16), :].astype(jnp.float32).reshape(CHIPS // 2, 2, 16, 128)
    low_rows = lax.broadcasted_iota(jnp.int32, (CHIPS // 2, 8, 128), 1) < 4
    for q in (0, 2):
        even, odd = part[:, 0, q * 4 : q * 4 + 8], part[:, 1, q * 4 : q * 4 + 8]
        quarters = (
            jnp.where(low_rows, even, pltpu.roll(odd, 4, 1)),
            jnp.where(low_rows, pltpu.roll(even, 4, 1), odd),
        )
        for k in range(2):
            late[:, pl.ds((q + k) * 128, 128)] = (
                quarters[k].reshape(CHIPS * 4, 128).astype(jnp.bfloat16)
            )


def tile(lines, late, n):
    if n == TILES - 1:
        return late[...]
    sources = pl.ds(n * (TILE // EARLY), TILE // EARLY)
    quarters = [lines[sources, pl.ds(q * EARLY, EARLY), :] for q in range(4)]
    return jnp.concatenate([part.reshape(TILE, 128) for part in quarters], axis=1)


def tiles(lines, late, some):
    return jnp.concatenate([tile(lines, late, n) for n in some], axis=0)


def keys_of(lines):
    tags = lines[:, pl.ds(TAGS_AT, 8), :].astype(jnp.float32)
    row = lax.broadcasted_iota(jnp.int32, (8, 128), 0)
    first = jnp.where(row == 0, 128.0, 0.0) + jnp.where(row == 1, 1.0, 0.0)
    last = jnp.where(row == 2, 128.0, 0.0) + jnp.where(row == 3, 1.0, 0.0)
    eights = [jnp.sum(tags[c * 8 : (c + 1) * 8], axis=0) for c in range(CHIPS // 8)]
    early = [eight * first for eight in eights]
    late = [sum(eights[c * 4 : (c + 1) * 4]) * last for c in range(CHIPS // 32)]
    key = jnp.concatenate([jnp.sum(k, axis=0, keepdims=True) for k in early + late], axis=1)
    return jnp.where(key == 0.0, EMPTY, key)


def scores_of(rows, columns):
    return lax.dot_general(
        rows, columns, (((1,), (1,)), ((), ())), preferred_element_type=jnp.float32
    )


def is_odd(key):
    return jnp.where(key >= ODD, 1.0, 0.0)


def highest(part):
    return jnp.max(part.reshape(part.shape[0] // 8, 8, 128), axis=0)


def lanes_of(chip):
    first = chip % 8 * EARLY
    last = chip % 32 * 4
    meet = (last > first - 4) & (last < first + EARLY)
    return first, jnp.where(meet, (last + 64) % 128, last)


def own_kernel(lines, shared, best, key_rows, late, key_lanes):
    unfold_late(lines, late)
    key_lanes[...] = keys_of(lines)
    for c in range(HELD // 128):
        chunk = pl.ds(c * 128, 128)
        key_rows[chunk, :] = jnp.transpose(jnp.broadcast_to(key_lanes[:, chunk], (128, 128)))

    def work(mixed):
        for j in range(TILES):
            score = scores_of(tiles(lines, late, range(TILES)), tile(lines, late, j))
            row = key_rows[...]
            for c in range(TILE // 128):
                lanes = pl.ds(j * TILE + c * 128, 128)
                col = key_lanes[:, lanes]
                earlier = row < col
                if mixed:
                    earlier = earlier & (is_odd(col) == is_odd(row))
                part = score[:, c * 128 : (c + 1) * 128]
                best[:, lanes] = highest(jnp.where(earlier, part, -1.0))

    mixed = shared[...][0, 0] > 0.5
    pl.when(mixed)(lambda: work(True))
    pl.when(~mixed)(lambda: work(False))


def cross_kernel(
    lines, late, start, key_rows, other_lines, shared, out, other_late, key_lanes, best
):
    core = lax.axis_index("core")
    halves = ((0, 1, 2), (3, 4))

    def answer(at, chunks):
        rows = [jnp.broadcast_to(chunk, (8, 128)) for chunk in chunks[:-2]]
        early = jnp.concatenate(rows, axis=0)
        last = jnp.concatenate([jnp.broadcast_to(c, (32, 128)) for c in chunks[-2:]], axis=0)
        chip = lax.broadcasted_iota(jnp.int32, (CHIPS, 128), 0)
        lane = lax.broadcasted_iota(jnp.int32, (CHIPS, 128), 1)
        first, final = lanes_of(chip)
        last = jnp.where(final == chip % 32 * 4, last, pltpu.roll(last, 64, 1))
        here = (lane >= first) & (lane < first + EARLY)
        out[pl.ds(at, CHIPS), :] = jnp.where(here, early, last)

    def work(mixed, swap):
        unfold_late(other_lines, other_late)
        key_lanes[...] = keys_of(other_lines)
        mine, theirs = {}, {}
        for h in range(2):
            rows = pl.ds(halves[h][0] * TILE, len(halves[h]) * TILE)
            some = halves[1 - h if swap else h]
            for j in some:
                row = key_rows[rows, :]
                top = None if j == some[0] else best[rows, :]
                score = scores_of(tiles(lines, late, halves[h]), tile(other_lines, other_late, j))
                for c in range(TILE // 128):
                    lanes = pl.ds(j * TILE + c * 128, 128)
                    col = key_lanes[:, lanes]
                    part = score[:, c * 128 : (c + 1) * 128]
                    earlier = col < row
                    if mixed:
                        same = is_odd(col) == is_odd(row)
                        above = jnp.where(earlier & same, part, -1.0)
                        below = jnp.where((row < col) & same, part, -1.0)
                    else:
                        above = jnp.where(earlier, part, -1.0)
                        below = jnp.where(earlier, -1.0, part)
                    top = above if top is None else jnp.maximum(top, above)
                    theirs[j * 2 + c] = jnp.max(highest(below), axis=0, keepdims=True)
                best[rows, :] = top
            for c in range(len(halves[h]) * TILE // 128):
                at = halves[h][0] * 2 + c
                eight = highest(jnp.transpose(best[pl.ds(at * 128, 128), :]))
                eight = jnp.maximum(eight, start[:, pl.ds(at * 128, 128)])
                mine[at] = jnp.max(eight, axis=0, keepdims=True)
        order = range(HELD // 128)
        answer(CHIPS if swap else 0, [mine[c] for c in order])
        answer(0 if swap else CHIPS, [theirs[c] for c in order])

    mixed = shared[...][0, 0] > 0.5
    for swap in (False, True):
        here = core == (1 if swap else 0)
        pl.when(here & mixed)(lambda swap=swap: work(True, swap))
        pl.when(here & ~mixed)(lambda swap=swap: work(False, swap))


def merge_kernel(answers, slot_key, row_key, extra, out):
    keys = row_key[...]
    chip = chip_index()
    answer = jnp.maximum(answers[pl.ds(0, CHIPS), :], answers[pl.ds(CHIPS, CHIPS), :])
    first, last = lanes_of(chip)
    early = pltpu.roll(answer, 128 - first, 1)
    late = pltpu.roll(answer, 128 - last, 1)
    half = jnp.floor((keys + 0.5) * 0.125) * 8.0
    seat = keys - half
    best = jnp.full((CHIPS, LOCAL), -1.0, jnp.float32)
    for a in range(4):
        value = None
        for k in range(PART):
            t = PART * a + k
            column = early[:, t : t + 1] if t < EARLY else late[:, t - EARLY : t - EARLY + 1]
            value = column if value is None else jnp.where(seat == float(k), column, value)
        slot = slot_key[pl.ds(a * CHIPS, CHIPS), :]
        slot = jnp.concatenate([slot] * (LOCAL // 128), axis=1)
        best = jnp.maximum(best, jnp.where(slot == half, value, -1.0))
    out[...] = jnp.maximum(jnp.max(best, axis=0, keepdims=True), extra[...])


VMEM = pl.BlockSpec(memory_space=pltpu.VMEM)
SMEM = pl.BlockSpec(memory_space=pltpu.SMEM)
LIMIT = 16 * 1024 * 1024


def pack(sizes, first_unit, emb, cluster, rank):
    later = first_unit is not None

    def kernel(*refs):
        if later:
            pack_kernel(refs[0][0], *refs[1:])
        else:
            pack_kernel(0, *refs)

    return pl.pallas_call(
        kernel,
        out_shape=(
            jax.ShapeDtypeStruct((CHIPS, LINES, 128), jnp.bfloat16),
            jax.ShapeDtypeStruct((1, LOCAL), jnp.float32),
            jax.ShapeDtypeStruct((4 * CHIPS, 128), jnp.float32),
            jax.ShapeDtypeStruct((1, 128), jnp.int32),
            jax.ShapeDtypeStruct((8, 128), jnp.float32),
            jax.ShapeDtypeStruct((1, LOCAL), jnp.float32),
        ),
        in_specs=[SMEM] * later + [VMEM, VMEM, VMEM, VMEM],
        out_specs=(VMEM,) * 6,
        scratch_shapes=[pltpu.VMEM((LOCAL, WIDTH), jnp.bfloat16)],
        compiler_params=pltpu.CompilerParams(vmem_limit_bytes=LIMIT),
        cost_estimate=pl.CostEstimate(
            flops=2 * CHIPS * 24 * LOCAL * 640, bytes_accessed=2**21, transcendentals=0
        ),
        name="pack_later" if later else "pack",
    )(*((first_unit,) if later else ()), sizes, emb, cluster, rank)


def own_best(lines, shared):
    return pl.pallas_call(
        own_kernel,
        out_shape=(
            jax.ShapeDtypeStruct((8, HELD), jnp.float32),
            jax.ShapeDtypeStruct((HELD, 128), jnp.float32),
            jax.ShapeDtypeStruct((TILE, WIDTH), jnp.bfloat16),
        ),
        in_specs=[VMEM] * 2,
        out_specs=(VMEM,) * 3,
        scratch_shapes=[pltpu.VMEM((1, HELD), jnp.float32)],
        compiler_params=pltpu.CompilerParams(vmem_limit_bytes=LIMIT),
        cost_estimate=pl.CostEstimate(
            flops=2 * HELD * HELD * WIDTH, bytes_accessed=2**21, transcendentals=0
        ),
        name="own_best",
    )(lines, shared)


def cross_best(lines, other, shared):
    start, key_rows, late = own_best(lines, shared)
    return pl.pallas_call(
        cross_kernel,
        out_shape=jax.ShapeDtypeStruct((2 * CHIPS, 128), jnp.float32),
        in_specs=[VMEM] * 6,
        out_specs=VMEM,
        scratch_shapes=[
            pltpu.VMEM((TILE, WIDTH), jnp.bfloat16),
            pltpu.VMEM((1, HELD), jnp.float32),
            pltpu.VMEM((HELD, 128), jnp.float32),
        ],
        compiler_params=pltpu.CompilerParams(vmem_limit_bytes=LIMIT),
        cost_estimate=pl.CostEstimate(
            flops=HELD * HELD * WIDTH, bytes_accessed=2**21, transcendentals=0
        ),
        name="cross_best",
    )(lines, late, start, key_rows, other, shared)


def merge(answers, slot_key, row_key, extra):
    return pl.pallas_call(
        merge_kernel,
        out_shape=jax.ShapeDtypeStruct((1, LOCAL), jnp.float32),
        in_specs=[VMEM] * 4,
        out_specs=VMEM,
        compiler_params=pltpu.CompilerParams(vmem_limit_bytes=16 * 1024 * 1024),
        name="merge",
    )(answers, slot_key, row_key, extra)


def exchange(values, axes):
    return lax.all_to_all(values, axes, split_axis=0, concat_axis=0, tiled=True)


def answers_of(sent, shared):
    lines = exchange(sent, ("x", "y", "z"))
    other = lax.ppermute(lines, "core", [(0, 1), (1, 0)])
    return exchange(cross_best(lines, other, shared), ("core", "x", "y", "z"))


def body(embeddings, cluster_sizes, cluster_of, rank_in):
    sizes = cluster_sizes.reshape(1, 2 * GROUPS)
    cluster = cluster_of.reshape(1, LOCAL)
    rank = rank_in.reshape(1, LOCAL)
    sent, row_key, slot_key, total, shared, none = pack(sizes, None, embeddings, cluster, rank)

    def more(carry):
        return carry[0] < total[0, 0]

    def again(carry):
        unit, best = carry
        sent, row_key, slot_key, _, _, _ = pack(sizes, unit.reshape(1), embeddings, cluster, rank)
        return unit + CHIPS, merge(answers_of(sent, shared), slot_key, row_key, best)

    def rounds():
        return lax.while_loop(more, again, (jnp.int32(CHIPS), none))[1]

    extra = lax.cond(total[0, 0] > CHIPS, rounds, lambda: none)
    return merge(answers_of(sent, shared), slot_key, row_key, extra).reshape(LOCAL)


def solution(mesh):
    chips = Mesh(mesh.devices.reshape(4, 4, 4, 2), ("x", "y", "z", "core"))
    every = ("x", "y", "z", "core")
    in_specs = (P(every, None), P(), P(every), P(every))
    return jax.shard_map(
        body, mesh=chips, in_specs=in_specs, out_specs=P(every), check_vma=False
    )
```

```python
import itertools

import jax
import jax.numpy as jnp
from jax import lax
from jax.experimental import pallas as pl
from jax.experimental.pallas import tpu as pltpu
from jax.sharding import Mesh
from jax.sharding import PartitionSpec as P

SLOTS = 1280
GROUPS = 16
BLOCKS = 8
WIDTH = 512
LOCAL = 512
CHIPS = 64
DATA = 20
EARLY = 16
PART = 5
HELD = CHIPS * DATA
TILE = 256
TILES = HELD // TILE
LATE_AT = 4 * EARLY
TAGS_AT = LATE_AT + 16
LINES = TAGS_AT + 8
ODD = 16384
EMPTY = 1048576.0

COVERS = {
    1: ((0, 1, 0, 1),),
    2: ((0, 1, 2, 3),),
    3: ((0, 1, 4, 5), (1, 2, 3, 5), (0, 2, 3, 4)),
    4: ((1, 3, 6, 7), (1, 4, 5, 7), (0, 3, 4, 6), (0, 2, 3, 5), (0, 1, 2, 7), (2, 4, 5, 6)),
    5: (
        (3, 4, 6, 8), (3, 5, 8, 9), (2, 5, 6, 9), (1, 2, 3, 8), (0, 1, 6, 7),
        (1, 4, 5, 9), (0, 2, 4, 7), (0, 7, 8, 9), (0, 3, 5, 7),
    ),
    6: (
        (4, 5, 8, 10), (3, 6, 8, 11), (0, 4, 7, 11), (0, 1, 6, 10), (1, 7, 8, 9),
        (3, 5, 7, 10), (1, 3, 4, 9), (0, 5, 6, 9), (2, 9, 10, 11), (0, 2, 3, 8),
        (1, 2, 5, 11), (2, 4, 6, 7),
    ),
    7: (
        (0, 1, 5, 13), (3, 5, 8, 10), (0, 7, 10, 11), (2, 11, 12, 13), (2, 7, 8, 11),
        (1, 4, 10, 12), (8, 9, 12, 13), (1, 3, 4, 7), (4, 7, 9, 13), (3, 6, 10, 13),
        (0, 1, 2, 8), (0, 4, 6, 8), (2, 4, 5, 11), (0, 3, 9, 12), (5, 6, 7, 12),
        (2, 5, 9, 10), (1, 6, 9, 11), (2, 3, 6, 11),
    ),
}


def affine_plane():
    times = ((0, 0, 0, 0), (0, 1, 2, 3), (0, 2, 3, 1), (0, 3, 1, 2))
    lines = [tuple(4 * x + y for y in range(4)) for x in range(4)]
    for slope in range(4):
        for shift in range(4):
            lines.append(tuple(4 * x + (times[slope][x] ^ shift) for x in range(4)))
    return tuple(lines)


COVERS[8] = affine_plane()
for _m, _units in COVERS.items():
    _met = {frozenset(p) for unit in _units for p in itertools.combinations(unit, 2)}
    assert all(frozenset(p) in _met for p in itertools.combinations(range(2 * _m), 2))


def covers_by_lane():
    lane = lax.broadcasted_iota(jnp.int32, (8, 128), 1)
    packed = jnp.zeros((8, 128), jnp.int32)
    at = 0
    for m in range(1, BLOCKS + 1):
        for unit in COVERS[m]:
            value = sum(point << (4 * k) for k, point in enumerate(unit))
            packed = packed + jnp.where(lane == at, value, 0)
            at += 1
    assert at <= 128
    return packed


def by_blocks(m, values):
    picked = jnp.zeros_like(m)
    for k in range(1, BLOCKS + 1):
        picked = jnp.where(m == k, float(values[k]), picked)
    return picked


def full_blocks(places):
    return jnp.floor((places + 0.5) * (1.0 / SLOTS))


def plan(row, first_unit):
    clusters = 2 * GROUPS
    down = lax.broadcasted_iota(jnp.int32, (clusters, clusters), 0)
    across = lax.broadcasted_iota(jnp.int32, (clusters, clusters), 1)
    row = jnp.broadcast_to(row, (clusters, clusters))

    def column(mask):
        picked = jnp.sum(jnp.where(mask, row, 0.0), axis=1, keepdims=True)
        return jnp.broadcast_to(picked, (clusters, 128))

    size = column(down == across)
    partner = column(down == across + 1 - 2 * (across % 2))
    index = lax.broadcasted_iota(jnp.int32, (clusters, 128), 0)
    odd = index % 2 == 1
    first = jnp.where(odd, partner, size)
    blocks_a = full_blocks(first + (SLOTS - 1))
    start_b = full_blocks(first)
    blocks_b = full_blocks(size + partner + (SLOTS - 1)) - start_b
    blocks = jnp.where(odd, blocks_b, blocks_a)
    begin = jnp.where(odd, start_b, 0.0)
    counts = [0] + [len(COVERS[m]) for m in range(1, BLOCKS + 1)]
    alone = by_blocks(blocks, counts)
    held = (blocks == 1.0) & (blocks_a > start_b) & (odd | (blocks_b >= 2.0))
    shared = jnp.where(jnp.sum(alone, axis=0, keepdims=True) <= CHIPS, 0.0, 1.0)
    count = alone * (1.0 - shared * jnp.where(held, 1.0, 0.0))
    total = jnp.sum(count, axis=0, keepdims=True)
    start = jnp.dot(
        jnp.where(across < down, 1.0, 0.0).astype(jnp.bfloat16),
        count.astype(jnp.bfloat16),
        preferred_element_type=jnp.float32,
    )
    unit = (lax.broadcasted_iota(jnp.int32, (1, 128), 1) + first_unit).astype(jnp.float32)
    mine = (unit >= start) & (unit < start + count)

    def of_unit(values):
        return jnp.sum(jnp.where(mine, values, 0.0), axis=0, keepdims=True)

    bases = [0] + [sum(counts[:m]) for m in range(1, BLOCKS + 1)]
    entry = of_unit(by_blocks(blocks, bases) - start) + unit
    group = (index // 2).astype(jnp.float32)
    kind = 2.0 * shared + (1.0 - shared) * jnp.where(odd, 1.0, 0.0)
    half = of_unit(group * (2 * BLOCKS) + 2.0 * begin + 256.0 * kind)
    used = of_unit(jnp.where(blocks == 1.0, 1.0, 2.0))
    entry = jnp.broadcast_to(jnp.clip(entry, 0.0, 127.0).astype(jnp.int32), (8, 128))
    points = jnp.take_along_axis(covers_by_lane(), entry, axis=1)[0:1, :]
    diagonal = lax.broadcasted_iota(jnp.int32, (CHIPS, 128), 0) == lax.broadcasted_iota(
        jnp.int32, (CHIPS, 128), 1
    )
    table = []
    for a in range(4):
        point = ((points >> (4 * a)) & 15).astype(jnp.float32)
        held_by = jnp.where(used > (a // 2) + 0.5, half + point, 1024.0)
        held_by = jnp.sum(jnp.where(diagonal, held_by, 0.0), axis=1, keepdims=True)
        table.append(jnp.broadcast_to(held_by, (CHIPS, 128)))
    return table, size, jnp.where(odd, partner, 0.0), shared, total


def chip_index():
    return (lax.axis_index("x") * 4 + lax.axis_index("y")) * 4 + lax.axis_index("z")


def pack_kernel(
    first_unit, sizes, emb, cluster, rank,
    sent, row_key_out, slot_key_out, total_out, shared_out, none_out, unit,
):
    table, size, previous, shared, total = plan(sizes[...].astype(jnp.float32), first_unit)
    total_out[...] = total.astype(jnp.int32)
    shared_out[...] = jnp.broadcast_to(shared, (8, 128))
    none_out[...] = jnp.full((1, LOCAL), -1.0, jnp.float32)

    def wide(column):
        return jnp.concatenate([column] * (LOCAL // 128), axis=1)

    cluster_of = cluster[...]
    rank_in = rank[...].astype(jnp.float32)
    own = lax.broadcasted_iota(jnp.int32, (2 * GROUPS, LOCAL), 0) == cluster_of
    own_size = jnp.sum(jnp.where(own, wide(size), 0.0), axis=0, keepdims=True)
    place = rank_in + jnp.sum(jnp.where(own, wide(previous), 0.0), axis=0, keepdims=True)
    bin_of = (cluster_of // 2) * BLOCKS + full_blocks(place).astype(jnp.int32)
    bins = lax.broadcasted_iota(jnp.int32, (GROUPS * BLOCKS, LOCAL), 0)
    member = jnp.where(bins == bin_of, 1.0, 0.0)
    until = lax.broadcasted_iota(jnp.int32, (128, 256), 0) <= lax.broadcasted_iota(
        jnp.int32, (128, 256), 1
    )
    until = jnp.where(until, 1.0, 0.0).astype(jnp.bfloat16)
    passed = jnp.full((GROUPS * BLOCKS, 128), -1.0, jnp.float32)
    bucket = []
    for c in range(LOCAL // 128):
        part = member[:, c * 128 : (c + 1) * 128]
        seen = jnp.dot(part.astype(jnp.bfloat16), until, preferred_element_type=jnp.float32)
        before = passed + seen[:, :128]
        passed = passed + seen[:, 128:]
        bucket.append(jnp.sum(part * before, axis=0, keepdims=True))
    bucket = jnp.concatenate(bucket, axis=1)
    upper = jnp.floor((bucket + 0.5) * 0.5)
    odd = cluster_of % 2
    kind = wide(shared)
    kind = 2.0 * kind + (1.0 - kind) * odd.astype(jnp.float32)
    half_key = bin_of.astype(jnp.float32) * 2.0 + (bucket - 2.0 * upper) + 256.0 * kind
    row_key = half_key * 8.0 + upper
    row_key_out[...] = jnp.where(rank_in < own_size, row_key, -7.0)

    high = jnp.floor((rank_in + 0.5) * (1.0 / 128))
    low = rank_in - 128.0 * high
    high = high + 1.0 + (odd * (ODD // 128)).astype(jnp.float32)
    down = lax.broadcasted_iota(jnp.int32, (128, LOCAL), 0)
    parts = jnp.where(down >= 64, low, high)
    seat = (down % 64).astype(jnp.float32)
    holds, tags = [], []
    for a in range(4):
        holds.append(jnp.where(wide(table[a]) == half_key, 1.0, 0.0).astype(jnp.bfloat16))
        here = seat == upper + float(PART * a)
        tags.append(jnp.where(here, parts, 0.0).astype(jnp.bfloat16))
    tag = lax.dot_general(
        jnp.concatenate(holds, axis=1),
        jnp.concatenate(tags, axis=1),
        (((1,), (1,)), ((), ())),
        preferred_element_type=jnp.float32,
    )
    chip = chip_index()
    lane = lax.broadcasted_iota(jnp.int32, (CHIPS, 128), 1)
    row = lax.broadcasted_iota(jnp.int32, (CHIPS, 8, 128), 1)
    lines = jnp.zeros((CHIPS, 8, 128), jnp.float32)
    moves = (
        (0, EARLY, chip % 8 * EARLY),
        (64, EARLY, chip % 8 * EARLY),
        (EARLY, 4, chip % 32 * 4),
        (64 + EARLY, 4, chip % 32 * 4),
    )
    for k, (first, count, to) in enumerate(moves):
        part = jnp.where((lane >= first) & (lane < first + count), tag, 0.0)
        part = pltpu.roll(part, (to + 128 - first) % 128, 1).reshape(CHIPS, 1, 128)
        lines = jnp.where(row == k, jnp.broadcast_to(part, (CHIPS, 8, 128)), lines)
    sent[:, pl.ds(TAGS_AT, 8), :] = lines.astype(jnp.bfloat16)

    for a in range(4):
        table[a] = table[a] * 8.0
        slot_key_out[pl.ds(a * CHIPS, CHIPS), :] = table[a]

    values = emb[...].astype(jnp.float32)
    scale = 1.0 / jnp.sqrt(jnp.sum(values * values, axis=1, keepdims=True) + 1e-06)
    unit[...] = (values * scale).astype(jnp.bfloat16)

    def picked(parts, slot):
        key = jnp.broadcast_to(parts[-1], slot.shape)
        rest = slot
        for a in range(1, 4):
            rest = rest - jnp.where(slot >= PART * a, PART, 0)
        for a in range(2, -1, -1):
            part = jnp.broadcast_to(parts[a], slot.shape)
            key = jnp.where(slot < PART * (a + 1), part, key)
        key = (key + rest.astype(jnp.float32)).reshape(slot.shape[0] * slot.shape[1], 128)
        chosen = []
        for c in range(LOCAL // 128):
            hit = key == row_key[:, c * 128 : (c + 1) * 128]
            chosen.append(jnp.where(hit, 1.0, 0.0).astype(jnp.bfloat16))
        data = jnp.dot(
            jnp.concatenate(chosen, axis=1), unit[...], preferred_element_type=jnp.float32
        )
        return [data[:, q * 128 : (q + 1) * 128].reshape(slot.shape) for q in range(4)]

    pairs = CHIPS // 2
    row = lax.broadcasted_iota(jnp.int32, (pairs, 8, 128), 1)
    last = table[3].reshape(pairs, 2, 1, 128)
    even, odd_one = (jnp.broadcast_to(last[:, k], (pairs, 8, 128)) for k in range(2))
    last = jnp.where(row < 4, even, odd_one)
    late = picked([last] * 4, EARLY + row % 4)
    moved = [pltpu.roll(part, 4, 1) for part in late]
    folded = [
        jnp.concatenate([jnp.where(row < 4, late[q], moved[q + 1]) for q in (0, 2)], axis=1),
        jnp.concatenate([jnp.where(row < 4, moved[q], late[q + 1]) for q in (0, 2)], axis=1),
    ]
    folded = jnp.stack(folded, axis=1).reshape(CHIPS, 16, 128)
    sent[:, pl.ds(LATE_AT, 16), :] = folded.astype(jnp.bfloat16)

    some = 16
    slot = lax.broadcasted_iota(jnp.int32, (some, EARLY, 128), 1)
    for k in range(CHIPS // some):
        chips = pl.ds(k * some, some)
        parts = [part[k * some : (k + 1) * some, :].reshape(some, 1, 128) for part in table]
        quarters = picked(parts, slot)
        for q in range(4):
            sent[chips, pl.ds(q * EARLY, EARLY), :] = quarters[q].astype(jnp.bfloat16)


def unfold_late(lines, late):
    part = lines[:, pl.ds(LATE_AT, 16), :].astype(jnp.float32).reshape(CHIPS // 2, 2, 16, 128)
    low_rows = lax.broadcasted_iota(jnp.int32, (CHIPS // 2, 8, 128), 1) < 4
    for q in (0, 2):
        even, odd = part[:, 0, q * 4 : q * 4 + 8], part[:, 1, q * 4 : q * 4 + 8]
        quarters = (
            jnp.where(low_rows, even, pltpu.roll(odd, 4, 1)),
            jnp.where(low_rows, pltpu.roll(even, 4, 1), odd),
        )
        for k in range(2):
            late[:, pl.ds((q + k) * 128, 128)] = (
                quarters[k].reshape(CHIPS * 4, 128).astype(jnp.bfloat16)
            )


def tile(lines, late, n):
    if n == TILES - 1:
        return late[...]
    sources = pl.ds(n * (TILE // EARLY), TILE // EARLY)
    quarters = [lines[sources, pl.ds(q * EARLY, EARLY), :] for q in range(4)]
    return jnp.concatenate([part.reshape(TILE, 128) for part in quarters], axis=1)


def tiles(lines, late, some):
    return jnp.concatenate([tile(lines, late, n) for n in some], axis=0)


def keys_of(lines):
    tags = lines[:, pl.ds(TAGS_AT, 8), :].astype(jnp.float32)
    row = lax.broadcasted_iota(jnp.int32, (8, 128), 0)
    first = jnp.where(row == 0, 128.0, 0.0) + jnp.where(row == 1, 1.0, 0.0)
    last = jnp.where(row == 2, 128.0, 0.0) + jnp.where(row == 3, 1.0, 0.0)
    eights = [jnp.sum(tags[c * 8 : (c + 1) * 8], axis=0) for c in range(CHIPS // 8)]
    early = [eight * first for eight in eights]
    late = [sum(eights[c * 4 : (c + 1) * 4]) * last for c in range(CHIPS // 32)]
    key = jnp.concatenate([jnp.sum(k, axis=0, keepdims=True) for k in early + late], axis=1)
    return jnp.where(key == 0.0, EMPTY, key)


def scores_of(rows, columns):
    return lax.dot_general(
        rows, columns, (((1,), (1,)), ((), ())), preferred_element_type=jnp.float32
    )


def is_odd(key):
    return jnp.where(key >= ODD, 1.0, 0.0)


def highest(part):
    return jnp.max(part.reshape(part.shape[0] // 8, 8, 128), axis=0)


def lanes_of(chip):
    first = chip % 8 * EARLY
    last = chip % 32 * 4
    meet = (last > first - 4) & (last < first + EARLY)
    return first, jnp.where(meet, (last + 64) % 128, last)


def own_kernel(lines, shared, best, key_rows, late, key_lanes):
    def work(mixed):
        unfold_late(lines, late)
        key_lanes[...] = keys_of(lines)
        for c in range(HELD // 128):
            chunk = pl.ds(c * 128, 128)
            key_rows[chunk, :] = jnp.transpose(jnp.broadcast_to(key_lanes[:, chunk], (128, 128)))
        for j in range(TILES):
            score = scores_of(tiles(lines, late, range(TILES)), tile(lines, late, j))
            row = key_rows[...]
            for c in range(TILE // 128):
                lanes = pl.ds(j * TILE + c * 128, 128)
                col = key_lanes[:, lanes]
                earlier = row < col
                if mixed:
                    earlier = earlier & (is_odd(col) == is_odd(row))
                part = score[:, c * 128 : (c + 1) * 128]
                best[:, lanes] = highest(jnp.where(earlier, part, -1.0))

    mixed = shared[...][0, 0] > 0.5
    pl.when(mixed)(lambda: work(True))
    pl.when(~mixed)(lambda: work(False))


def cross_kernel(
    lines, late, start, key_rows, other_lines, shared, out, other_late, key_lanes
):
    core = lax.axis_index("core")
    halves = ((0, 1, 2), (3, 4))

    def answer(at, chunks):
        rows = [jnp.broadcast_to(chunk, (8, 128)) for chunk in chunks[:-2]]
        early = jnp.concatenate(rows, axis=0)
        last = jnp.concatenate([jnp.broadcast_to(c, (32, 128)) for c in chunks[-2:]], axis=0)
        chip = lax.broadcasted_iota(jnp.int32, (CHIPS, 128), 0)
        lane = lax.broadcasted_iota(jnp.int32, (CHIPS, 128), 1)
        first, final = lanes_of(chip)
        last = jnp.where(final == chip % 32 * 4, last, pltpu.roll(last, 64, 1))
        here = (lane >= first) & (lane < first + EARLY)
        out[pl.ds(at, CHIPS), :] = jnp.where(here, early, last)

    def work(mixed, swap):
        unfold_late(other_lines, other_late)
        key_lanes[...] = keys_of(other_lines)
        mine, theirs = {}, {}
        for h in range(2):
            some = halves[1 - h if swap else h]
            for n in halves[h]:
                row = key_rows[pl.ds(n * TILE, TILE), :]
                top = None
                scores = scores_of(tile(lines, late, n), tiles(other_lines, other_late, some))
                for c in range(len(some) * TILE // 128):
                    at = some[0] * 2 + c
                    col = key_lanes[:, pl.ds(at * 128, 128)]
                    part = scores[:, c * 128 : (c + 1) * 128]
                    earlier = col < row
                    if mixed:
                        same = is_odd(col) == is_odd(row)
                        above = jnp.where(earlier & same, part, -1.0)
                        below = jnp.where((row < col) & same, part, -1.0)
                    else:
                        above = jnp.where(earlier, part, -1.0)
                        below = jnp.where(earlier, -1.0, part)
                    top = above if top is None else jnp.maximum(top, above)
                    low = highest(below)
                    theirs[at] = low if at not in theirs else jnp.maximum(theirs[at], low)
                for c in range(TILE // 128):
                    at = n * 2 + c
                    eight = highest(jnp.transpose(top[c * 128 : (c + 1) * 128, :]))
                    eight = jnp.maximum(eight, start[:, pl.ds(at * 128, 128)])
                    mine[at] = jnp.max(eight, axis=0, keepdims=True)
            for c in some:
                for k in (2 * c, 2 * c + 1):
                    theirs[k] = jnp.max(theirs[k], axis=0, keepdims=True)
        order = range(HELD // 128)
        answer(CHIPS if swap else 0, [mine[c] for c in order])
        answer(0 if swap else CHIPS, [theirs[c] for c in order])

    mixed = shared[...][0, 0] > 0.5
    for swap in (False, True):
        here = core == (1 if swap else 0)
        pl.when(here & mixed)(lambda swap=swap: work(True, swap))
        pl.when(here & ~mixed)(lambda swap=swap: work(False, swap))


def merge_kernel(answers, slot_key, row_key, extra, out):
    keys = row_key[...]
    chip = chip_index()
    answer = jnp.maximum(answers[pl.ds(0, CHIPS), :], answers[pl.ds(CHIPS, CHIPS), :])
    first, last = lanes_of(chip)
    early = pltpu.roll(answer, 128 - first, 1)
    late = pltpu.roll(answer, 128 - last, 1)
    half = jnp.floor((keys + 0.5) * 0.125) * 8.0
    seat = keys - half
    best = jnp.full((CHIPS, LOCAL), -1.0, jnp.float32)
    for a in range(4):
        value = None
        for k in range(PART):
            t = PART * a + k
            column = early[:, t : t + 1] if t < EARLY else late[:, t - EARLY : t - EARLY + 1]
            value = column if value is None else jnp.where(seat == float(k), column, value)
        slot = slot_key[pl.ds(a * CHIPS, CHIPS), :]
        slot = jnp.concatenate([slot] * (LOCAL // 128), axis=1)
        best = jnp.maximum(best, jnp.where(slot == half, value, -1.0))
    out[...] = jnp.maximum(jnp.max(best, axis=0, keepdims=True), extra[...])


VMEM = pl.BlockSpec(memory_space=pltpu.VMEM)
SMEM = pl.BlockSpec(memory_space=pltpu.SMEM)
LIMIT = 16 * 1024 * 1024


def pack(sizes, first_unit, emb, cluster, rank):
    later = first_unit is not None

    def kernel(*refs):
        if later:
            pack_kernel(refs[0][0], *refs[1:])
        else:
            pack_kernel(0, *refs)

    return pl.pallas_call(
        kernel,
        out_shape=(
            jax.ShapeDtypeStruct((CHIPS, LINES, 128), jnp.bfloat16),
            jax.ShapeDtypeStruct((1, LOCAL), jnp.float32),
            jax.ShapeDtypeStruct((4 * CHIPS, 128), jnp.float32),
            jax.ShapeDtypeStruct((1, 128), jnp.int32),
            jax.ShapeDtypeStruct((8, 128), jnp.float32),
            jax.ShapeDtypeStruct((1, LOCAL), jnp.float32),
        ),
        in_specs=[SMEM] * later + [VMEM, VMEM, VMEM, VMEM],
        out_specs=(VMEM,) * 6,
        scratch_shapes=[pltpu.VMEM((LOCAL, WIDTH), jnp.bfloat16)],
        compiler_params=pltpu.CompilerParams(vmem_limit_bytes=LIMIT),
        cost_estimate=pl.CostEstimate(
            flops=2 * CHIPS * 24 * LOCAL * 640, bytes_accessed=2**21, transcendentals=0
        ),
        name="pack_later" if later else "pack",
    )(*((first_unit,) if later else ()), sizes, emb, cluster, rank)


def own_best(lines, shared):
    return pl.pallas_call(
        own_kernel,
        out_shape=(
            jax.ShapeDtypeStruct((8, HELD), jnp.float32),
            jax.ShapeDtypeStruct((HELD, 128), jnp.float32),
            jax.ShapeDtypeStruct((TILE, WIDTH), jnp.bfloat16),
        ),
        in_specs=[VMEM] * 2,
        out_specs=(VMEM,) * 3,
        scratch_shapes=[pltpu.VMEM((1, HELD), jnp.float32)],
        compiler_params=pltpu.CompilerParams(vmem_limit_bytes=LIMIT),
        cost_estimate=pl.CostEstimate(
            flops=2 * HELD * HELD * WIDTH, bytes_accessed=2**21, transcendentals=0
        ),
        name="own_best",
    )(lines, shared)


def cross_best(lines, other, shared):
    start, key_rows, late = own_best(lines, shared)
    return pl.pallas_call(
        cross_kernel,
        out_shape=jax.ShapeDtypeStruct((2 * CHIPS, 128), jnp.float32),
        in_specs=[VMEM] * 6,
        out_specs=VMEM,
        scratch_shapes=[
            pltpu.VMEM((TILE, WIDTH), jnp.bfloat16),
            pltpu.VMEM((1, HELD), jnp.float32),
        ],
        compiler_params=pltpu.CompilerParams(vmem_limit_bytes=LIMIT),
        cost_estimate=pl.CostEstimate(
            flops=HELD * HELD * WIDTH, bytes_accessed=2**21, transcendentals=0
        ),
        name="cross_best",
    )(lines, late, start, key_rows, other, shared)


def merge(answers, slot_key, row_key, extra):
    return pl.pallas_call(
        merge_kernel,
        out_shape=jax.ShapeDtypeStruct((1, LOCAL), jnp.float32),
        in_specs=[VMEM] * 4,
        out_specs=VMEM,
        compiler_params=pltpu.CompilerParams(vmem_limit_bytes=16 * 1024 * 1024),
        name="merge",
    )(answers, slot_key, row_key, extra)


def exchange(values, axes):
    return lax.all_to_all(values, axes, split_axis=0, concat_axis=0, tiled=True)


def answers_of(sent, shared):
    lines = exchange(sent, ("x", "y", "z"))
    other = lax.ppermute(lines, "core", [(0, 1), (1, 0)])
    return exchange(cross_best(lines, other, shared), ("core", "x", "y", "z"))


def body(embeddings, cluster_sizes, cluster_of, rank_in):
    sizes = cluster_sizes.reshape(1, 2 * GROUPS)
    cluster = cluster_of.reshape(1, LOCAL)
    rank = rank_in.reshape(1, LOCAL)
    sent, row_key, slot_key, total, shared, none = pack(sizes, None, embeddings, cluster, rank)

    def more(carry):
        return carry[0] < total[0, 0]

    def again(carry):
        unit, best = carry
        sent, row_key, slot_key, _, _, _ = pack(sizes, unit.reshape(1), embeddings, cluster, rank)
        return unit + CHIPS, merge(answers_of(sent, shared), slot_key, row_key, best)

    def rounds():
        return lax.while_loop(more, again, (jnp.int32(CHIPS), none))[1]

    extra = lax.cond(total[0, 0] > CHIPS, rounds, lambda: none)
    return merge(answers_of(sent, shared), slot_key, row_key, extra).reshape(LOCAL)


def solution(mesh):
    chips = Mesh(mesh.devices.reshape(4, 4, 4, 2), ("x", "y", "z", "core"))
    every = ("x", "y", "z", "core")
    in_specs = (P(every, None), P(), P(every), P(every))
    return jax.shard_map(
        body, mesh=chips, in_specs=in_specs, out_specs=P(every), check_vma=False
    )
```

```python
import itertools

import jax
import jax.numpy as jnp
from jax import lax
from jax.experimental import pallas as pl
from jax.experimental.pallas import tpu as pltpu
from jax.sharding import Mesh
from jax.sharding import PartitionSpec as P

SLOTS = 1280
GROUPS = 16
BLOCKS = 8
WIDTH = 512
LOCAL = 512
CHIPS = 64
DATA = 20
EARLY = 16
PART = 5
HELD = CHIPS * DATA
TILE = 256
TILES = HELD // TILE
LATE_AT = 4 * EARLY
TAGS_AT = LATE_AT + 16
LINES = TAGS_AT + 8
ODD = 16384
EMPTY = 1048576.0

COVERS = {
    1: ((0, 1, 0, 1),),
    2: ((0, 1, 2, 3),),
    3: ((0, 1, 4, 5), (1, 2, 3, 5), (0, 2, 3, 4)),
    4: ((1, 3, 6, 7), (1, 4, 5, 7), (0, 3, 4, 6), (0, 2, 3, 5), (0, 1, 2, 7), (2, 4, 5, 6)),
    5: (
        (3, 4, 6, 8), (3, 5, 8, 9), (2, 5, 6, 9), (1, 2, 3, 8), (0, 1, 6, 7),
        (1, 4, 5, 9), (0, 2, 4, 7), (0, 7, 8, 9), (0, 3, 5, 7),
    ),
    6: (
        (4, 5, 8, 10), (3, 6, 8, 11), (0, 4, 7, 11), (0, 1, 6, 10), (1, 7, 8, 9),
        (3, 5, 7, 10), (1, 3, 4, 9), (0, 5, 6, 9), (2, 9, 10, 11), (0, 2, 3, 8),
        (1, 2, 5, 11), (2, 4, 6, 7),
    ),
    7: (
        (0, 1, 5, 13), (3, 5, 8, 10), (0, 7, 10, 11), (2, 11, 12, 13), (2, 7, 8, 11),
        (1, 4, 10, 12), (8, 9, 12, 13), (1, 3, 4, 7), (4, 7, 9, 13), (3, 6, 10, 13),
        (0, 1, 2, 8), (0, 4, 6, 8), (2, 4, 5, 11), (0, 3, 9, 12), (5, 6, 7, 12),
        (2, 5, 9, 10), (1, 6, 9, 11), (2, 3, 6, 11),
    ),
}


def affine_plane():
    times = ((0, 0, 0, 0), (0, 1, 2, 3), (0, 2, 3, 1), (0, 3, 1, 2))
    lines = [tuple(4 * x + y for y in range(4)) for x in range(4)]
    for slope in range(4):
        for shift in range(4):
            lines.append(tuple(4 * x + (times[slope][x] ^ shift) for x in range(4)))
    return tuple(lines)


COVERS[8] = affine_plane()
for _m, _units in COVERS.items():
    _met = {frozenset(p) for unit in _units for p in itertools.combinations(unit, 2)}
    assert all(frozenset(p) in _met for p in itertools.combinations(range(2 * _m), 2))


def covers_by_lane():
    lane = lax.broadcasted_iota(jnp.int32, (8, 128), 1)
    packed = jnp.zeros((8, 128), jnp.int32)
    at = 0
    for m in range(1, BLOCKS + 1):
        for unit in COVERS[m]:
            value = sum(point << (4 * k) for k, point in enumerate(unit))
            packed = packed + jnp.where(lane == at, value, 0)
            at += 1
    assert at <= 128
    return packed


def by_blocks(m, values):
    picked = jnp.zeros_like(m)
    for k in range(1, BLOCKS + 1):
        picked = jnp.where(m == k, float(values[k]), picked)
    return picked


def full_blocks(places):
    return jnp.floor((places + 0.5) * (1.0 / SLOTS))


def plan(row, first_unit):
    clusters = 2 * GROUPS
    down = lax.broadcasted_iota(jnp.int32, (clusters, clusters), 0)
    across = lax.broadcasted_iota(jnp.int32, (clusters, clusters), 1)
    row = jnp.broadcast_to(row, (clusters, clusters))

    def column(mask):
        picked = jnp.sum(jnp.where(mask, row, 0.0), axis=1, keepdims=True)
        return jnp.broadcast_to(picked, (clusters, 128))

    size = column(down == across)
    partner = column(down == across + 1 - 2 * (across % 2))
    index = lax.broadcasted_iota(jnp.int32, (clusters, 128), 0)
    odd = index % 2 == 1
    first = jnp.where(odd, partner, size)
    blocks_a = full_blocks(first + (SLOTS - 1))
    start_b = full_blocks(first)
    blocks_b = full_blocks(size + partner + (SLOTS - 1)) - start_b
    blocks = jnp.where(odd, blocks_b, blocks_a)
    begin = jnp.where(odd, start_b, 0.0)
    counts = [0] + [len(COVERS[m]) for m in range(1, BLOCKS + 1)]
    alone = by_blocks(blocks, counts)
    held = (blocks == 1.0) & (blocks_a > start_b) & (odd | (blocks_b >= 2.0))
    shared = jnp.where(jnp.sum(alone, axis=0, keepdims=True) <= CHIPS, 0.0, 1.0)
    count = alone * (1.0 - shared * jnp.where(held, 1.0, 0.0))
    total = jnp.sum(count, axis=0, keepdims=True)
    start = jnp.dot(
        jnp.where(across < down, 1.0, 0.0).astype(jnp.bfloat16),
        count.astype(jnp.bfloat16),
        preferred_element_type=jnp.float32,
    )
    unit = (lax.broadcasted_iota(jnp.int32, (1, 128), 1) + first_unit).astype(jnp.float32)
    mine = (unit >= start) & (unit < start + count)

    def of_unit(values):
        return jnp.sum(jnp.where(mine, values, 0.0), axis=0, keepdims=True)

    bases = [0] + [sum(counts[:m]) for m in range(1, BLOCKS + 1)]
    entry = of_unit(by_blocks(blocks, bases) - start) + unit
    group = (index // 2).astype(jnp.float32)
    kind = 2.0 * shared + (1.0 - shared) * jnp.where(odd, 1.0, 0.0)
    half = of_unit(group * (2 * BLOCKS) + 2.0 * begin + 256.0 * kind)
    used = of_unit(jnp.where(blocks == 1.0, 1.0, 2.0))
    entry = jnp.broadcast_to(jnp.clip(entry, 0.0, 127.0).astype(jnp.int32), (8, 128))
    points = jnp.take_along_axis(covers_by_lane(), entry, axis=1)[0:1, :]
    diagonal = lax.broadcasted_iota(jnp.int32, (CHIPS, 128), 0) == lax.broadcasted_iota(
        jnp.int32, (CHIPS, 128), 1
    )
    table = []
    for a in range(4):
        point = ((points >> (4 * a)) & 15).astype(jnp.float32)
        held_by = jnp.where(used > (a // 2) + 0.5, half + point, 1024.0)
        held_by = jnp.sum(jnp.where(diagonal, held_by, 0.0), axis=1, keepdims=True)
        table.append(jnp.broadcast_to(held_by, (CHIPS, 128)))
    return table, size, jnp.where(odd, partner, 0.0), shared, total


def chip_index():
    return (lax.axis_index("x") * 4 + lax.axis_index("y")) * 4 + lax.axis_index("z")


def pack_kernel(
    first_unit, sizes, emb, cluster, rank,
    sent, row_key_out, slot_key_out, total_out, shared_out, none_out, unit,
):
    table, size, previous, shared, total = plan(sizes[...].astype(jnp.float32), first_unit)
    total_out[...] = total.astype(jnp.int32)
    shared_out[...] = jnp.broadcast_to(shared, (8, 128))
    none_out[...] = jnp.full((1, LOCAL), -1.0, jnp.float32)

    def wide(column):
        return jnp.concatenate([column] * (LOCAL // 128), axis=1)

    cluster_of = cluster[...]
    rank_in = rank[...].astype(jnp.float32)
    own = lax.broadcasted_iota(jnp.int32, (2 * GROUPS, LOCAL), 0) == cluster_of
    own_size = jnp.sum(jnp.where(own, wide(size), 0.0), axis=0, keepdims=True)
    place = rank_in + jnp.sum(jnp.where(own, wide(previous), 0.0), axis=0, keepdims=True)
    bin_of = (cluster_of // 2) * BLOCKS + full_blocks(place).astype(jnp.int32)
    bins = lax.broadcasted_iota(jnp.int32, (GROUPS * BLOCKS, LOCAL), 0)
    member = jnp.where(bins == bin_of, 1.0, 0.0)
    until = lax.broadcasted_iota(jnp.int32, (128, 256), 0) <= lax.broadcasted_iota(
        jnp.int32, (128, 256), 1
    )
    until = jnp.where(until, 1.0, 0.0).astype(jnp.bfloat16)
    passed = jnp.full((GROUPS * BLOCKS, 128), -1.0, jnp.float32)
    bucket = []
    for c in range(LOCAL // 128):
        part = member[:, c * 128 : (c + 1) * 128]
        seen = jnp.dot(part.astype(jnp.bfloat16), until, preferred_element_type=jnp.float32)
        before = passed + seen[:, :128]
        passed = passed + seen[:, 128:]
        bucket.append(jnp.sum(part * before, axis=0, keepdims=True))
    bucket = jnp.concatenate(bucket, axis=1)
    upper = jnp.floor((bucket + 0.5) * 0.5)
    odd = cluster_of % 2
    kind = wide(shared)
    kind = 2.0 * kind + (1.0 - kind) * odd.astype(jnp.float32)
    half_key = bin_of.astype(jnp.float32) * 2.0 + (bucket - 2.0 * upper) + 256.0 * kind
    row_key = half_key * 8.0 + upper
    row_key_out[...] = jnp.where(rank_in < own_size, row_key, -7.0)

    high = jnp.floor((rank_in + 0.5) * (1.0 / 128))
    low = rank_in - 128.0 * high
    high = high + 1.0 + (odd * (ODD // 128)).astype(jnp.float32)
    down = lax.broadcasted_iota(jnp.int32, (128, LOCAL), 0)
    parts = jnp.where(down >= 64, low, high)
    seat = (down % 64).astype(jnp.float32)
    holds, tags = [], []
    for a in range(4):
        holds.append(jnp.where(wide(table[a]) == half_key, 1.0, 0.0).astype(jnp.bfloat16))
        here = seat == upper + float(PART * a)
        tags.append(jnp.where(here, parts, 0.0).astype(jnp.bfloat16))
    tag = lax.dot_general(
        jnp.concatenate(holds, axis=1),
        jnp.concatenate(tags, axis=1),
        (((1,), (1,)), ((), ())),
        preferred_element_type=jnp.float32,
    )
    chip = chip_index()
    lane = lax.broadcasted_iota(jnp.int32, (CHIPS, 128), 1)
    row = lax.broadcasted_iota(jnp.int32, (CHIPS, 8, 128), 1)
    lines = jnp.zeros((CHIPS, 8, 128), jnp.float32)
    moves = (
        (0, EARLY, chip % 8 * EARLY),
        (64, EARLY, chip % 8 * EARLY),
        (EARLY, 4, chip % 32 * 4),
        (64 + EARLY, 4, chip % 32 * 4),
    )
    for k, (first, count, to) in enumerate(moves):
        part = jnp.where((lane >= first) & (lane < first + count), tag, 0.0)
        part = pltpu.roll(part, (to + 128 - first) % 128, 1).reshape(CHIPS, 1, 128)
        lines = jnp.where(row == k, jnp.broadcast_to(part, (CHIPS, 8, 128)), lines)
    sent[:, pl.ds(TAGS_AT, 8), :] = lines.astype(jnp.bfloat16)

    for a in range(4):
        table[a] = table[a] * 8.0
        slot_key_out[pl.ds(a * CHIPS, CHIPS), :] = table[a]

    values = emb[...].astype(jnp.float32)
    scale = 1.0 / jnp.sqrt(jnp.sum(values * values, axis=1, keepdims=True) + 1e-06)
    unit[...] = (values * scale).astype(jnp.bfloat16)

    row_key_16 = jnp.broadcast_to(row_key, (16, LOCAL)).astype(jnp.int32).astype(jnp.int16)
    one, zero = jnp.ones((), jnp.bfloat16), jnp.zeros((), jnp.bfloat16)

    def picked(parts, slot):
        key = jnp.broadcast_to(parts[-1], slot.shape)
        rest = slot
        for a in range(1, 4):
            rest = rest - jnp.where(slot >= PART * a, PART, 0)
        for a in range(2, -1, -1):
            part = jnp.broadcast_to(parts[a], slot.shape)
            key = jnp.where(slot < PART * (a + 1), part, key)
        key = (key + rest.astype(jnp.float32)).astype(jnp.int32).astype(jnp.int16)
        key = key.reshape(slot.shape[0] * slot.shape[1] // 16, 16, 128)
        chosen = []
        for c in range(LOCAL // 128):
            hit = key == row_key_16[:, c * 128 : (c + 1) * 128]
            chosen.append(jnp.where(hit, one, zero).reshape(key.shape[0] * 16, 128))
        data = jnp.dot(
            jnp.concatenate(chosen, axis=1), unit[...], preferred_element_type=jnp.float32
        )
        return [data[:, q * 128 : (q + 1) * 128].reshape(slot.shape) for q in range(4)]

    some = 16
    slot = lax.broadcasted_iota(jnp.int32, (some, EARLY, 128), 1)
    for k in range(CHIPS // some):
        chips = pl.ds(k * some, some)
        parts = [part[k * some : (k + 1) * some, :].reshape(some, 1, 128) for part in table]
        quarters = picked(parts, slot)
        for q in range(4):
            sent[chips, pl.ds(q * EARLY, EARLY), :] = quarters[q].astype(jnp.bfloat16)

    pairs = CHIPS // 2
    row = lax.broadcasted_iota(jnp.int32, (pairs, 8, 128), 1)
    last = table[3].reshape(pairs, 2, 1, 128)
    even, odd_one = (jnp.broadcast_to(last[:, k], (pairs, 8, 128)) for k in range(2))
    last = jnp.where(row < 4, even, odd_one)
    late = picked([last] * 4, EARLY + row % 4)
    moved = [pltpu.roll(part, 4, 1) for part in late]
    folded = [
        jnp.concatenate([jnp.where(row < 4, late[q], moved[q + 1]) for q in (0, 2)], axis=1),
        jnp.concatenate([jnp.where(row < 4, moved[q], late[q + 1]) for q in (0, 2)], axis=1),
    ]
    folded = jnp.stack(folded, axis=1).reshape(CHIPS, 16, 128)
    sent[:, pl.ds(LATE_AT, 16), :] = folded.astype(jnp.bfloat16)


def unfold_late(lines, late):
    part = lines[:, pl.ds(LATE_AT, 16), :].astype(jnp.float32).reshape(CHIPS // 2, 2, 16, 128)
    low_rows = lax.broadcasted_iota(jnp.int32, (CHIPS // 2, 8, 128), 1) < 4
    for q in (0, 2):
        even, odd = part[:, 0, q * 4 : q * 4 + 8], part[:, 1, q * 4 : q * 4 + 8]
        quarters = (
            jnp.where(low_rows, even, pltpu.roll(odd, 4, 1)),
            jnp.where(low_rows, pltpu.roll(even, 4, 1), odd),
        )
        for k in range(2):
            late[:, pl.ds((q + k) * 128, 128)] = (
                quarters[k].reshape(CHIPS * 4, 128).astype(jnp.bfloat16)
            )


def tile(lines, late, n):
    if n == TILES - 1:
        return late[...]
    sources = pl.ds(n * (TILE // EARLY), TILE // EARLY)
    quarters = [lines[sources, pl.ds(q * EARLY, EARLY), :] for q in range(4)]
    return jnp.concatenate([part.reshape(TILE, 128) for part in quarters], axis=1)


def tiles(lines, late, some):
    return jnp.concatenate([tile(lines, late, n) for n in some], axis=0)


def keys_of(lines):
    tags = lines[:, pl.ds(TAGS_AT, 8), :].astype(jnp.float32)
    row = lax.broadcasted_iota(jnp.int32, (8, 128), 0)
    first = jnp.where(row == 0, 128.0, 0.0) + jnp.where(row == 1, 1.0, 0.0)
    last = jnp.where(row == 2, 128.0, 0.0) + jnp.where(row == 3, 1.0, 0.0)
    eights = [jnp.sum(tags[c * 8 : (c + 1) * 8], axis=0) for c in range(CHIPS // 8)]
    early = [eight * first for eight in eights]
    late = [sum(eights[c * 4 : (c + 1) * 4]) * last for c in range(CHIPS // 32)]
    key = jnp.concatenate([jnp.sum(k, axis=0, keepdims=True) for k in early + late], axis=1)
    return jnp.where(key == 0.0, EMPTY, key)


def scores_of(rows, columns):
    return lax.dot_general(
        rows, columns, (((1,), (1,)), ((), ())), preferred_element_type=jnp.float32
    )


def is_odd(key):
    return jnp.where(key >= ODD, 1.0, 0.0)


def highest(part):
    return jnp.max(part.reshape(part.shape[0] // 8, 8, 128), axis=0)


def lanes_of(chip):
    first = chip % 8 * EARLY
    last = chip % 32 * 4
    meet = (last > first - 4) & (last < first + EARLY)
    return first, jnp.where(meet, (last + 64) % 128, last)


def own_kernel(lines, shared, best, key_rows, late, key_lanes):
    def work(mixed):
        unfold_late(lines, late)
        key_lanes[...] = keys_of(lines)
        for c in range(HELD // 128):
            chunk = pl.ds(c * 128, 128)
            key_rows[chunk, :] = jnp.transpose(jnp.broadcast_to(key_lanes[:, chunk], (128, 128)))
        for j in range(TILES):
            score = scores_of(tiles(lines, late, range(TILES)), tile(lines, late, j))
            row = key_rows[...]
            for c in range(TILE // 128):
                lanes = pl.ds(j * TILE + c * 128, 128)
                col = key_lanes[:, lanes]
                earlier = row < col
                if mixed:
                    earlier = earlier & (is_odd(col) == is_odd(row))
                part = score[:, c * 128 : (c + 1) * 128]
                best[:, lanes] = highest(jnp.where(earlier, part, -1.0))

    mixed = shared[...][0, 0] > 0.5
    pl.when(mixed)(lambda: work(True))
    pl.when(~mixed)(lambda: work(False))


def cross_kernel(
    lines, late, start, key_rows, other_lines, shared, out, other_late, key_lanes
):
    core = lax.axis_index("core")
    halves = ((0, 1, 2), (3, 4))

    def answer(at, chunks):
        rows = [jnp.broadcast_to(chunk, (8, 128)) for chunk in chunks[:-2]]
        early = jnp.concatenate(rows, axis=0)
        last = jnp.concatenate([jnp.broadcast_to(c, (32, 128)) for c in chunks[-2:]], axis=0)
        chip = lax.broadcasted_iota(jnp.int32, (CHIPS, 128), 0)
        lane = lax.broadcasted_iota(jnp.int32, (CHIPS, 128), 1)
        first, final = lanes_of(chip)
        last = jnp.where(final == chip % 32 * 4, last, pltpu.roll(last, 64, 1))
        here = (lane >= first) & (lane < first + EARLY)
        out[pl.ds(at, CHIPS), :] = jnp.where(here, early, last)

    def work(mixed, swap):
        unfold_late(other_lines, other_late)
        key_lanes[...] = keys_of(other_lines)
        mine, theirs = {}, {}
        for h in range(2):
            some = halves[1 - h if swap else h]
            for n in halves[h]:
                row = key_rows[pl.ds(n * TILE, TILE), :]
                top = None
                scores = scores_of(tile(lines, late, n), tiles(other_lines, other_late, some))
                for c in range(len(some) * TILE // 128):
                    at = some[0] * 2 + c
                    col = key_lanes[:, pl.ds(at * 128, 128)]
                    part = scores[:, c * 128 : (c + 1) * 128]
                    earlier = col < row
                    if mixed:
                        same = is_odd(col) == is_odd(row)
                        above = jnp.where(earlier & same, part, -1.0)
                        below = jnp.where((row < col) & same, part, -1.0)
                    else:
                        above = jnp.where(earlier, part, -1.0)
                        below = jnp.where(earlier, -1.0, part)
                    top = above if top is None else jnp.maximum(top, above)
                    low = highest(below)
                    theirs[at] = low if at not in theirs else jnp.maximum(theirs[at], low)
                for c in range(TILE // 128):
                    at = n * 2 + c
                    eight = highest(jnp.transpose(top[c * 128 : (c + 1) * 128, :]))
                    eight = jnp.maximum(eight, start[:, pl.ds(at * 128, 128)])
                    mine[at] = jnp.max(eight, axis=0, keepdims=True)
            for c in some:
                for k in (2 * c, 2 * c + 1):
                    theirs[k] = jnp.max(theirs[k], axis=0, keepdims=True)
        order = range(HELD // 128)
        answer(CHIPS if swap else 0, [mine[c] for c in order])
        answer(0 if swap else CHIPS, [theirs[c] for c in order])

    mixed = shared[...][0, 0] > 0.5
    for swap in (False, True):
        here = core == (1 if swap else 0)
        pl.when(here & mixed)(lambda swap=swap: work(True, swap))
        pl.when(here & ~mixed)(lambda swap=swap: work(False, swap))


def merge_kernel(answers, slot_key, row_key, extra, out):
    keys = row_key[...]
    chip = chip_index()
    answer = jnp.maximum(answers[pl.ds(0, CHIPS), :], answers[pl.ds(CHIPS, CHIPS), :])
    first, last = lanes_of(chip)
    early = pltpu.roll(answer, 128 - first, 1)
    late = pltpu.roll(answer, 128 - last, 1)
    half = jnp.floor((keys + 0.5) * 0.125) * 8.0
    seat = keys - half
    best = jnp.full((CHIPS, LOCAL), -1.0, jnp.float32)
    for a in range(4):
        value = None
        for k in range(PART):
            t = PART * a + k
            column = early[:, t : t + 1] if t < EARLY else late[:, t - EARLY : t - EARLY + 1]
            value = column if value is None else jnp.where(seat == float(k), column, value)
        slot = slot_key[pl.ds(a * CHIPS, CHIPS), :]
        slot = jnp.concatenate([slot] * (LOCAL // 128), axis=1)
        best = jnp.maximum(best, jnp.where(slot == half, value, -1.0))
    out[...] = jnp.maximum(jnp.max(best, axis=0, keepdims=True), extra[...])


VMEM = pl.BlockSpec(memory_space=pltpu.VMEM)
SMEM = pl.BlockSpec(memory_space=pltpu.SMEM)
LIMIT = 16 * 1024 * 1024


def pack(sizes, first_unit, emb, cluster, rank):
    later = first_unit is not None

    def kernel(*refs):
        if later:
            pack_kernel(refs[0][0], *refs[1:])
        else:
            pack_kernel(0, *refs)

    return pl.pallas_call(
        kernel,
        out_shape=(
            jax.ShapeDtypeStruct((CHIPS, LINES, 128), jnp.bfloat16),
            jax.ShapeDtypeStruct((1, LOCAL), jnp.float32),
            jax.ShapeDtypeStruct((4 * CHIPS, 128), jnp.float32),
            jax.ShapeDtypeStruct((1, 128), jnp.int32),
            jax.ShapeDtypeStruct((8, 128), jnp.float32),
            jax.ShapeDtypeStruct((1, LOCAL), jnp.float32),
        ),
        in_specs=[SMEM] * later + [VMEM, VMEM, VMEM, VMEM],
        out_specs=(VMEM,) * 6,
        scratch_shapes=[pltpu.VMEM((LOCAL, WIDTH), jnp.bfloat16)],
        compiler_params=pltpu.CompilerParams(vmem_limit_bytes=LIMIT),
        cost_estimate=pl.CostEstimate(
            flops=2 * CHIPS * 24 * LOCAL * 640, bytes_accessed=2**21, transcendentals=0
        ),
        name="pack_later" if later else "pack",
    )(*((first_unit,) if later else ()), sizes, emb, cluster, rank)


def own_best(lines, shared):
    return pl.pallas_call(
        own_kernel,
        out_shape=(
            jax.ShapeDtypeStruct((8, HELD), jnp.float32),
            jax.ShapeDtypeStruct((HELD, 128), jnp.float32),
            jax.ShapeDtypeStruct((TILE, WIDTH), jnp.bfloat16),
        ),
        in_specs=[VMEM] * 2,
        out_specs=(VMEM,) * 3,
        scratch_shapes=[pltpu.VMEM((1, HELD), jnp.float32)],
        compiler_params=pltpu.CompilerParams(vmem_limit_bytes=LIMIT),
        cost_estimate=pl.CostEstimate(
            flops=2 * HELD * HELD * WIDTH, bytes_accessed=2**21, transcendentals=0
        ),
        name="own_best",
    )(lines, shared)


def cross_best(lines, other, shared):
    start, key_rows, late = own_best(lines, shared)
    return pl.pallas_call(
        cross_kernel,
        out_shape=jax.ShapeDtypeStruct((2 * CHIPS, 128), jnp.float32),
        in_specs=[VMEM] * 6,
        out_specs=VMEM,
        scratch_shapes=[
            pltpu.VMEM((TILE, WIDTH), jnp.bfloat16),
            pltpu.VMEM((1, HELD), jnp.float32),
        ],
        compiler_params=pltpu.CompilerParams(vmem_limit_bytes=LIMIT),
        cost_estimate=pl.CostEstimate(
            flops=HELD * HELD * WIDTH, bytes_accessed=2**21, transcendentals=0
        ),
        name="cross_best",
    )(lines, late, start, key_rows, other, shared)


def merge(answers, slot_key, row_key, extra):
    return pl.pallas_call(
        merge_kernel,
        out_shape=jax.ShapeDtypeStruct((1, LOCAL), jnp.float32),
        in_specs=[VMEM] * 4,
        out_specs=VMEM,
        compiler_params=pltpu.CompilerParams(vmem_limit_bytes=16 * 1024 * 1024),
        name="merge",
    )(answers, slot_key, row_key, extra)


def exchange(values, axes):
    return lax.all_to_all(values, axes, split_axis=0, concat_axis=0, tiled=True)


def answers_of(sent, shared):
    lines = exchange(sent, ("x", "y", "z"))
    other = lax.ppermute(lines, "core", [(0, 1), (1, 0)])
    return exchange(cross_best(lines, other, shared), ("core", "x", "y", "z"))


def body(embeddings, cluster_sizes, cluster_of, rank_in):
    sizes = cluster_sizes.reshape(1, 2 * GROUPS)
    cluster = cluster_of.reshape(1, LOCAL)
    rank = rank_in.reshape(1, LOCAL)
    sent, row_key, slot_key, total, shared, none = pack(sizes, None, embeddings, cluster, rank)

    def more(carry):
        return carry[0] < total[0, 0]

    def again(carry):
        unit, best = carry
        sent, row_key, slot_key, _, _, _ = pack(sizes, unit.reshape(1), embeddings, cluster, rank)
        return unit + CHIPS, merge(answers_of(sent, shared), slot_key, row_key, best)

    def rounds():
        return lax.while_loop(more, again, (jnp.int32(CHIPS), none))[1]

    extra = lax.cond(total[0, 0] > CHIPS, rounds, lambda: none)
    return merge(answers_of(sent, shared), slot_key, row_key, extra).reshape(LOCAL)


def solution(mesh):
    chips = Mesh(mesh.devices.reshape(4, 4, 4, 2), ("x", "y", "z", "core"))
    every = ("x", "y", "z", "core")
    in_specs = (P(every, None), P(), P(every), P(every))
    return jax.shard_map(
        body, mesh=chips, in_specs=in_specs, out_specs=P(every), check_vma=False
    )
```

```python
import itertools

import jax
import jax.numpy as jnp
from jax import lax
from jax.experimental import pallas as pl
from jax.experimental.pallas import tpu as pltpu
from jax.sharding import Mesh
from jax.sharding import PartitionSpec as P

SLOTS = 1280
GROUPS = 16
BLOCKS = 8
WIDTH = 512
LOCAL = 512
CHIPS = 64
DATA = 20
EARLY = 16
PART = 5
HELD = CHIPS * DATA
TILE = 256
TILES = HELD // TILE
LATE_AT = 4 * EARLY
TAGS_AT = LATE_AT + 16
LINES = TAGS_AT + 8
ODD = 16384
EMPTY = 1048576.0

COVERS = {
    1: ((0, 1, 0, 1),),
    2: ((0, 1, 2, 3),),
    3: ((0, 1, 4, 5), (1, 2, 3, 5), (0, 2, 3, 4)),
    4: ((1, 3, 6, 7), (1, 4, 5, 7), (0, 3, 4, 6), (0, 2, 3, 5), (0, 1, 2, 7), (2, 4, 5, 6)),
    5: (
        (3, 4, 6, 8), (3, 5, 8, 9), (2, 5, 6, 9), (1, 2, 3, 8), (0, 1, 6, 7),
        (1, 4, 5, 9), (0, 2, 4, 7), (0, 7, 8, 9), (0, 3, 5, 7),
    ),
    6: (
        (4, 5, 8, 10), (3, 6, 8, 11), (0, 4, 7, 11), (0, 1, 6, 10), (1, 7, 8, 9),
        (3, 5, 7, 10), (1, 3, 4, 9), (0, 5, 6, 9), (2, 9, 10, 11), (0, 2, 3, 8),
        (1, 2, 5, 11), (2, 4, 6, 7),
    ),
    7: (
        (0, 1, 5, 13), (3, 5, 8, 10), (0, 7, 10, 11), (2, 11, 12, 13), (2, 7, 8, 11),
        (1, 4, 10, 12), (8, 9, 12, 13), (1, 3, 4, 7), (4, 7, 9, 13), (3, 6, 10, 13),
        (0, 1, 2, 8), (0, 4, 6, 8), (2, 4, 5, 11), (0, 3, 9, 12), (5, 6, 7, 12),
        (2, 5, 9, 10), (1, 6, 9, 11), (2, 3, 6, 11),
    ),
}


def affine_plane():
    times = ((0, 0, 0, 0), (0, 1, 2, 3), (0, 2, 3, 1), (0, 3, 1, 2))
    lines = [tuple(4 * x + y for y in range(4)) for x in range(4)]
    for slope in range(4):
        for shift in range(4):
            lines.append(tuple(4 * x + (times[slope][x] ^ shift) for x in range(4)))
    return tuple(lines)


COVERS[8] = affine_plane()
for _m, _units in COVERS.items():
    _met = {frozenset(p) for unit in _units for p in itertools.combinations(unit, 2)}
    assert all(frozenset(p) in _met for p in itertools.combinations(range(2 * _m), 2))


def covers_by_lane():
    lane = lax.broadcasted_iota(jnp.int32, (8, 128), 1)
    packed = jnp.zeros((8, 128), jnp.int32)
    at = 0
    for m in range(1, BLOCKS + 1):
        for unit in COVERS[m]:
            value = sum(point << (4 * k) for k, point in enumerate(unit))
            packed = packed + jnp.where(lane == at, value, 0)
            at += 1
    assert at <= 128
    return packed


def by_blocks(m, values):
    picked = jnp.zeros_like(m)
    for k in range(1, BLOCKS + 1):
        picked = jnp.where(m == k, float(values[k]), picked)
    return picked


def full_blocks(places):
    return jnp.floor((places + 0.5) * (1.0 / SLOTS))


def plan(row, first_unit):
    clusters = 2 * GROUPS
    down = lax.broadcasted_iota(jnp.int32, (clusters, clusters), 0)
    across = lax.broadcasted_iota(jnp.int32, (clusters, clusters), 1)
    row = jnp.broadcast_to(row, (clusters, clusters))

    def column(mask):
        picked = jnp.sum(jnp.where(mask, row, 0.0), axis=1, keepdims=True)
        return jnp.broadcast_to(picked, (clusters, 128))

    size = column(down == across)
    partner = column(down == across + 1 - 2 * (across % 2))
    index = lax.broadcasted_iota(jnp.int32, (clusters, 128), 0)
    odd = index % 2 == 1
    first = jnp.where(odd, partner, size)
    blocks_a = full_blocks(first + (SLOTS - 1))
    start_b = full_blocks(first)
    blocks_b = full_blocks(size + partner + (SLOTS - 1)) - start_b
    blocks = jnp.where(odd, blocks_b, blocks_a)
    begin = jnp.where(odd, start_b, 0.0)
    counts = [0] + [len(COVERS[m]) for m in range(1, BLOCKS + 1)]
    alone = by_blocks(blocks, counts)
    held = (blocks == 1.0) & (blocks_a > start_b) & (odd | (blocks_b >= 2.0))
    shared = jnp.where(jnp.sum(alone, axis=0, keepdims=True) <= CHIPS, 0.0, 1.0)
    count = alone * (1.0 - shared * jnp.where(held, 1.0, 0.0))
    total = jnp.sum(count, axis=0, keepdims=True)
    start = jnp.dot(
        jnp.where(across < down, 1.0, 0.0).astype(jnp.bfloat16),
        count.astype(jnp.bfloat16),
        preferred_element_type=jnp.float32,
    )
    unit = (lax.broadcasted_iota(jnp.int32, (1, 128), 1) + first_unit).astype(jnp.float32)
    mine = (unit >= start) & (unit < start + count)

    def of_unit(values):
        return jnp.sum(jnp.where(mine, values, 0.0), axis=0, keepdims=True)

    bases = [0] + [sum(counts[:m]) for m in range(1, BLOCKS + 1)]
    entry = of_unit(by_blocks(blocks, bases) - start) + unit
    group = (index // 2).astype(jnp.float32)
    kind = 2.0 * shared + (1.0 - shared) * jnp.where(odd, 1.0, 0.0)
    half = of_unit(group * (2 * BLOCKS) + 2.0 * begin + 256.0 * kind)
    used = of_unit(jnp.where(blocks == 1.0, 1.0, 2.0))
    entry = jnp.broadcast_to(jnp.clip(entry, 0.0, 127.0).astype(jnp.int32), (8, 128))
    points = jnp.take_along_axis(covers_by_lane(), entry, axis=1)[0:1, :]
    diagonal = lax.broadcasted_iota(jnp.int32, (CHIPS, 128), 0) == lax.broadcasted_iota(
        jnp.int32, (CHIPS, 128), 1
    )
    table = []
    for a in range(4):
        point = ((points >> (4 * a)) & 15).astype(jnp.float32)
        held_by = jnp.where(used > (a // 2) + 0.5, half + point, 1024.0)
        held_by = jnp.sum(jnp.where(diagonal, held_by, 0.0), axis=1, keepdims=True)
        table.append(jnp.broadcast_to(held_by, (CHIPS, 128)))
    return table, size, jnp.where(odd, partner, 0.0), shared, total


def chip_index():
    return (lax.axis_index("x") * 4 + lax.axis_index("y")) * 4 + lax.axis_index("z")


def pack_kernel(
    first_unit, sizes, emb, cluster, rank,
    sent, row_key_out, slot_key_out, total_out, shared_out, none_out, unit,
):
    table, size, previous, shared, total = plan(sizes[...].astype(jnp.float32), first_unit)
    total_out[...] = total.astype(jnp.int32)
    shared_out[...] = jnp.broadcast_to(shared, (8, 128))
    none_out[...] = jnp.full((1, LOCAL), -1.0, jnp.float32)

    def wide(column):
        return jnp.concatenate([column] * (LOCAL // 128), axis=1)

    cluster_of = cluster[...]
    rank_in = rank[...].astype(jnp.float32)
    own = lax.broadcasted_iota(jnp.int32, (2 * GROUPS, LOCAL), 0) == cluster_of
    own_size = jnp.sum(jnp.where(own, wide(size), 0.0), axis=0, keepdims=True)
    place = rank_in + jnp.sum(jnp.where(own, wide(previous), 0.0), axis=0, keepdims=True)
    bin_of = (cluster_of // 2) * BLOCKS + full_blocks(place).astype(jnp.int32)
    bins = lax.broadcasted_iota(jnp.int32, (GROUPS * BLOCKS, LOCAL), 0)
    member = jnp.where(bins == bin_of, 1.0, 0.0)
    until = lax.broadcasted_iota(jnp.int32, (128, 256), 0) <= lax.broadcasted_iota(
        jnp.int32, (128, 256), 1
    )
    until = jnp.where(until, 1.0, 0.0).astype(jnp.bfloat16)
    passed = jnp.full((GROUPS * BLOCKS, 128), -1.0, jnp.float32)
    bucket = []
    for c in range(LOCAL // 128):
        part = member[:, c * 128 : (c + 1) * 128]
        seen = jnp.dot(part.astype(jnp.bfloat16), until, preferred_element_type=jnp.float32)
        before = passed + seen[:, :128]
        passed = passed + seen[:, 128:]
        bucket.append(jnp.sum(part * before, axis=0, keepdims=True))
    bucket = jnp.concatenate(bucket, axis=1)
    upper = jnp.floor((bucket + 0.5) * 0.5)
    odd = cluster_of % 2
    kind = wide(shared)
    kind = 2.0 * kind + (1.0 - kind) * odd.astype(jnp.float32)
    half_key = bin_of.astype(jnp.float32) * 2.0 + (bucket - 2.0 * upper) + 256.0 * kind
    row_key = half_key * 8.0 + upper
    row_key_out[...] = jnp.where(rank_in < own_size, row_key, -7.0)

    high = jnp.floor((rank_in + 0.5) * (1.0 / 128))
    low = rank_in - 128.0 * high
    high = high + 1.0 + (odd * (ODD // 128)).astype(jnp.float32)
    down = lax.broadcasted_iota(jnp.int32, (128, LOCAL), 0)
    parts = jnp.where(down >= 64, low, high)
    seat = (down % 64).astype(jnp.float32)
    holds, tags = [], []
    for a in range(4):
        holds.append(jnp.where(wide(table[a]) == half_key, 1.0, 0.0).astype(jnp.bfloat16))
        here = seat == upper + float(PART * a)
        tags.append(jnp.where(here, parts, 0.0).astype(jnp.bfloat16))
    tag = lax.dot_general(
        jnp.concatenate(holds, axis=1),
        jnp.concatenate(tags, axis=1),
        (((1,), (1,)), ((), ())),
        preferred_element_type=jnp.float32,
    )
    chip = chip_index()
    lane = lax.broadcasted_iota(jnp.int32, (CHIPS, 128), 1)
    row = lax.broadcasted_iota(jnp.int32, (CHIPS, 8, 128), 1)
    lines = jnp.zeros((CHIPS, 8, 128), jnp.float32)
    moves = (
        (0, EARLY, chip % 8 * EARLY),
        (64, EARLY, chip % 8 * EARLY),
        (EARLY, 4, chip % 32 * 4),
        (64 + EARLY, 4, chip % 32 * 4),
    )
    for k, (first, count, to) in enumerate(moves):
        part = jnp.where((lane >= first) & (lane < first + count), tag, 0.0)
        part = pltpu.roll(part, (to + 128 - first) % 128, 1).reshape(CHIPS, 1, 128)
        lines = jnp.where(row == k, jnp.broadcast_to(part, (CHIPS, 8, 128)), lines)
    sent[:, pl.ds(TAGS_AT, 8), :] = lines.astype(jnp.bfloat16)

    for a in range(4):
        table[a] = table[a] * 8.0
        slot_key_out[pl.ds(a * CHIPS, CHIPS), :] = table[a]

    values = emb[...].astype(jnp.float32)
    scale = lax.rsqrt(jnp.sum(values * values, axis=1, keepdims=True) + 1e-06)
    unit[...] = (values * scale).astype(jnp.bfloat16)

    row_key_16 = jnp.broadcast_to(row_key, (16, LOCAL)).astype(jnp.int32).astype(jnp.int16)
    one, zero = jnp.ones((), jnp.bfloat16), jnp.zeros((), jnp.bfloat16)

    def picked(parts, slot):
        key = jnp.broadcast_to(parts[-1], slot.shape)
        rest = slot
        for a in range(1, 4):
            rest = rest - jnp.where(slot >= PART * a, PART, 0)
        for a in range(2, -1, -1):
            part = jnp.broadcast_to(parts[a], slot.shape)
            key = jnp.where(slot < PART * (a + 1), part, key)
        key = (key + rest.astype(jnp.float32)).astype(jnp.int32).astype(jnp.int16)
        key = key.reshape(slot.shape[0] * slot.shape[1] // 16, 16, 128)
        chosen = []
        for c in range(LOCAL // 128):
            hit = key == row_key_16[:, c * 128 : (c + 1) * 128]
            chosen.append(jnp.where(hit, one, zero).reshape(key.shape[0] * 16, 128))
        data = jnp.dot(
            jnp.concatenate(chosen, axis=1), unit[...], preferred_element_type=jnp.float32
        )
        return [data[:, q * 128 : (q + 1) * 128].reshape(slot.shape) for q in range(4)]

    some = 16
    slot = lax.broadcasted_iota(jnp.int32, (some, EARLY, 128), 1)
    for k in range(CHIPS // some):
        chips = pl.ds(k * some, some)
        parts = [part[k * some : (k + 1) * some, :].reshape(some, 1, 128) for part in table]
        quarters = picked(parts, slot)
        for q in range(4):
            sent[chips, pl.ds(q * EARLY, EARLY), :] = quarters[q].astype(jnp.bfloat16)

    pairs = CHIPS // 2
    row = lax.broadcasted_iota(jnp.int32, (pairs, 8, 128), 1)
    last = table[3].reshape(pairs, 2, 1, 128)
    even, odd_one = (jnp.broadcast_to(last[:, k], (pairs, 8, 128)) for k in range(2))
    last = jnp.where(row < 4, even, odd_one)
    late = picked([last] * 4, EARLY + row % 4)
    moved = [pltpu.roll(part, 4, 1) for part in late]
    folded = [
        jnp.concatenate([jnp.where(row < 4, late[q], moved[q + 1]) for q in (0, 2)], axis=1),
        jnp.concatenate([jnp.where(row < 4, moved[q], late[q + 1]) for q in (0, 2)], axis=1),
    ]
    folded = jnp.stack(folded, axis=1).reshape(CHIPS, 16, 128)
    sent[:, pl.ds(LATE_AT, 16), :] = folded.astype(jnp.bfloat16)


def unfold_late(lines, late):
    part = lines[:, pl.ds(LATE_AT, 16), :].astype(jnp.float32).reshape(CHIPS // 2, 2, 16, 128)
    low_rows = lax.broadcasted_iota(jnp.int32, (CHIPS // 2, 8, 128), 1) < 4
    for q in (0, 2):
        even, odd = part[:, 0, q * 4 : q * 4 + 8], part[:, 1, q * 4 : q * 4 + 8]
        quarters = (
            jnp.where(low_rows, even, pltpu.roll(odd, 4, 1)),
            jnp.where(low_rows, pltpu.roll(even, 4, 1), odd),
        )
        for k in range(2):
            late[:, pl.ds((q + k) * 128, 128)] = (
                quarters[k].reshape(CHIPS * 4, 128).astype(jnp.bfloat16)
            )


def tile(lines, late, n):
    if n == TILES - 1:
        return late[...]
    sources = pl.ds(n * (TILE // EARLY), TILE // EARLY)
    quarters = [lines[sources, pl.ds(q * EARLY, EARLY), :] for q in range(4)]
    return jnp.concatenate([part.reshape(TILE, 128) for part in quarters], axis=1)


def tiles(lines, late, some):
    return jnp.concatenate([tile(lines, late, n) for n in some], axis=0)


def keys_of(lines):
    tags = lines[:, pl.ds(TAGS_AT, 8), :].astype(jnp.float32)
    row = lax.broadcasted_iota(jnp.int32, (8, 128), 0)
    first = jnp.where(row == 0, 128.0, 0.0) + jnp.where(row == 1, 1.0, 0.0)
    last = jnp.where(row == 2, 128.0, 0.0) + jnp.where(row == 3, 1.0, 0.0)
    eights = [jnp.sum(tags[c * 8 : (c + 1) * 8], axis=0) for c in range(CHIPS // 8)]
    early = [eight * first for eight in eights]
    late = [sum(eights[c * 4 : (c + 1) * 4]) * last for c in range(CHIPS // 32)]
    key = jnp.concatenate([jnp.sum(k, axis=0, keepdims=True) for k in early + late], axis=1)
    return jnp.where(key == 0.0, EMPTY, key)


def scores_of(rows, columns):
    return lax.dot_general(
        rows, columns, (((1,), (1,)), ((), ())), preferred_element_type=jnp.float32
    )


def is_odd(key):
    return jnp.where(key >= ODD, 1.0, 0.0)


def highest(part):
    return jnp.max(part.reshape(part.shape[0] // 8, 8, 128), axis=0)


def lanes_of(chip):
    first = chip % 8 * EARLY
    last = chip % 32 * 4
    meet = (last > first - 4) & (last < first + EARLY)
    return first, jnp.where(meet, (last + 64) % 128, last)


def own_kernel(lines, shared, best, key_rows, late, key_lanes):
    def work(mixed):
        unfold_late(lines, late)
        key_lanes[...] = keys_of(lines)
        for c in range(HELD // 128):
            chunk = pl.ds(c * 128, 128)
            key_rows[chunk, :] = jnp.transpose(jnp.broadcast_to(key_lanes[:, chunk], (128, 128)))
        for j in range(TILES):
            score = scores_of(tiles(lines, late, range(TILES)), tile(lines, late, j))
            row = key_rows[...]
            for c in range(TILE // 128):
                lanes = pl.ds(j * TILE + c * 128, 128)
                col = key_lanes[:, lanes]
                earlier = row < col
                if mixed:
                    earlier = earlier & (is_odd(col) == is_odd(row))
                part = score[:, c * 128 : (c + 1) * 128]
                best[:, lanes] = highest(jnp.where(earlier, part, -1.0))

    mixed = shared[...][0, 0] > 0.5
    pl.when(mixed)(lambda: work(True))
    pl.when(~mixed)(lambda: work(False))


def cross_kernel(
    lines, late, start, key_rows, other_lines, shared, out, other_late, key_lanes
):
    core = lax.axis_index("core")
    halves = ((0, 1, 2), (3, 4))

    def answer(at, chunks):
        rows = [jnp.broadcast_to(chunk, (8, 128)) for chunk in chunks[:-2]]
        early = jnp.concatenate(rows, axis=0)
        last = jnp.concatenate([jnp.broadcast_to(c, (32, 128)) for c in chunks[-2:]], axis=0)
        chip = lax.broadcasted_iota(jnp.int32, (CHIPS, 128), 0)
        lane = lax.broadcasted_iota(jnp.int32, (CHIPS, 128), 1)
        first, final = lanes_of(chip)
        last = jnp.where(final == chip % 32 * 4, last, pltpu.roll(last, 64, 1))
        here = (lane >= first) & (lane < first + EARLY)
        out[pl.ds(at, CHIPS), :] = jnp.where(here, early, last)

    def work(mixed, swap):
        unfold_late(other_lines, other_late)
        key_lanes[...] = keys_of(other_lines)
        mine, theirs = {}, {}
        for h in range(2):
            some = halves[1 - h if swap else h]
            for n in halves[h]:
                row = key_rows[pl.ds(n * TILE, TILE), :]
                top = None
                scores = scores_of(tile(lines, late, n), tiles(other_lines, other_late, some))
                for c in range(len(some) * TILE // 128):
                    at = some[0] * 2 + c
                    col = key_lanes[:, pl.ds(at * 128, 128)]
                    part = scores[:, c * 128 : (c + 1) * 128]
                    earlier = col < row
                    if mixed:
                        same = is_odd(col) == is_odd(row)
                        above = jnp.where(earlier & same, part, -1.0)
                        below = jnp.where((row < col) & same, part, -1.0)
                    else:
                        above = jnp.where(earlier, part, -1.0)
                        below = jnp.where(earlier, -1.0, part)
                    top = above if top is None else jnp.maximum(top, above)
                    low = highest(below)
                    theirs[at] = low if at not in theirs else jnp.maximum(theirs[at], low)
                for c in range(TILE // 128):
                    at = n * 2 + c
                    eight = highest(jnp.transpose(top[c * 128 : (c + 1) * 128, :]))
                    eight = jnp.maximum(eight, start[:, pl.ds(at * 128, 128)])
                    mine[at] = jnp.max(eight, axis=0, keepdims=True)
            for c in some:
                for k in (2 * c, 2 * c + 1):
                    theirs[k] = jnp.max(theirs[k], axis=0, keepdims=True)
        order = range(HELD // 128)
        answer(CHIPS if swap else 0, [mine[c] for c in order])
        answer(0 if swap else CHIPS, [theirs[c] for c in order])

    mixed = shared[...][0, 0] > 0.5
    for swap in (False, True):
        here = core == (1 if swap else 0)
        pl.when(here & mixed)(lambda swap=swap: work(True, swap))
        pl.when(here & ~mixed)(lambda swap=swap: work(False, swap))


def merge_kernel(answers, slot_key, row_key, extra, out):
    keys = row_key[...]
    chip = chip_index()
    answer = jnp.maximum(answers[pl.ds(0, CHIPS), :], answers[pl.ds(CHIPS, CHIPS), :])
    first, last = lanes_of(chip)
    early = pltpu.roll(answer, 128 - first, 1)
    late = pltpu.roll(answer, 128 - last, 1)
    half = jnp.floor((keys + 0.5) * 0.125) * 8.0
    seat = keys - half
    best = jnp.full((CHIPS, LOCAL), -1.0, jnp.float32)
    for a in range(4):
        value = None
        for k in range(PART):
            t = PART * a + k
            column = early[:, t : t + 1] if t < EARLY else late[:, t - EARLY : t - EARLY + 1]
            value = column if value is None else jnp.where(seat == float(k), column, value)
        slot = slot_key[pl.ds(a * CHIPS, CHIPS), :]
        slot = jnp.concatenate([slot] * (LOCAL // 128), axis=1)
        best = jnp.maximum(best, jnp.where(slot == half, value, -1.0))
    out[...] = jnp.maximum(jnp.max(best, axis=0, keepdims=True), extra[...])


VMEM = pl.BlockSpec(memory_space=pltpu.VMEM)
SMEM = pl.BlockSpec(memory_space=pltpu.SMEM)
LIMIT = 16 * 1024 * 1024


def pack(sizes, first_unit, emb, cluster, rank):
    later = first_unit is not None

    def kernel(*refs):
        if later:
            pack_kernel(refs[0][0], *refs[1:])
        else:
            pack_kernel(0, *refs)

    return pl.pallas_call(
        kernel,
        out_shape=(
            jax.ShapeDtypeStruct((CHIPS, LINES, 128), jnp.bfloat16),
            jax.ShapeDtypeStruct((1, LOCAL), jnp.float32),
            jax.ShapeDtypeStruct((4 * CHIPS, 128), jnp.float32),
            jax.ShapeDtypeStruct((1, 128), jnp.int32),
            jax.ShapeDtypeStruct((8, 128), jnp.float32),
            jax.ShapeDtypeStruct((1, LOCAL), jnp.float32),
        ),
        in_specs=[SMEM] * later + [VMEM, VMEM, VMEM, VMEM],
        out_specs=(VMEM,) * 6,
        scratch_shapes=[pltpu.VMEM((LOCAL, WIDTH), jnp.bfloat16)],
        compiler_params=pltpu.CompilerParams(vmem_limit_bytes=LIMIT),
        cost_estimate=pl.CostEstimate(
            flops=2 * CHIPS * 24 * LOCAL * 640, bytes_accessed=2**21, transcendentals=0
        ),
        name="pack_later" if later else "pack",
    )(*((first_unit,) if later else ()), sizes, emb, cluster, rank)


def own_best(lines, shared):
    return pl.pallas_call(
        own_kernel,
        out_shape=(
            jax.ShapeDtypeStruct((8, HELD), jnp.float32),
            jax.ShapeDtypeStruct((HELD, 128), jnp.float32),
            jax.ShapeDtypeStruct((TILE, WIDTH), jnp.bfloat16),
        ),
        in_specs=[VMEM] * 2,
        out_specs=(VMEM,) * 3,
        scratch_shapes=[pltpu.VMEM((1, HELD), jnp.float32)],
        compiler_params=pltpu.CompilerParams(vmem_limit_bytes=LIMIT),
        cost_estimate=pl.CostEstimate(
            flops=2 * HELD * HELD * WIDTH, bytes_accessed=2**21, transcendentals=0
        ),
        name="own_best",
    )(lines, shared)


def cross_best(lines, other, shared):
    start, key_rows, late = own_best(lines, shared)
    return pl.pallas_call(
        cross_kernel,
        out_shape=jax.ShapeDtypeStruct((2 * CHIPS, 128), jnp.float32),
        in_specs=[VMEM] * 6,
        out_specs=VMEM,
        scratch_shapes=[
            pltpu.VMEM((TILE, WIDTH), jnp.bfloat16),
            pltpu.VMEM((1, HELD), jnp.float32),
        ],
        compiler_params=pltpu.CompilerParams(vmem_limit_bytes=LIMIT),
        cost_estimate=pl.CostEstimate(
            flops=HELD * HELD * WIDTH, bytes_accessed=2**21, transcendentals=0
        ),
        name="cross_best",
    )(lines, late, start, key_rows, other, shared)


def merge(answers, slot_key, row_key, extra):
    return pl.pallas_call(
        merge_kernel,
        out_shape=jax.ShapeDtypeStruct((1, LOCAL), jnp.float32),
        in_specs=[VMEM] * 4,
        out_specs=VMEM,
        compiler_params=pltpu.CompilerParams(vmem_limit_bytes=16 * 1024 * 1024),
        name="merge",
    )(answers, slot_key, row_key, extra)


def exchange(values, axes):
    return lax.all_to_all(values, axes, split_axis=0, concat_axis=0, tiled=True)


def answers_of(sent, shared):
    lines = exchange(sent, ("x", "y", "z"))
    other = lax.ppermute(lines, "core", [(0, 1), (1, 0)])
    return exchange(cross_best(lines, other, shared), ("core", "x", "y", "z"))


def body(embeddings, cluster_sizes, cluster_of, rank_in):
    sizes = cluster_sizes.reshape(1, 2 * GROUPS)
    cluster = cluster_of.reshape(1, LOCAL)
    rank = rank_in.reshape(1, LOCAL)
    sent, row_key, slot_key, total, shared, none = pack(sizes, None, embeddings, cluster, rank)

    def more(carry):
        return carry[0] < total[0, 0]

    def again(carry):
        unit, best = carry
        sent, row_key, slot_key, _, _, _ = pack(sizes, unit.reshape(1), embeddings, cluster, rank)
        return unit + CHIPS, merge(answers_of(sent, shared), slot_key, row_key, best)

    def rounds():
        return lax.while_loop(more, again, (jnp.int32(CHIPS), none))[1]

    extra = lax.cond(total[0, 0] > CHIPS, rounds, lambda: none)
    return merge(answers_of(sent, shared), slot_key, row_key, extra).reshape(LOCAL)


def solution(mesh):
    chips = Mesh(mesh.devices.reshape(4, 4, 4, 2), ("x", "y", "z", "core"))
    every = ("x", "y", "z", "core")
    in_specs = (P(every, None), P(), P(every), P(every))
    return jax.shard_map(
        body, mesh=chips, in_specs=in_specs, out_specs=P(every), check_vma=False
    )
```

```python
import itertools

import jax
import jax.numpy as jnp
from jax import lax
from jax.experimental import pallas as pl
from jax.experimental.pallas import tpu as pltpu
from jax.sharding import Mesh
from jax.sharding import PartitionSpec as P

SLOTS = 1280
GROUPS = 16
BLOCKS = 8
WIDTH = 512
LOCAL = 512
CHIPS = 64
DATA = 20
EARLY = 16
PART = 5
HELD = CHIPS * DATA
TILE = 256
TILES = HELD // TILE
LATE_AT = 4 * EARLY
TAGS_AT = LATE_AT + 16
LINES = TAGS_AT + 8
ODD = 16384
EMPTY = 1048576.0

COVERS = {
    1: ((0, 1, 0, 1),),
    2: ((0, 1, 2, 3),),
    3: ((0, 1, 4, 5), (1, 2, 3, 5), (0, 2, 3, 4)),
    4: ((1, 3, 6, 7), (1, 4, 5, 7), (0, 3, 4, 6), (0, 2, 3, 5), (0, 1, 2, 7), (2, 4, 5, 6)),
    5: (
        (3, 4, 6, 8), (3, 5, 8, 9), (2, 5, 6, 9), (1, 2, 3, 8), (0, 1, 6, 7),
        (1, 4, 5, 9), (0, 2, 4, 7), (0, 7, 8, 9), (0, 3, 5, 7),
    ),
    6: (
        (4, 5, 8, 10), (3, 6, 8, 11), (0, 4, 7, 11), (0, 1, 6, 10), (1, 7, 8, 9),
        (3, 5, 7, 10), (1, 3, 4, 9), (0, 5, 6, 9), (2, 9, 10, 11), (0, 2, 3, 8),
        (1, 2, 5, 11), (2, 4, 6, 7),
    ),
    7: (
        (0, 1, 5, 13), (3, 5, 8, 10), (0, 7, 10, 11), (2, 11, 12, 13), (2, 7, 8, 11),
        (1, 4, 10, 12), (8, 9, 12, 13), (1, 3, 4, 7), (4, 7, 9, 13), (3, 6, 10, 13),
        (0, 1, 2, 8), (0, 4, 6, 8), (2, 4, 5, 11), (0, 3, 9, 12), (5, 6, 7, 12),
        (2, 5, 9, 10), (1, 6, 9, 11), (2, 3, 6, 11),
    ),
}


def affine_plane():
    times = ((0, 0, 0, 0), (0, 1, 2, 3), (0, 2, 3, 1), (0, 3, 1, 2))
    lines = [tuple(4 * x + y for y in range(4)) for x in range(4)]
    for slope in range(4):
        for shift in range(4):
            lines.append(tuple(4 * x + (times[slope][x] ^ shift) for x in range(4)))
    return tuple(lines)


COVERS[8] = affine_plane()
for _m, _units in COVERS.items():
    _met = {frozenset(p) for unit in _units for p in itertools.combinations(unit, 2)}
    assert all(frozenset(p) in _met for p in itertools.combinations(range(2 * _m), 2))


def covers_by_lane():
    lane = lax.broadcasted_iota(jnp.int32, (8, 128), 1)
    packed = jnp.zeros((8, 128), jnp.int32)
    at = 0
    for m in range(1, BLOCKS + 1):
        for unit in COVERS[m]:
            value = sum(point << (4 * k) for k, point in enumerate(unit))
            packed = packed + jnp.where(lane == at, value, 0)
            at += 1
    assert at <= 128
    return packed


def by_blocks(m, values):
    picked = jnp.zeros_like(m)
    for k in range(1, BLOCKS + 1):
        picked = jnp.where(m == k, float(values[k]), picked)
    return picked


def full_blocks(places):
    return jnp.floor((places + 0.5) * (1.0 / SLOTS))


def plan(row, first_unit):
    clusters = 2 * GROUPS
    down = lax.broadcasted_iota(jnp.int32, (clusters, clusters), 0)
    across = lax.broadcasted_iota(jnp.int32, (clusters, clusters), 1)
    row = jnp.broadcast_to(row, (clusters, clusters))

    def column(mask):
        picked = jnp.sum(jnp.where(mask, row, 0.0), axis=1, keepdims=True)
        return jnp.broadcast_to(picked, (clusters, 128))

    size = column(down == across)
    partner = column(down == across + 1 - 2 * (across % 2))
    index = lax.broadcasted_iota(jnp.int32, (clusters, 128), 0)
    odd = index % 2 == 1
    first = jnp.where(odd, partner, size)
    blocks_a = full_blocks(first + (SLOTS - 1))
    start_b = full_blocks(first)
    blocks_b = full_blocks(size + partner + (SLOTS - 1)) - start_b
    blocks = jnp.where(odd, blocks_b, blocks_a)
    begin = jnp.where(odd, start_b, 0.0)
    counts = [0] + [len(COVERS[m]) for m in range(1, BLOCKS + 1)]
    alone = by_blocks(blocks, counts)
    held = (blocks == 1.0) & (blocks_a > start_b) & (odd | (blocks_b >= 2.0))
    shared = jnp.where(jnp.sum(alone, axis=0, keepdims=True) <= CHIPS, 0.0, 1.0)
    count = alone * (1.0 - shared * jnp.where(held, 1.0, 0.0))
    total = jnp.sum(count, axis=0, keepdims=True)
    start = jnp.dot(
        jnp.where(across < down, 1.0, 0.0).astype(jnp.bfloat16),
        count.astype(jnp.bfloat16),
        preferred_element_type=jnp.float32,
    )
    unit = (lax.broadcasted_iota(jnp.int32, (1, 128), 1) + first_unit).astype(jnp.float32)
    mine = (unit >= start) & (unit < start + count)

    def of_unit(values):
        return jnp.sum(jnp.where(mine, values, 0.0), axis=0, keepdims=True)

    bases = [0] + [sum(counts[:m]) for m in range(1, BLOCKS + 1)]
    entry = of_unit(by_blocks(blocks, bases) - start) + unit
    group = (index // 2).astype(jnp.float32)
    kind = 2.0 * shared + (1.0 - shared) * jnp.where(odd, 1.0, 0.0)
    half = of_unit(group * (2 * BLOCKS) + 2.0 * begin + 256.0 * kind)
    used = of_unit(jnp.where(blocks == 1.0, 1.0, 2.0))
    entry = jnp.broadcast_to(jnp.clip(entry, 0.0, 127.0).astype(jnp.int32), (8, 128))
    points = jnp.take_along_axis(covers_by_lane(), entry, axis=1)[0:1, :]
    diagonal = lax.broadcasted_iota(jnp.int32, (CHIPS, 128), 0) == lax.broadcasted_iota(
        jnp.int32, (CHIPS, 128), 1
    )
    table = []
    for a in range(4):
        point = ((points >> (4 * a)) & 15).astype(jnp.float32)
        held_by = jnp.where(used > (a // 2) + 0.5, half + point, 1024.0)
        held_by = jnp.sum(jnp.where(diagonal, held_by, 0.0), axis=1, keepdims=True)
        table.append(jnp.broadcast_to(held_by, (CHIPS, 128)))
    return table, size, jnp.where(odd, partner, 0.0), shared, total


def chip_index():
    return (lax.axis_index("x") * 4 + lax.axis_index("y")) * 4 + lax.axis_index("z")


def pack_kernel(
    first_unit, sizes, emb, cluster, rank,
    sent, row_key_out, slot_key_out, total_out, shared_out, none_out, unit,
):
    table, size, previous, shared, total = plan(sizes[...].astype(jnp.float32), first_unit)
    total_out[...] = total.astype(jnp.int32)
    shared_out[...] = jnp.broadcast_to(shared, (8, 128))
    none_out[...] = jnp.full((1, LOCAL), -1.0, jnp.float32)

    def wide(column):
        return jnp.concatenate([column] * (LOCAL // 128), axis=1)

    cluster_of = cluster[...]
    rank_in = rank[...].astype(jnp.float32)
    own = lax.broadcasted_iota(jnp.int32, (2 * GROUPS, LOCAL), 0) == cluster_of
    own_size = jnp.sum(jnp.where(own, wide(size), 0.0), axis=0, keepdims=True)
    place = rank_in + jnp.sum(jnp.where(own, wide(previous), 0.0), axis=0, keepdims=True)
    bin_of = (cluster_of // 2) * BLOCKS + full_blocks(place).astype(jnp.int32)
    bins = lax.broadcasted_iota(jnp.int32, (GROUPS * BLOCKS, LOCAL), 0)
    member = jnp.where(bins == bin_of, 1.0, 0.0)
    until = lax.broadcasted_iota(jnp.int32, (128, 256), 0) <= lax.broadcasted_iota(
        jnp.int32, (128, 256), 1
    )
    until = jnp.where(until, 1.0, 0.0).astype(jnp.bfloat16)
    passed = jnp.full((GROUPS * BLOCKS, 128), -1.0, jnp.float32)
    bucket = []
    for c in range(LOCAL // 128):
        part = member[:, c * 128 : (c + 1) * 128]
        seen = jnp.dot(part.astype(jnp.bfloat16), until, preferred_element_type=jnp.float32)
        before = passed + seen[:, :128]
        passed = passed + seen[:, 128:]
        bucket.append(jnp.sum(part * before, axis=0, keepdims=True))
    bucket = jnp.concatenate(bucket, axis=1)
    upper = jnp.floor((bucket + 0.5) * 0.5)
    odd = cluster_of % 2
    kind = wide(shared)
    kind = 2.0 * kind + (1.0 - kind) * odd.astype(jnp.float32)
    half_key = bin_of.astype(jnp.float32) * 2.0 + (bucket - 2.0 * upper) + 256.0 * kind
    row_key = half_key * 8.0 + upper
    row_key_out[...] = jnp.where(rank_in < own_size, row_key, -7.0)

    high = jnp.floor((rank_in + 0.5) * (1.0 / 128))
    low = rank_in - 128.0 * high
    high = high + 1.0 + (odd * (ODD // 128)).astype(jnp.float32)
    down = lax.broadcasted_iota(jnp.int32, (128, LOCAL), 0)
    parts = jnp.where(down >= 64, low, high)
    seat = (down % 64).astype(jnp.float32)
    holds, tags = [], []
    for a in range(4):
        holds.append(jnp.where(wide(table[a]) == half_key, 1.0, 0.0).astype(jnp.bfloat16))
        here = seat == upper + float(PART * a)
        tags.append(jnp.where(here, parts, 0.0).astype(jnp.bfloat16))
    tag = lax.dot_general(
        jnp.concatenate(holds, axis=1),
        jnp.concatenate(tags, axis=1),
        (((1,), (1,)), ((), ())),
        preferred_element_type=jnp.float32,
    )
    chip = chip_index()
    lane = lax.broadcasted_iota(jnp.int32, (CHIPS, 128), 1)
    row = lax.broadcasted_iota(jnp.int32, (CHIPS, 8, 128), 1)
    lines = jnp.zeros((CHIPS, 8, 128), jnp.float32)
    moves = (
        (0, EARLY, chip % 8 * EARLY),
        (64, EARLY, chip % 8 * EARLY),
        (EARLY, 4, chip % 32 * 4),
        (64 + EARLY, 4, chip % 32 * 4),
    )
    for k, (first, count, to) in enumerate(moves):
        part = jnp.where((lane >= first) & (lane < first + count), tag, 0.0)
        part = pltpu.roll(part, (to + 128 - first) % 128, 1).reshape(CHIPS, 1, 128)
        lines = jnp.where(row == k, jnp.broadcast_to(part, (CHIPS, 8, 128)), lines)
    sent[:, pl.ds(TAGS_AT, 8), :] = lines.astype(jnp.bfloat16)

    for a in range(4):
        table[a] = table[a] * 8.0
        slot_key_out[pl.ds(a * CHIPS, CHIPS), :] = table[a]

    values = emb[...].astype(jnp.float32)
    scale = lax.rsqrt(jnp.sum(values * values, axis=1, keepdims=True) + 1e-06)
    unit[...] = (values * scale).astype(jnp.bfloat16)

    def picked(parts, slot):
        key = jnp.broadcast_to(parts[-1], slot.shape)
        rest = slot
        for a in range(1, 4):
            rest = rest - jnp.where(slot >= PART * a, PART, 0)
        for a in range(2, -1, -1):
            part = jnp.broadcast_to(parts[a], slot.shape)
            key = jnp.where(slot < PART * (a + 1), part, key)
        key = (key + rest.astype(jnp.float32)).reshape(slot.shape[0] * slot.shape[1], 128)
        chosen = []
        for c in range(LOCAL // 128):
            hit = key == row_key[:, c * 128 : (c + 1) * 128]
            chosen.append(jnp.where(hit, 1.0, 0.0).astype(jnp.bfloat16))
        data = jnp.dot(
            jnp.concatenate(chosen, axis=1), unit[...], preferred_element_type=jnp.float32
        )
        return [data[:, q * 128 : (q + 1) * 128].reshape(slot.shape) for q in range(4)]

    pairs = CHIPS // 2
    row = lax.broadcasted_iota(jnp.int32, (pairs, 8, 128), 1)
    last = table[3].reshape(pairs, 2, 1, 128)
    even, odd_one = (jnp.broadcast_to(last[:, k], (pairs, 8, 128)) for k in range(2))
    last = jnp.where(row < 4, even, odd_one)
    late = picked([last] * 4, EARLY + row % 4)
    moved = [pltpu.roll(part, 4, 1) for part in late]
    folded = [
        jnp.concatenate([jnp.where(row < 4, late[q], moved[q + 1]) for q in (0, 2)], axis=1),
        jnp.concatenate([jnp.where(row < 4, moved[q], late[q + 1]) for q in (0, 2)], axis=1),
    ]
    folded = jnp.stack(folded, axis=1).reshape(CHIPS, 16, 128)
    sent[:, pl.ds(LATE_AT, 16), :] = folded.astype(jnp.bfloat16)

    some = 16
    slot = lax.broadcasted_iota(jnp.int32, (some, EARLY, 128), 1)
    for k in range(CHIPS // some):
        chips = pl.ds(k * some, some)
        parts = [part[k * some : (k + 1) * some, :].reshape(some, 1, 128) for part in table]
        quarters = picked(parts, slot)
        for q in range(4):
            sent[chips, pl.ds(q * EARLY, EARLY), :] = quarters[q].astype(jnp.bfloat16)


def unfold_late(lines, late):
    part = lines[:, pl.ds(LATE_AT, 16), :].astype(jnp.float32).reshape(CHIPS // 2, 2, 16, 128)
    low_rows = lax.broadcasted_iota(jnp.int32, (CHIPS // 2, 8, 128), 1) < 4
    for q in (0, 2):
        even, odd = part[:, 0, q * 4 : q * 4 + 8], part[:, 1, q * 4 : q * 4 + 8]
        quarters = (
            jnp.where(low_rows, even, pltpu.roll(odd, 4, 1)),
            jnp.where(low_rows, pltpu.roll(even, 4, 1), odd),
        )
        for k in range(2):
            late[:, pl.ds((q + k) * 128, 128)] = (
                quarters[k].reshape(CHIPS * 4, 128).astype(jnp.bfloat16)
            )


def tile(lines, late, n):
    if n == TILES - 1:
        return late[...]
    sources = pl.ds(n * (TILE // EARLY), TILE // EARLY)
    quarters = [lines[sources, pl.ds(q * EARLY, EARLY), :] for q in range(4)]
    return jnp.concatenate([part.reshape(TILE, 128) for part in quarters], axis=1)


def tiles(lines, late, some):
    return jnp.concatenate([tile(lines, late, n) for n in some], axis=0)


def keys_of(lines):
    tags = lines[:, pl.ds(TAGS_AT, 8), :].astype(jnp.float32)
    row = lax.broadcasted_iota(jnp.int32, (8, 128), 0)
    first = jnp.where(row == 0, 128.0, 0.0) + jnp.where(row == 1, 1.0, 0.0)
    last = jnp.where(row == 2, 128.0, 0.0) + jnp.where(row == 3, 1.0, 0.0)
    eights = [jnp.sum(tags[c * 8 : (c + 1) * 8], axis=0) for c in range(CHIPS // 8)]
    early = [eight * first for eight in eights]
    late = [sum(eights[c * 4 : (c + 1) * 4]) * last for c in range(CHIPS // 32)]
    key = jnp.concatenate([jnp.sum(k, axis=0, keepdims=True) for k in early + late], axis=1)
    return jnp.where(key == 0.0, EMPTY, key)


def scores_of(rows, columns):
    return lax.dot_general(
        rows, columns, (((1,), (1,)), ((), ())), preferred_element_type=jnp.float32
    )


def is_odd(key):
    return jnp.where(key >= ODD, 1.0, 0.0)


def highest(part):
    return jnp.max(part.reshape(part.shape[0] // 8, 8, 128), axis=0)


def lanes_of(chip):
    first = chip % 8 * EARLY
    last = chip % 32 * 4
    meet = (last > first - 4) & (last < first + EARLY)
    return first, jnp.where(meet, (last + 64) % 128, last)


def own_kernel(lines, shared, best, key_rows, late, key_lanes):
    def work(mixed):
        unfold_late(lines, late)
        key_lanes[...] = keys_of(lines)
        for c in range(HELD // 128):
            chunk = pl.ds(c * 128, 128)
            key_rows[chunk, :] = jnp.transpose(jnp.broadcast_to(key_lanes[:, chunk], (128, 128)))
        for j in range(TILES):
            score = scores_of(tiles(lines, late, range(TILES)), tile(lines, late, j))
            row = key_rows[...]
            for c in range(TILE // 128):
                lanes = pl.ds(j * TILE + c * 128, 128)
                col = key_lanes[:, lanes]
                earlier = row < col
                if mixed:
                    earlier = earlier & (is_odd(col) == is_odd(row))
                part = score[:, c * 128 : (c + 1) * 128]
                best[:, lanes] = highest(jnp.where(earlier, part, -1.0))

    mixed = shared[...][0, 0] > 0.5
    pl.when(mixed)(lambda: work(True))
    pl.when(~mixed)(lambda: work(False))


def cross_kernel(
    lines, late, start, key_rows, other_lines, shared, out, other_late, key_lanes
):
    core = lax.axis_index("core")
    halves = ((0, 1, 2), (3, 4))

    def answer(at, chunks):
        rows = [jnp.broadcast_to(chunk, (8, 128)) for chunk in chunks[:-2]]
        early = jnp.concatenate(rows, axis=0)
        last = jnp.concatenate([jnp.broadcast_to(c, (32, 128)) for c in chunks[-2:]], axis=0)
        chip = lax.broadcasted_iota(jnp.int32, (CHIPS, 128), 0)
        lane = lax.broadcasted_iota(jnp.int32, (CHIPS, 128), 1)
        first, final = lanes_of(chip)
        last = jnp.where(final == chip % 32 * 4, last, pltpu.roll(last, 64, 1))
        here = (lane >= first) & (lane < first + EARLY)
        out[pl.ds(at, CHIPS), :] = jnp.where(here, early, last)

    def work(mixed, swap):
        unfold_late(other_lines, other_late)
        key_lanes[...] = keys_of(other_lines)
        mine, theirs = {}, {}
        for h in range(2):
            some = halves[1 - h if swap else h]
            for n in halves[h]:
                row = key_rows[pl.ds(n * TILE, TILE), :]
                top = None
                scores = scores_of(tile(lines, late, n), tiles(other_lines, other_late, some))
                for c in range(len(some) * TILE // 128):
                    at = some[0] * 2 + c
                    col = key_lanes[:, pl.ds(at * 128, 128)]
                    part = scores[:, c * 128 : (c + 1) * 128]
                    earlier = col < row
                    if mixed:
                        same = is_odd(col) == is_odd(row)
                        above = jnp.where(earlier & same, part, -1.0)
                        below = jnp.where((row < col) & same, part, -1.0)
                    else:
                        above = jnp.where(earlier, part, -1.0)
                        below = jnp.where(earlier, -1.0, part)
                    top = above if top is None else jnp.maximum(top, above)
                    low = highest(below)
                    theirs[at] = low if at not in theirs else jnp.maximum(theirs[at], low)
                for c in range(TILE // 128):
                    at = n * 2 + c
                    eight = highest(jnp.transpose(top[c * 128 : (c + 1) * 128, :]))
                    eight = jnp.maximum(eight, start[:, pl.ds(at * 128, 128)])
                    mine[at] = jnp.max(eight, axis=0, keepdims=True)
            for c in some:
                for k in (2 * c, 2 * c + 1):
                    theirs[k] = jnp.max(theirs[k], axis=0, keepdims=True)
        order = range(HELD // 128)
        answer(CHIPS if swap else 0, [mine[c] for c in order])
        answer(0 if swap else CHIPS, [theirs[c] for c in order])

    mixed = shared[...][0, 0] > 0.5
    for swap in (False, True):
        here = core == (1 if swap else 0)
        pl.when(here & mixed)(lambda swap=swap: work(True, swap))
        pl.when(here & ~mixed)(lambda swap=swap: work(False, swap))


def merge_kernel(answers, slot_key, row_key, extra, out):
    keys = row_key[...]
    chip = chip_index()
    answer = jnp.maximum(answers[pl.ds(0, CHIPS), :], answers[pl.ds(CHIPS, CHIPS), :])
    first, last = lanes_of(chip)
    early = pltpu.roll(answer, 128 - first, 1)
    late = pltpu.roll(answer, 128 - last, 1)
    half = jnp.floor((keys + 0.5) * 0.125) * 8.0
    seat = keys - half
    best = jnp.full((CHIPS, LOCAL), -1.0, jnp.float32)
    for a in range(4):
        value = None
        for k in range(PART):
            t = PART * a + k
            column = early[:, t : t + 1] if t < EARLY else late[:, t - EARLY : t - EARLY + 1]
            value = column if value is None else jnp.where(seat == float(k), column, value)
        slot = slot_key[pl.ds(a * CHIPS, CHIPS), :]
        slot = jnp.concatenate([slot] * (LOCAL // 128), axis=1)
        best = jnp.maximum(best, jnp.where(slot == half, value, -1.0))
    out[...] = jnp.maximum(jnp.max(best, axis=0, keepdims=True), extra[...])


VMEM = pl.BlockSpec(memory_space=pltpu.VMEM)
SMEM = pl.BlockSpec(memory_space=pltpu.SMEM)
LIMIT = 16 * 1024 * 1024


def pack(sizes, first_unit, emb, cluster, rank):
    later = first_unit is not None

    def kernel(*refs):
        if later:
            pack_kernel(refs[0][0], *refs[1:])
        else:
            pack_kernel(0, *refs)

    return pl.pallas_call(
        kernel,
        out_shape=(
            jax.ShapeDtypeStruct((CHIPS, LINES, 128), jnp.bfloat16),
            jax.ShapeDtypeStruct((1, LOCAL), jnp.float32),
            jax.ShapeDtypeStruct((4 * CHIPS, 128), jnp.float32),
            jax.ShapeDtypeStruct((1, 128), jnp.int32),
            jax.ShapeDtypeStruct((8, 128), jnp.float32),
            jax.ShapeDtypeStruct((1, LOCAL), jnp.float32),
        ),
        in_specs=[SMEM] * later + [VMEM, VMEM, VMEM, VMEM],
        out_specs=(VMEM,) * 6,
        scratch_shapes=[pltpu.VMEM((LOCAL, WIDTH), jnp.bfloat16)],
        compiler_params=pltpu.CompilerParams(vmem_limit_bytes=LIMIT),
        cost_estimate=pl.CostEstimate(
            flops=2 * CHIPS * 24 * LOCAL * 640, bytes_accessed=2**21, transcendentals=0
        ),
        name="pack_later" if later else "pack",
    )(*((first_unit,) if later else ()), sizes, emb, cluster, rank)


def own_best(lines, shared):
    return pl.pallas_call(
        own_kernel,
        out_shape=(
            jax.ShapeDtypeStruct((8, HELD), jnp.float32),
            jax.ShapeDtypeStruct((HELD, 128), jnp.float32),
            jax.ShapeDtypeStruct((TILE, WIDTH), jnp.bfloat16),
        ),
        in_specs=[VMEM] * 2,
        out_specs=(VMEM,) * 3,
        scratch_shapes=[pltpu.VMEM((1, HELD), jnp.float32)],
        compiler_params=pltpu.CompilerParams(vmem_limit_bytes=LIMIT),
        cost_estimate=pl.CostEstimate(
            flops=2 * HELD * HELD * WIDTH, bytes_accessed=2**21, transcendentals=0
        ),
        name="own_best",
    )(lines, shared)


def cross_best(lines, other, shared):
    start, key_rows, late = own_best(lines, shared)
    return pl.pallas_call(
        cross_kernel,
        out_shape=jax.ShapeDtypeStruct((2 * CHIPS, 128), jnp.float32),
        in_specs=[VMEM] * 6,
        out_specs=VMEM,
        scratch_shapes=[
            pltpu.VMEM((TILE, WIDTH), jnp.bfloat16),
            pltpu.VMEM((1, HELD), jnp.float32),
        ],
        compiler_params=pltpu.CompilerParams(vmem_limit_bytes=LIMIT),
        cost_estimate=pl.CostEstimate(
            flops=HELD * HELD * WIDTH, bytes_accessed=2**21, transcendentals=0
        ),
        name="cross_best",
    )(lines, late, start, key_rows, other, shared)


def merge(answers, slot_key, row_key, extra):
    return pl.pallas_call(
        merge_kernel,
        out_shape=jax.ShapeDtypeStruct((1, LOCAL), jnp.float32),
        in_specs=[VMEM] * 4,
        out_specs=VMEM,
        compiler_params=pltpu.CompilerParams(vmem_limit_bytes=16 * 1024 * 1024),
        name="merge",
    )(answers, slot_key, row_key, extra)


def exchange(values, axes):
    return lax.all_to_all(values, axes, split_axis=0, concat_axis=0, tiled=True)


def answers_of(sent, shared):
    lines = exchange(sent, ("x", "y", "z"))
    other = lax.ppermute(lines, "core", [(0, 1), (1, 0)])
    return exchange(cross_best(lines, other, shared), ("core", "x", "y", "z"))


def body(embeddings, cluster_sizes, cluster_of, rank_in):
    sizes = cluster_sizes.reshape(1, 2 * GROUPS)
    cluster = cluster_of.reshape(1, LOCAL)
    rank = rank_in.reshape(1, LOCAL)
    sent, row_key, slot_key, total, shared, none = pack(sizes, None, embeddings, cluster, rank)

    def more(carry):
        return carry[0] < total[0, 0]

    def again(carry):
        unit, best = carry
        sent, row_key, slot_key, _, _, _ = pack(sizes, unit.reshape(1), embeddings, cluster, rank)
        return unit + CHIPS, merge(answers_of(sent, shared), slot_key, row_key, best)

    def rounds():
        return lax.while_loop(more, again, (jnp.int32(CHIPS), none))[1]

    extra = lax.cond(total[0, 0] > CHIPS, rounds, lambda: none)
    return merge(answers_of(sent, shared), slot_key, row_key, extra).reshape(LOCAL)


def solution(mesh):
    chips = Mesh(mesh.devices.reshape(4, 4, 4, 2), ("x", "y", "z", "core"))
    every = ("x", "y", "z", "core")
    in_specs = (P(every, None), P(), P(every), P(every))
    return jax.shard_map(
        body, mesh=chips, in_specs=in_specs, out_specs=P(every), check_vma=False
    )
```
